32 devices in a mesh: seq: 8 (over z, core), grp: 4 (over y, x).
Axes of the slice: x: 2, y: 2, z: 4, core: 2. Of those that a mesh axis runs over, the one named last changes fastest.
Arguments:
- tokens: bfloat16 [2, 2048, 2048], P(None, ('seq', 'grp')), may hold values from -6 to 6
- lengths: int32 [2], replicated, may hold values from 1 to 2048, as said below
- attn_gain: float32 [2048], P(('seq', 'grp')), may hold values from 0.5 to 1.5
- w_query: bfloat16 [2048, 2048], P('seq', 'grp'), may hold values from -0.125 to 0.125
- w_key: bfloat16 [2048, 1024], P('seq', 'grp'), may hold values from -0.125 to 0.125
- w_value: bfloat16 [2048, 1024], P('seq', 'grp'), may hold values from -0.125 to 0.125
- query_gain: float32 [128], replicated, may hold values from 1 to 2
- key_gain: float32 [128], replicated, may hold values from 1 to 2
- w_out: bfloat16 [2048, 2048], P('grp', 'seq'), may hold values from -0.75 to 0.75
- mlp_gain: float32 [2048], P(('seq', 'grp')), may hold values from 0.5 to 1.5
- w_gate: bfloat16 [2048, 6144], P('seq', 'grp'), may hold values from -0.125 to 0.125
- w_up: bfloat16 [2048, 6144], P('seq', 'grp'), may hold values from -0.125 to 0.125
- w_down: bfloat16 [6144, 2048], P('grp', 'seq'), may hold values from -0.078125 to 0.078125
- cotangent: bfloat16 [2, 2048, 2048], P(None, ('seq', 'grp')), may hold values from -6 to 6
Outputs:
- output: bfloat16 [2, 2048, 2048], P(None, ('seq', 'grp'))
- grad_tokens: float32 [2, 2048, 2048], P(None, ('seq', 'grp'))
- grad_attn_gain: float32 [2048], P(('seq', 'grp'))
- grad_w_query: float32 [2048, 2048], P('seq', 'grp')
- grad_w_key: float32 [2048, 1024], P('seq', 'grp')
- grad_w_value: float32 [2048, 1024], P('seq', 'grp')
- grad_query_gain: float32 [128], replicated
- grad_key_gain: float32 [128], replicated
- grad_w_out: float32 [2048, 2048], P('grp', 'seq')
- grad_mlp_gain: float32 [2048], P(('seq', 'grp'))
- grad_w_gate: float32 [2048, 6144], P('seq', 'grp')
- grad_w_up: float32 [2048, 6144], P('seq', 'grp')
- grad_w_down: float32 [6144, 2048], P('grp', 'seq')
The draws below stay inside these ranges and needn't reach their ends.
Inputs may be any that keep to these rules, and one draw needn't show every extreme that they name: `lengths`: each row holds 1 to 2048 valid tokens followed by padding; one of the two rows, drawn from the seed, is full.
All inputs are finite; a program needn't handle non-finite values.
Results may differ from the reference program's by a relative error of at most 0.025.
Values may be sent and summed in bfloat16 or wider, within the bound.
A program may use at most 128 MiB of HBM per device.

```python
import math
from functools import partial
import jax
import jax.numpy as jnp
from jax import lax

D = 2048
H = 16
KV = 8
HD = 128
FF = 6144
SEQLEN = 2048


def draw_lengths(key, part):
    key = jax.random.fold_in(key, 7)
    first_key, second_key = jax.random.split(key)
    full_row = jax.random.randint(first_key, (), 0, 2, dtype=jnp.int32)
    other_length = jax.random.randint(second_key, (), 1, SEQLEN + 1, dtype=jnp.int32)
    return jnp.where(jnp.arange(2, dtype=jnp.int32) == full_row, SEQLEN, other_length).astype(jnp.int32)


def level_of(stream_key, shape, pieces, low, largest):
    def one(dim, parts):
        heights = jax.random.uniform(jax.random.fold_in(jax.random.fold_in(stream_key, 6), dim), (parts,), jnp.float32, low / len(pieces), largest / len(pieces))
        return jnp.repeat(jnp.exp(heights), shape[dim] // parts).reshape((-1,) + (1,) * (len(shape) - dim - 1))

    level = one(*pieces[0])
    for cut in pieces[1:]:
        level = level * one(*cut)
    return level


def bell_draw(rng, dims, spread, limit, shards=(), kind=jnp.bfloat16):
    loudness = level_of(rng, dims, shards, -0.22, 0.18) if shards else 1.0
    values = jax.random.normal(rng, dims, jnp.float32) * spread * loudness
    return jnp.minimum(jnp.maximum(values, -limit), limit).astype(kind)


def setup_inputs(seed: int = 0) -> dict:
    arg_keys = jax.random.split(jax.random.key(seed), 15)
    return {
        "tokens": bell_draw(arg_keys[0], (2, SEQLEN, D), 1.0, 6.0, ((1, 32),)),
        "lengths": draw_lengths(jax.random.fold_in(arg_keys[14], 71), 0),
        "attn_gain": jnp.clip(1.0 + 0.1 * jax.random.normal(arg_keys[2], (D,), jnp.float32), 0.5, 1.5),
        "w_query": bell_draw(arg_keys[3], (D, H * HD), D ** -0.5, 0.125, ((0, 8), (1, 4))),
        "w_key": bell_draw(arg_keys[4], (D, KV * HD), D ** -0.5, 0.125, ((0, 8), (1, 4))),
        "w_value": bell_draw(arg_keys[5], (D, KV * HD), D ** -0.5, 0.125, ((0, 8), (1, 4))),
        "query_gain": jnp.clip(jnp.exp(jax.random.uniform(arg_keys[6], (HD,), jnp.float32, math.log(1.0), math.log(2.0))), 1.0, 2.0),
        "key_gain": jnp.clip(jnp.exp(jax.random.uniform(arg_keys[7], (HD,), jnp.float32, math.log(1.0), math.log(2.0))), 1.0, 2.0),
        "w_out": bell_draw(arg_keys[8], (H * HD, D), (H * HD // 32) ** -0.5, 0.75, ((0, 4), (1, 8))),
        "mlp_gain": jnp.clip(1.0 + 0.1 * jax.random.normal(arg_keys[9], (D,), jnp.float32), 0.5, 1.5),
        "w_gate": bell_draw(arg_keys[10], (D, FF), D ** -0.5, 0.125, ((0, 8), (1, 4))),
        "w_up": bell_draw(arg_keys[11], (D, FF), D ** -0.5, 0.125, ((0, 8), (1, 4))),
        "w_down": bell_draw(arg_keys[12], (FF, D), FF ** -0.5, 0.078125, ((0, 4), (1, 8))),
        "cotangent": bell_draw(arg_keys[13], (2, SEQLEN, D), 1.0, 6.0, ((1, 32),)),
    }


EPSILON = 1e-06
ROPE_BASE = 1000000.0
NEGATIVE = -1e+30
HIGHEST = lax.Precision.HIGHEST

@jax.custom_vjp
def low(v):
    return lax.optimization_barrier(v.astype(jnp.bfloat16)).astype(jnp.float32)

@jax.custom_vjp
def low_back(v):
    return v

def low_keep(v):
    return (low(v), None)

def low_pass(kept, grad):
    return (grad,)

def back_keep(v):
    return (v, None)

def back_low(kept, grad):
    return (low(grad),)
low.defvjp(low_keep, low_pass)
low_back.defvjp(back_keep, back_low)

def normalize(values):
    return values * lax.rsqrt(lax.optimization_barrier(jnp.mean(values * values, axis=-1, keepdims=True)) + EPSILON)

def turn_half(values):
    half_dim = values.shape[-1] // 2
    return jnp.concatenate([-values[..., half_dim:], values[..., :half_dim]], axis=-1)

def rotary(values, positions):
    head_dim = values.shape[-1]
    half_dim = head_dim // 2
    frequency = ROPE_BASE ** (-jnp.arange(half_dim, dtype=jnp.float32) * 2.0 / head_dim)
    angles = positions.astype(jnp.float32)[:, None] * frequency[None, :]
    cosine = jnp.concatenate([jnp.cos(angles), jnp.cos(angles)], axis=-1)[None, :, None, :]
    sine_table = jnp.concatenate([jnp.sin(angles), jnp.sin(angles)], axis=-1)[None, :, None, :]
    return values * cosine + turn_half(values) * sine_table

def attend_row(queries, keys, values, length):
    seq_len = queries.shape[0]
    block_rows = math.gcd(seq_len, 512)
    key_pos = jnp.arange(seq_len, dtype=jnp.int32)
    score_scale = 1.0 / math.sqrt(queries.shape[-1])

    def one_block(block_index):
        query_block = lax.dynamic_slice_in_dim(queries, block_index * block_rows, block_rows, 0)
        query_pos = block_index * block_rows + jnp.arange(block_rows, dtype=jnp.int32)
        scores = low_back(jnp.einsum('qkrd,jkd->krqj', query_block, keys, precision=HIGHEST) * score_scale)
        allowed = (key_pos[None, :] <= query_pos[:, None]) & (key_pos[None, :] < length)
        weights = jax.nn.softmax(jnp.where(allowed[None, None], scores, NEGATIVE), axis=-1)
        return jnp.einsum('krqj,jkd->qkrd', low(weights), values, precision=HIGHEST)
    blocks = lax.map(jax.checkpoint(one_block), jnp.arange(seq_len // block_rows, dtype=jnp.int32))
    return blocks.reshape(queries.shape)

def layer(tokens, attn_gain, w_query, w_key, w_value, query_gain, key_gain, w_out, mlp_gain, w_gate, w_up, w_down, lengths):
    seq_len = tokens.shape[1]
    positions = jnp.arange(seq_len, dtype=jnp.int32)
    attn_in = low(normalize(tokens) * attn_gain)
    queries = low_back(jnp.einsum('bsd,dc->bsc', attn_in, w_query, precision=HIGHEST)).reshape(2, seq_len, H, HD)
    keys = low_back(jnp.einsum('bsd,dc->bsc', attn_in, w_key, precision=HIGHEST)).reshape(2, seq_len, KV, HD)
    values = low(low_back(jnp.einsum('bsd,dc->bsc', attn_in, w_value, precision=HIGHEST))).reshape(2, seq_len, KV, HD)
    queries = low(rotary(normalize(queries) * query_gain, positions)).reshape(2, seq_len, KV, H // KV, HD)
    keys = low(rotary(normalize(keys) * key_gain, positions))
    row_outputs = [attend_row(queries[row_index], keys[row_index], values[row_index], lengths[row_index]) for row_index in range(2)]
    mixed = low(low_back(jnp.stack(row_outputs).reshape(2, seq_len, H * HD)))
    hidden = tokens + low_back(jnp.einsum('bsc,cd->bsd', mixed, w_out, precision=HIGHEST))
    mlp_in = low(normalize(hidden) * mlp_gain)
    gate_pre = low_back(jnp.einsum('bsd,df->bsf', mlp_in, w_gate, precision=HIGHEST))
    up_pre = low_back(jnp.einsum('bsd,df->bsf', mlp_in, w_up, precision=HIGHEST))
    inner_low = low(jax.nn.silu(gate_pre) * up_pre)
    return hidden + low_back(jnp.einsum('bsf,fd->bsd', inner_low, w_down, precision=HIGHEST))

def reference(tokens, lengths, attn_gain, w_query, w_key, w_value, query_gain, key_gain, w_out, mlp_gain, w_gate, w_up, w_down, cotangent):
    floats = tuple((argument.astype(jnp.float32) for argument in (tokens, attn_gain, w_query, w_key, w_value, query_gain, key_gain, w_out, mlp_gain, w_gate, w_up, w_down)))
    valid_rows = (jnp.arange(SEQLEN, dtype=jnp.int32)[None, :] < lengths[:, None]).astype(jnp.float32)
    cot_rows = cotangent.astype(jnp.float32) * valid_rows[:, :, None]
    layer_out, pull_back = jax.vjp(partial(layer, lengths=lengths), *floats)
    gradients = pull_back(cot_rows)
    return (layer_out.astype(jnp.bfloat16), gradients[0], gradients[1], gradients[2], gradients[3], gradients[4], gradients[5], gradients[6], gradients[7], gradients[8], gradients[9], gradients[10], gradients[11])
```

```python
from functools import partial
import math

import jax
import jax.numpy as jnp
from jax import lax
from jax.experimental import pallas as pl
from jax.experimental.pallas import tpu as pltpu
from jax.sharding import PartitionSpec as P

EPSILON = 1e-06
ROPE_BASE = 1000000.0
MESH = pl.DeviceIdType.MESH
ANY = pl.BlockSpec(memory_space=pl.ANY)
VMEM = pl.BlockSpec(memory_space=pltpu.VMEM)
DMA = pltpu.SemaphoreType.DMA
F32 = jnp.float32
BF16 = jnp.bfloat16


def normalize(values):
    inverse = lax.rsqrt(jnp.mean(values * values, axis=-1, keepdims=True) + EPSILON)
    return (values * inverse, inverse)


def norm_back(gradient, unit_values, inverse):
    return inverse * (
        gradient - unit_values * jnp.mean(gradient * unit_values, axis=-1, keepdims=True)
    )


def after(value, earlier):
    return lax.optimization_barrier((value, earlier))[0]


def nt(a, b):
    return lax.dot_general(a, b, (((1,), (1,)), ((), ())), preferred_element_type=F32)


def tn(a, b):
    return lax.dot_general(a, b, (((0,), (0,)), ((), ())), preferred_element_type=F32)


def nn(a, b):
    return jnp.dot(a, b, preferred_element_type=F32)


def comm_params(collective_id, mib=32):
    return pltpu.CompilerParams(
        collective_id=collective_id, has_side_effects=True, vmem_limit_bytes=mib * 2**20
    )


def greet(peers):
    barrier = pltpu.get_barrier_semaphore()
    for peer in peers:
        pl.semaphore_signal(barrier, inc=1, device_id=peer, device_id_type=MESH)
    pl.semaphore_wait(barrier, len(peers))


def send(src, dst, send_sem, recv_sem, peer):
    copy = pltpu.make_async_remote_copy(
        src_ref=src,
        dst_ref=dst,
        send_sem=send_sem,
        recv_sem=recv_sem,
        device_id=peer,
        device_id_type=MESH,
    )
    copy.start()
    return copy


def spread_kernel(seq, grp, x_ref, out_ref, send1, recv1, send2, recv2):
    s, g = lax.axis_index("seq"), lax.axis_index("grp")
    line = [(lax.rem(s + k, seq), g) for k in range(1, seq)]
    plane = [(s, lax.rem(g + k, grp)) for k in range(1, grp)]
    greet(line + plane)
    out_ref[pl.ds(g, 1), pl.ds(s, 1)] = x_ref[...][None, None]
    first = [
        send(x_ref, out_ref.at[g, s], send1.at[k], recv1.at[k], peer) for k, peer in enumerate(line)
    ]
    for copy in first:
        copy.wait()
    second = [
        send(out_ref.at[g], out_ref.at[g], send2.at[k], recv2.at[k], peer)
        for k, peer in enumerate(plane)
    ]
    for copy in second:
        copy.wait()


def spread(block, seq, grp, collective_id):
    return pl.pallas_call(
        partial(spread_kernel, seq, grp),
        name="gather_gains",
        out_shape=jax.ShapeDtypeStruct((grp, seq) + block.shape, block.dtype),
        in_specs=[VMEM],
        out_specs=VMEM,
        scratch_shapes=[DMA((seq - 1,)), DMA((seq - 1,)), DMA((grp - 1,)), DMA((grp - 1,))],
        compiler_params=comm_params(collective_id),
    )(block)


def total_kernel(seq, grp, x_ref, out_ref, line_buf, part, plane_buf, send1, recv1, send2, recv2):
    s, g = lax.axis_index("seq"), lax.axis_index("grp")
    line = [(lax.rem(s + k, seq), g) for k in range(1, seq)]
    plane = [(s, lax.rem(g + k, grp)) for k in range(1, grp)]
    greet(line + plane)
    line_buf[pl.ds(s, 1)] = x_ref[...][None]
    first = [
        send(x_ref, line_buf.at[s], send1.at[k], recv1.at[k], peer) for k, peer in enumerate(line)
    ]
    for copy in first:
        copy.wait()
    part[...] = jnp.sum(line_buf[...], axis=0)
    plane_buf[pl.ds(g, 1)] = part[...][None]
    second = [
        send(part, plane_buf.at[g], send2.at[k], recv2.at[k], peer) for k, peer in enumerate(plane)
    ]
    for copy in second:
        copy.wait()
    out_ref[...] = jnp.sum(plane_buf[...], axis=0)


def total(block, seq, grp, collective_id):
    return pl.pallas_call(
        partial(total_kernel, seq, grp),
        name="sum_gains",
        out_shape=jax.ShapeDtypeStruct(block.shape, block.dtype),
        in_specs=[VMEM],
        out_specs=VMEM,
        scratch_shapes=[
            pltpu.VMEM((seq,) + block.shape, block.dtype),
            pltpu.VMEM(block.shape, block.dtype),
            pltpu.VMEM((grp,) + block.shape, block.dtype),
            DMA((seq - 1,)),
            DMA((seq - 1,)),
            DMA((grp - 1,)),
            DMA((grp - 1,)),
        ],
        compiler_params=comm_params(collective_id),
    )(block)


def plane_peers(high):
    s, g = lax.axis_index("seq"), lax.axis_index("grp")
    a, b = g // 2, lax.rem(g, 2)
    across = (s, a * 2 + 1 - b)
    along = [(s, lax.rem(a + k, high) * 2 + b) for k in range(1, high)]
    return a, b, across, along


def gather_rows_kernel(count, high, *refs):
    sources, targets = refs[:count], refs[count : 2 * count]
    send_sems, recv_sems, local_sems = refs[2 * count :]
    a, b, across, along = plane_peers(high)
    greet([across] + along)
    def pusher(i):
        slots = iter(range(4 * high))

        def push(what, where, peer):
            k = next(slots)
            return send(what, where, send_sems.at[i, k], recv_sems.at[i, k], peer)

        return push

    started, local = [], []
    for i in range(count):
        src, dst, push = sources[i], targets[i], pusher(i)
        copy = pltpu.make_async_copy(src, dst.at[:, a, b], local_sems.at[i])
        copy.start()
        local.append(copy)
        over0 = push(src.at[0], dst.at[0, a, b], across)
        up1 = [push(src.at[1], dst.at[1, a, b], peer) for peer in along]
        over1 = push(src.at[1], dst.at[1, a, b], across)
        up0 = [push(src.at[0], dst.at[0, a, b], peer) for peer in along]
        started.append((over0, up1, over1, up0, push))
    for i in range(count):
        dst = targets[i]
        over0, up1, over1, up0, push = started[i]
        over0.wait_recv()
        later = [push(dst.at[0, a, 1 - b], dst.at[0, a, 1 - b], peer) for peer in along]
        for k in range(1, high):
            up1[k - 1].wait_recv()
            origin = lax.rem(a + high - k, high)
            later.append(push(dst.at[1, origin, b], dst.at[1, origin, b], across))
        over1.wait_recv()
        for copy in up0 + later:
            copy.wait_recv()
        for copy in [over0, over1] + up0 + up1 + later:
            copy.wait_send()
        local[i].wait()


def gather_rows(arrays, grp, collective_id, name):
    count, high = len(arrays), grp // 2
    rows, rest = arrays[0].shape[1:]
    result = pl.pallas_call(
        partial(gather_rows_kernel, count, high),
        name=name,
        out_shape=[jax.ShapeDtypeStruct((2, high, 2, rows, rest), x.dtype) for x in arrays],
        in_specs=[ANY] * count,
        out_specs=[ANY] * count,
        scratch_shapes=[DMA((count, 4 * high)), DMA((count, 4 * high)), DMA((count,))],
        compiler_params=comm_params(collective_id),
    )(*arrays)
    return [x.reshape(2 * grp * rows, rest) for x in result]


def sum_rows_kernel(high, src, out, recv0, mid0, last0, recv1, mid1, last1, own0, own1, send_sems, recv_sems, local_sems):
    a, b, across, along = plane_peers(high)
    greet([across] + along)
    slots = iter(range(2 * high))

    def push(what, where, peer):
        k = next(slots)
        return send(what, where, send_sems.at[k], recv_sems.at[k], peer)

    over0 = push(src.at[0, :, 1 - b], recv0, across)
    up1 = [
        push(src.at[1, lax.rem(a + k, high)], recv1.at[k - 1], along[k - 1]) for k in range(1, high)
    ]
    load0 = pltpu.make_async_copy(src.at[0, :, b], own0, local_sems.at[0])
    load1 = pltpu.make_async_copy(src.at[1, a], own1, local_sems.at[1])
    load0.start()
    load1.start()
    load0.wait()
    load1.wait()
    over0.wait_recv()
    mid0[...] = (own0[...].astype(F32) + recv0[...].astype(F32)).astype(BF16)
    up0 = [
        push(mid0.at[lax.rem(a + k, high)], last0.at[k - 1], along[k - 1]) for k in range(1, high)
    ]
    for copy in up1:
        copy.wait_recv()
    joined = own1[...].astype(F32)
    for k in range(1, high):
        joined = joined + recv1[k - 1].astype(F32)
    mid1[...] = joined.astype(BF16)
    over1 = push(mid1.at[1 - b], last1, across)
    for copy in up0:
        copy.wait_recv()
    result = own0[pl.ds(a, 1)][0].astype(F32) + recv0[pl.ds(a, 1)][0].astype(F32)
    for k in range(1, high):
        result = result + last0[k - 1].astype(F32)
    out[0] = result
    over1.wait_recv()
    result = own1[pl.ds(b, 1)][0].astype(F32)
    for k in range(1, high):
        result = result + recv1[k - 1, pl.ds(b, 1)][0].astype(F32)
    out[1] = result + last1[...].astype(F32)
    for copy in [over0, over1] + up0 + up1:
        copy.wait_send()


def sum_rows(partial_sums, grp, collective_id, name):
    high = grp // 2
    tokens, width = partial_sums.shape
    rows = tokens // (2 * grp)
    parts = partial_sums.astype(BF16).reshape(2, high, 2, rows, width)
    return pl.pallas_call(
        partial(sum_rows_kernel, high),
        name=name,
        out_shape=jax.ShapeDtypeStruct((2, rows, width), F32),
        in_specs=[ANY],
        out_specs=VMEM,
        scratch_shapes=[
            pltpu.VMEM((high, rows, width), BF16),
            pltpu.VMEM((high, rows, width), BF16),
            pltpu.VMEM((high - 1, rows, width), BF16),
            pltpu.VMEM((high - 1, 2, rows, width), BF16),
            pltpu.VMEM((2, rows, width), BF16),
            pltpu.VMEM((rows, width), BF16),
            pltpu.VMEM((high, rows, width), BF16),
            pltpu.VMEM((2, rows, width), BF16),
            DMA((2 * high,)),
            DMA((2 * high,)),
            DMA((2,)),
        ],
        compiler_params=comm_params(collective_id),
    )(parts)


def turn_half(values):
    half = values.shape[-1] // 2
    return jnp.concatenate([-values[:, half:], values[:, :half]], axis=-1)


def heads_kernel(queries, keys, raw, gains, cosine, sine, out):
    head = pl.program_id(0)

    @pl.when(head < queries + keys)
    def _():
        unit, _ = normalize(raw[...])
        scaled = unit * jnp.where(head < queries, gains[0:1], gains[1:2])
        out[...] = (scaled * cosine[...] + turn_half(scaled) * sine[...]).astype(BF16)

    @pl.when(head >= queries + keys)
    def _():
        out[...] = raw[...].astype(BF16)


def heads_forward(raw, gains, cosine, sine, queries, keys, dim):
    tokens, width = raw.shape
    column = pl.BlockSpec((tokens, dim), lambda h: (0, h))
    table = pl.BlockSpec((tokens, dim), lambda h: (0, 0))
    return pl.pallas_call(
        partial(heads_kernel, queries, keys),
        name="heads_forward",
        grid=(width // dim,),
        out_shape=jax.ShapeDtypeStruct((tokens, width), BF16),
        in_specs=[column, pl.BlockSpec((8, dim), lambda h: (0, 0)), table, table],
        out_specs=column,
    )(raw, gains, cosine, sine)


def heads_back_kernel(queries, keys, raw, grads, gains, cosine, sine, out, gain_out):
    head = pl.program_id(0)

    @pl.when(head < queries + keys)
    def _():
        unit, inverse = normalize(raw[...])
        given = grads[...]
        turned = given * cosine[...] - turn_half(given * sine[...])
        gain_out[...] = jnp.broadcast_to(
            jnp.sum(turned * unit, axis=0, keepdims=True)[None], gain_out.shape
        )
        scaled = turned * jnp.where(head < queries, gains[0:1], gains[1:2])
        out[...] = norm_back(scaled, unit, inverse).astype(BF16)

    @pl.when(head >= queries + keys)
    def _():
        gain_out[...] = jnp.zeros_like(gain_out)
        out[...] = grads[...].astype(BF16)


def heads_backward(raw, grads, gains, cosine, sine, queries, keys, dim):
    tokens, width = raw.shape
    column = pl.BlockSpec((tokens, dim), lambda h: (0, h))
    table = pl.BlockSpec((tokens, dim), lambda h: (0, 0))
    return pl.pallas_call(
        partial(heads_back_kernel, queries, keys),
        name="heads_backward",
        grid=(width // dim,),
        out_shape=[
            jax.ShapeDtypeStruct((tokens, width), BF16),
            jax.ShapeDtypeStruct((width // dim, 8, dim), F32),
        ],
        in_specs=[column, column, pl.BlockSpec((8, dim), lambda h: (0, 0)), table, table],
        out_specs=[column, pl.BlockSpec((1, 8, dim), lambda h: (h, 0, 0))],
    )(raw, grads, gains, cosine, sine)


def allowed_pairs(info, row, block, rows, repeat):
    key_pos = block * rows + lax.broadcasted_iota(jnp.int32, (rows, repeat * rows), 0)
    query_pos = lax.broadcasted_iota(jnp.int32, (rows, repeat * rows), 1)
    query_pos = info[0] * rows + lax.rem(query_pos, rows)
    return (key_pos <= query_pos) & (key_pos < info[1 + row])


def stacked(ref, row, rows, first, repeat, dim):
    return jnp.concatenate(
        [
            ref[row * rows : (row + 1) * rows, (first + r) * dim : (first + r + 1) * dim]
            for r in range(repeat)
        ],
        axis=0,
    )


def attend_kernel(shape, info, q, kv, mixed, mixed_low, log_total, acc, sums):
    rows, keys, repeat, dim = shape
    block = pl.program_id(0)
    scale = 1.0 / math.sqrt(dim)

    @pl.when(block == 0)
    def _():
        acc[...] = jnp.zeros_like(acc)
        sums[...] = jnp.zeros_like(sums)

    @pl.when(block <= info[0])
    def _():
        for row in range(2):
            allowed = allowed_pairs(info, row, block, rows, repeat)
            for k in range(keys):
                unit = row * keys + k
                kk = kv[0, row * rows : (row + 1) * rows, k * dim : (k + 1) * dim]
                vv = kv[0, row * rows : (row + 1) * rows, (keys + k) * dim : (keys + k + 1) * dim]
                scores = nt(kk, stacked(q, row, rows, k * repeat, repeat, dim)) * scale
                weights = jnp.where(allowed, jnp.exp(scores), 0.0)
                sums[unit] += jnp.sum(weights, axis=0, keepdims=True)
                acc[unit] += tn(vv, weights.astype(BF16))

    @pl.when(block == info[0])
    def _():
        for row in range(2):
            for k in range(keys):
                unit = row * keys + k
                log_total[unit] = jnp.log(sums[unit])
                result = (acc[unit] / sums[unit]).T
                for r in range(repeat):
                    piece = result[r * rows : (r + 1) * rows]
                    h = k * repeat + r
                    mixed[row * rows : (row + 1) * rows, h * dim : (h + 1) * dim] = piece
                    mixed_low[row * rows : (row + 1) * rows, h * dim : (h + 1) * dim] = piece.astype(BF16)


def attend(info, q, kv, keys, repeat, dim):
    blocks, tokens, kv_width = kv.shape
    rows, width = tokens // 2, keys * repeat * dim
    whole = lambda j, info: (0, 0)
    return pl.pallas_call(
        partial(attend_kernel, (rows, keys, repeat, dim)),
        name="attend",
        grid_spec=pltpu.PrefetchScalarGridSpec(
            num_scalar_prefetch=1,
            grid=(blocks,),
            in_specs=[
                pl.BlockSpec((tokens, width), whole),
                pl.BlockSpec((1, tokens, kv_width), lambda j, info: (jnp.minimum(j, info[0]), 0, 0)),
            ],
            out_specs=[
                pl.BlockSpec((tokens, width), whole),
                pl.BlockSpec((tokens, width), whole),
                pl.BlockSpec((2 * keys, 1, repeat * rows), lambda j, info: (0, 0, 0)),
            ],
            scratch_shapes=[
                pltpu.VMEM((2 * keys, dim, repeat * rows), F32),
                pltpu.VMEM((2 * keys, 1, repeat * rows), F32),
            ],
        ),
        out_shape=[
            jax.ShapeDtypeStruct((tokens, width), F32),
            jax.ShapeDtypeStruct((tokens, width), BF16),
            jax.ShapeDtypeStruct((2 * keys, 1, repeat * rows), F32),
        ],
        compiler_params=pltpu.CompilerParams(vmem_limit_bytes=32 * 2**20),
    )(info, q, kv)


def attend_back_kernel(shape, info, q, kv, mixed, grad_mixed, log_total, grad_q, grad_kv, acc, delta):
    rows, keys, repeat, dim = shape
    block = pl.program_id(0)
    scale = 1.0 / math.sqrt(dim)

    @pl.when(block == 0)
    def _():
        acc[...] = jnp.zeros_like(acc)
        for row in range(2):
            for k in range(keys):
                product = stacked(mixed, row, rows, k * repeat, repeat, dim) * stacked(
                    grad_mixed, row, rows, k * repeat, repeat, dim
                ).astype(F32)
                delta[row * keys + k] = jnp.sum(product.T, axis=0, keepdims=True)

    @pl.when(block <= info[0])
    def _():
        for row in range(2):
            allowed = allowed_pairs(info, row, block, rows, repeat)
            here = slice(row * rows, (row + 1) * rows)
            for k in range(keys):
                unit = row * keys + k
                kk = kv[0, here, k * dim : (k + 1) * dim]
                vv = kv[0, here, (keys + k) * dim : (keys + k + 1) * dim]
                qq = stacked(q, row, rows, k * repeat, repeat, dim)
                gg = stacked(grad_mixed, row, rows, k * repeat, repeat, dim)
                weights = jnp.where(allowed, jnp.exp(nt(kk, qq) * scale - log_total[unit]), 0.0)
                grad_scores = (weights * (nt(vv, gg) - delta[unit])).astype(BF16)
                grad_kv[0, here, k * dim : (k + 1) * dim] = (nn(grad_scores, qq) * scale).astype(BF16)
                grad_kv[0, here, (keys + k) * dim : (keys + k + 1) * dim] = nn(
                    weights.astype(BF16), gg
                ).astype(BF16)
                acc[unit] += tn(grad_scores, kk)

    @pl.when(block > info[0])
    def _():
        grad_kv[...] = jnp.zeros_like(grad_kv)

    @pl.when(block == info[0])
    def _():
        for row in range(2):
            for k in range(keys):
                for r in range(repeat):
                    h = k * repeat + r
                    grad_q[row * rows : (row + 1) * rows, h * dim : (h + 1) * dim] = (
                        acc[row * keys + k, r * rows : (r + 1) * rows] * scale
                    )


def attend_back(info, q, kv, mixed, grad_mixed, log_total, keys, repeat, dim):
    blocks, tokens, kv_width = kv.shape
    rows, width = tokens // 2, keys * repeat * dim
    whole = lambda j, info: (0, 0)
    full = pl.BlockSpec((tokens, width), whole)
    return pl.pallas_call(
        partial(attend_back_kernel, (rows, keys, repeat, dim)),
        name="attend_back",
        grid_spec=pltpu.PrefetchScalarGridSpec(
            num_scalar_prefetch=1,
            grid=(blocks,),
            in_specs=[
                full,
                pl.BlockSpec((1, tokens, kv_width), lambda j, info: (jnp.minimum(j, info[0]), 0, 0)),
                full,
                full,
                pl.BlockSpec((2 * keys, 1, repeat * rows), lambda j, info: (0, 0, 0)),
            ],
            out_specs=[full, pl.BlockSpec((1, tokens, kv_width), lambda j, info: (j, 0, 0))],
            scratch_shapes=[
                pltpu.VMEM((2 * keys, repeat * rows, dim), F32),
                pltpu.VMEM((2 * keys, 1, repeat * rows), F32),
            ],
        ),
        out_shape=[
            jax.ShapeDtypeStruct((tokens, width), F32),
            jax.ShapeDtypeStruct((blocks, tokens, kv_width), BF16),
        ],
        compiler_params=pltpu.CompilerParams(vmem_limit_bytes=32 * 2**20),
    )(info, q, kv, mixed, grad_mixed, log_total)


def shards(
    tokens,
    lengths,
    attn_gain,
    w_query,
    w_key,
    w_value,
    query_gain,
    key_gain,
    w_out,
    mlp_gain,
    w_gate,
    w_up,
    w_down,
    cotangent,
):
    seq, grp = lax.axis_size("seq"), lax.axis_size("grp")
    seq_index, grp_index = lax.axis_index("seq"), lax.axis_index("grp")
    local_rows, width = tokens.shape[1:]
    rows = local_rows * grp
    dim = query_gain.shape[0]
    queries, keys = w_query.shape[1] // dim, w_key.shape[1] // dim
    repeat = queries // keys
    hidden_units = w_gate.shape[1]

    projections = jnp.concatenate([w_query, w_key, w_value], axis=1)
    full_qkv = lax.all_gather(projections, "seq", axis=0, tiled=True)
    full_out = lax.all_gather(after(w_out.T, full_qkv), "seq", axis=0, tiled=True)
    gate_up = jnp.concatenate([w_gate, w_up], axis=1)

    chunk = attn_gain.shape[0]
    lane = max(128, chunk)
    packed = jnp.zeros((8, lane), F32).at[0, :chunk].set(attn_gain).at[1, :chunk].set(mlp_gain)
    spread_gains = spread(packed, seq, grp, 1)[:, :, :, :chunk].transpose(2, 1, 0, 3)
    gain_attn = spread_gains[0].reshape(-1)
    gain_mlp = spread_gains[1].reshape(-1)
    residual = tokens.astype(F32)
    attn_unit, attn_inverse = normalize(residual)
    token_pos = (seq_index * grp + grp_index) * local_rows + jnp.arange(local_rows, dtype=jnp.int32)
    valid_rows = (token_pos[None, :] < lengths[:, None]).astype(F32)
    cot_rows = cotangent.astype(F32) * valid_rows[:, :, None]
    attn_rows, grad_out_rows = gather_rows(
        [(attn_unit * gain_attn).astype(BF16), cot_rows.astype(BF16)], grp, 2, "gather_inputs"
    )

    raw = nn(attn_rows, full_qkv)
    positions = seq_index * rows + jnp.arange(rows, dtype=jnp.int32)
    half = dim // 2
    frequency = ROPE_BASE ** (-jnp.arange(half, dtype=F32) * 2.0 / dim)
    angles = positions.astype(F32)[:, None] * frequency[None, :]
    cosine = jnp.tile(jnp.cos(angles), (2, 2))
    sine = jnp.tile(jnp.sin(angles), (2, 2))
    head_gains = jnp.zeros((8, dim), F32).at[0].set(query_gain).at[1].set(key_gain)
    heads = heads_forward(raw, head_gains, cosine, sine, queries, keys, dim)
    q, kv_home = heads[:, : queries * dim], heads[:, queries * dim :]
    kv = lax.all_gather(kv_home, "seq", axis=0, tiled=False)
    full_gate_up = lax.all_gather(after(gate_up, kv), "seq", axis=0, tiled=True)
    full_down = lax.all_gather(after(w_down.T, full_gate_up), "seq", axis=0, tiled=True)

    info = jnp.concatenate([seq_index.astype(jnp.int32)[None], lengths])
    mixed, mixed_low, log_total = attend(info, q, kv, keys, repeat, dim)
    hidden = residual + sum_rows(nt(mixed_low, full_out), grp, 3, "sum_attention")

    mlp_unit, mlp_inverse = normalize(hidden)
    (mlp_rows,) = gather_rows([(mlp_unit * gain_mlp).astype(BF16)], grp, 4, "gather_mlp")
    pre = nn(mlp_rows, full_gate_up)
    gate_pre, up_pre = pre[:, :hidden_units], pre[:, hidden_units:]
    inner_low = (jax.nn.silu(gate_pre) * up_pre).astype(BF16)
    grad_w_down = tn(grad_out_rows, inner_low).astype(BF16)
    sum_down = lax.psum_scatter(grad_w_down, "seq", scatter_dimension=0, tiled=True)
    grad_inner = nn(grad_out_rows, full_down)
    sigmoid_gate = jax.nn.sigmoid(gate_pre)
    grad_gate = grad_inner * up_pre * sigmoid_gate * (1.0 + gate_pre * (1.0 - sigmoid_gate))
    grad_up = grad_inner * gate_pre * sigmoid_gate
    grad_pre = jnp.concatenate([grad_gate.astype(BF16), grad_up.astype(BF16)], axis=1)
    grad_w_pre = tn(mlp_rows, grad_pre).astype(BF16)
    sum_pre = lax.psum_scatter(after(grad_w_pre, sum_down), "seq", scatter_dimension=0, tiled=True)
    grad_mlp_in = sum_rows(nt(grad_pre, full_gate_up), grp, 5, "sum_mlp_back")
    grad_gain_mlp = jnp.sum(grad_mlp_in * mlp_unit, axis=(0, 1))
    grad_hidden = cot_rows + norm_back(grad_mlp_in * gain_mlp, mlp_unit, mlp_inverse)
    (grad_branch,) = gather_rows([grad_hidden.astype(BF16)], grp, 6, "gather_branch")

    grad_mixed = nn(grad_branch, full_out).astype(BF16)
    grad_q, grad_kv = attend_back(info, q, kv, mixed, grad_mixed, log_total, keys, repeat, dim)
    sum_kv = lax.psum_scatter(grad_kv, "seq", scatter_dimension=0, tiled=False)
    layer_out = hidden + sum_rows(
        after(nt(inner_low, full_down), grad_kv), grp, 7, "sum_output"
    )
    output = layer_out.astype(BF16)
    grad_heads = jnp.concatenate([grad_q, sum_kv.astype(F32)], axis=1)
    grad_raw, head_gain_parts = heads_backward(
        raw, grad_heads, head_gains, cosine, sine, queries, keys, dim
    )
    grad_w_attn = jnp.concatenate(
        [tn(attn_rows, grad_raw).astype(BF16), tn(grad_branch, mixed_low).astype(BF16)], axis=1
    )
    sum_attn = lax.psum_scatter(after(grad_w_attn, sum_pre), "seq", scatter_dimension=0, tiled=True)
    grad_attn_in = sum_rows(nt(grad_raw, full_qkv), grp, 8, "sum_attention_back")
    grad_gain_attn = jnp.sum(grad_attn_in * attn_unit, axis=(0, 1))
    grad_tokens = grad_hidden + norm_back(grad_attn_in * gain_attn, attn_unit, attn_inverse)

    head_gain_grads = jnp.stack(
        [
            jnp.sum(head_gain_parts[:queries, 0], axis=0),
            jnp.sum(head_gain_parts[queries : queries + keys, 0], axis=0),
        ]
    )
    vector = jnp.concatenate([grad_gain_attn, grad_gain_mlp, head_gain_grads.reshape(-1)])
    padded = -(-vector.shape[0] // 1024) * 1024
    vector = jnp.pad(vector, (0, padded - vector.shape[0])).reshape(-1, 128)
    sums = total(vector, seq, grp, 9).reshape(-1)
    place = (seq_index * grp + grp_index) * chunk
    out_attn_gain = lax.dynamic_slice(sums, (place,), (chunk,))
    out_mlp_gain = lax.dynamic_slice(sums, (width + place,), (chunk,))
    out_query_gain = sums[2 * width : 2 * width + dim]
    out_key_gain = sums[2 * width + dim : 2 * width + 2 * dim]

    sum_attn = sum_attn.astype(F32)
    cuts = (queries * dim, (queries + keys) * dim, (queries + 2 * keys) * dim)
    sum_pre = sum_pre.astype(F32)
    return (
        output,
        grad_tokens,
        out_attn_gain,
        sum_attn[:, : cuts[0]],
        sum_attn[:, cuts[0] : cuts[1]],
        sum_attn[:, cuts[1] : cuts[2]],
        out_query_gain,
        out_key_gain,
        sum_attn[:, cuts[2] :].T,
        out_mlp_gain,
        sum_pre[:, :hidden_units],
        sum_pre[:, hidden_units:],
        sum_down.astype(F32).T,
    )


def solution(mesh):
    rows = P(None, ("seq", "grp"), None)
    vector = P(("seq", "grp"))
    wide, tall = P("seq", "grp"), P("grp", "seq")
    return jax.shard_map(
        shards,
        mesh=mesh,
        in_specs=(
            rows,
            P(),
            vector,
            wide,
            wide,
            wide,
            P(),
            P(),
            tall,
            vector,
            wide,
            wide,
            tall,
            rows,
        ),
        out_specs=(
            rows,
            rows,
            vector,
            wide,
            wide,
            wide,
            P(),
            P(),
            tall,
            vector,
            wide,
            wide,
            tall,
        ),
        check_vma=False,
    )
```

```python
from functools import partial
import math

import jax
import jax.numpy as jnp
from jax import lax
from jax.experimental import pallas as pl
from jax.experimental.pallas import tpu as pltpu
from jax.sharding import PartitionSpec as P

EPSILON = 1e-06
ROPE_BASE = 1000000.0
MESH = pl.DeviceIdType.MESH
ANY = pl.BlockSpec(memory_space=pl.ANY)
VMEM = pl.BlockSpec(memory_space=pltpu.VMEM)
DMA = pltpu.SemaphoreType.DMA
F32 = jnp.float32
BF16 = jnp.bfloat16


def normalize(values):
    inverse = lax.rsqrt(jnp.mean(values * values, axis=-1, keepdims=True) + EPSILON)
    return (values * inverse, inverse)


def norm_back(gradient, unit_values, inverse):
    return inverse * (
        gradient - unit_values * jnp.mean(gradient * unit_values, axis=-1, keepdims=True)
    )


def after(value, earlier):
    return lax.optimization_barrier((value, earlier))[0]


def nt(a, b):
    return lax.dot_general(a, b, (((1,), (1,)), ((), ())), preferred_element_type=F32)


def tn(a, b):
    return lax.dot_general(a, b, (((0,), (0,)), ((), ())), preferred_element_type=F32)


def nn(a, b):
    return jnp.dot(a, b, preferred_element_type=F32)


def comm_params(collective_id, mib=32):
    return pltpu.CompilerParams(
        collective_id=collective_id, has_side_effects=True, vmem_limit_bytes=mib * 2**20
    )


def greet(peers):
    barrier = pltpu.get_barrier_semaphore()
    for peer in peers:
        pl.semaphore_signal(barrier, inc=1, device_id=peer, device_id_type=MESH)
    pl.semaphore_wait(barrier, len(peers))


def send(src, dst, send_sem, recv_sem, peer):
    copy = pltpu.make_async_remote_copy(
        src_ref=src,
        dst_ref=dst,
        send_sem=send_sem,
        recv_sem=recv_sem,
        device_id=peer,
        device_id_type=MESH,
    )
    copy.start()
    return copy


class Riders:
    def __init__(self, kinds, sources, targets, send_sems, recv_sems):
        self.kinds, self.sources, self.targets = kinds, sources, targets
        self.send_sems, self.recv_sems = send_sems, recv_sems
        self.copies = []

    def peers(self):
        s, g = lax.axis_index("seq"), lax.axis_index("grp")
        seq = lax.axis_size("seq")
        where = {"opposite": lax.rem(s + seq // 2, seq), "pair": s + 2 - 4 * lax.rem(s // 2, 2)}
        return [(where[kind], g) for kind in self.kinds]

    def start(self):
        for i, peer in enumerate(self.peers()):
            self.copies.append(
                send(self.sources[i], self.targets[i], self.send_sems.at[i], self.recv_sems.at[i], peer)
            )

    def finish(self):
        for copy in self.copies:
            copy.wait()


def carried_call(kernel, operands, out_shape, in_specs, out_specs, scratch, params, name, riders=()):
    kinds = [kind for kind, _ in riders]
    arrays = [array for _, array in riders]
    count, ins, outs = len(riders), len(in_specs), len(out_specs)

    def body(*refs):
        sources, refs = refs[:count], refs[count:]
        own_in, refs = refs[:ins], refs[ins:]
        targets, refs = refs[:count], refs[count:]
        own_out, refs = refs[:outs], refs[outs:]
        sems, refs = (refs[:2], refs[2:]) if count else ((None, None), refs)
        kernel(Riders(kinds, sources, targets, *sems), *own_in, *own_out, *refs)

    results = pl.pallas_call(
        body,
        name=name,
        out_shape=[jax.ShapeDtypeStruct(x.shape, x.dtype) for x in arrays] + list(out_shape),
        in_specs=[ANY] * count + list(in_specs),
        out_specs=[ANY] * count + list(out_specs),
        scratch_shapes=([DMA((count,)), DMA((count,))] if count else []) + list(scratch),
        compiler_params=params,
    )(*arrays, *operands)
    return list(results[count:]), list(results[:count])


def spread_kernel(seq, grp, riders, x_ref, out_ref, send1, recv1, send2, recv2):
    s, g = lax.axis_index("seq"), lax.axis_index("grp")
    line = [(lax.rem(s + k, seq), g) for k in range(1, seq)]
    plane = [(s, lax.rem(g + k, grp)) for k in range(1, grp)]
    greet(line + plane + riders.peers())
    out_ref[pl.ds(g, 1), pl.ds(s, 1)] = x_ref[...][None, None]
    first = [
        send(x_ref, out_ref.at[g, s], send1.at[k], recv1.at[k], peer) for k, peer in enumerate(line)
    ]
    riders.start()
    for copy in first:
        copy.wait()
    second = [
        send(out_ref.at[g], out_ref.at[g], send2.at[k], recv2.at[k], peer)
        for k, peer in enumerate(plane)
    ]
    for copy in second:
        copy.wait()
    riders.finish()


def spread(block, seq, grp, collective_id, riders=()):
    (result,), arrived = carried_call(
        partial(spread_kernel, seq, grp),
        [block],
        [jax.ShapeDtypeStruct((grp, seq) + block.shape, block.dtype)],
        [VMEM],
        [VMEM],
        [DMA((seq - 1,)), DMA((seq - 1,)), DMA((grp - 1,)), DMA((grp - 1,))],
        comm_params(collective_id),
        "gather_gains",
        riders,
    )
    return result, arrived


def total_kernel(
    seq, grp, riders, x_ref, out_ref, line_buf, part, plane_buf, send1, recv1, send2, recv2
):
    s, g = lax.axis_index("seq"), lax.axis_index("grp")
    line = [(lax.rem(s + k, seq), g) for k in range(1, seq)]
    plane = [(s, lax.rem(g + k, grp)) for k in range(1, grp)]
    greet(line + plane + riders.peers())
    riders.start()
    line_buf[pl.ds(s, 1)] = x_ref[...][None]
    first = [
        send(x_ref, line_buf.at[s], send1.at[k], recv1.at[k], peer) for k, peer in enumerate(line)
    ]
    for copy in first:
        copy.wait()
    part[...] = jnp.sum(line_buf[...], axis=0)
    plane_buf[pl.ds(g, 1)] = part[...][None]
    second = [
        send(part, plane_buf.at[g], send2.at[k], recv2.at[k], peer) for k, peer in enumerate(plane)
    ]
    for copy in second:
        copy.wait()
    out_ref[...] = jnp.sum(plane_buf[...], axis=0)
    riders.finish()


def total(block, seq, grp, collective_id, riders=()):
    (result,), arrived = carried_call(
        partial(total_kernel, seq, grp),
        [block],
        [jax.ShapeDtypeStruct(block.shape, block.dtype)],
        [VMEM],
        [VMEM],
        [
            pltpu.VMEM((seq,) + block.shape, block.dtype),
            pltpu.VMEM(block.shape, block.dtype),
            pltpu.VMEM((grp,) + block.shape, block.dtype),
            DMA((seq - 1,)),
            DMA((seq - 1,)),
            DMA((grp - 1,)),
            DMA((grp - 1,)),
        ],
        comm_params(collective_id),
        "sum_gains",
        riders,
    )
    return result, arrived


def plane_peers(high):
    s, g = lax.axis_index("seq"), lax.axis_index("grp")
    a, b = g // 2, lax.rem(g, 2)
    across = (s, a * 2 + 1 - b)
    along = [(s, lax.rem(a + k, high) * 2 + b) for k in range(1, high)]
    return a, b, across, along


def gather_rows_kernel(count, high, riders, *refs):
    sources, targets = refs[:count], refs[count : 2 * count]
    send_sems, recv_sems, local_sems = refs[2 * count :]
    a, b, across, along = plane_peers(high)
    greet([across] + along + riders.peers())
    riders.start()
    def pusher(i):
        slots = iter(range(4 * high))

        def push(what, where, peer):
            k = next(slots)
            return send(what, where, send_sems.at[i, k], recv_sems.at[i, k], peer)

        return push

    started, local = [], []
    for i in range(count):
        src, dst, push = sources[i], targets[i], pusher(i)
        copy = pltpu.make_async_copy(src, dst.at[:, a, b], local_sems.at[i])
        copy.start()
        local.append(copy)
        over0 = push(src.at[0], dst.at[0, a, b], across)
        up1 = [push(src.at[1], dst.at[1, a, b], peer) for peer in along]
        over1 = push(src.at[1], dst.at[1, a, b], across)
        up0 = [push(src.at[0], dst.at[0, a, b], peer) for peer in along]
        started.append((over0, up1, over1, up0, push))
    for i in range(count):
        dst = targets[i]
        over0, up1, over1, up0, push = started[i]
        over0.wait_recv()
        later = [push(dst.at[0, a, 1 - b], dst.at[0, a, 1 - b], peer) for peer in along]
        for k in range(1, high):
            up1[k - 1].wait_recv()
            origin = lax.rem(a + high - k, high)
            later.append(push(dst.at[1, origin, b], dst.at[1, origin, b], across))
        over1.wait_recv()
        for copy in up0 + later:
            copy.wait_recv()
        for copy in [over0, over1] + up0 + up1 + later:
            copy.wait_send()
        local[i].wait()
    riders.finish()


def gather_rows(arrays, grp, collective_id, name, riders=()):
    count, high = len(arrays), grp // 2
    rows, rest = arrays[0].shape[1:]
    result, arrived = carried_call(
        partial(gather_rows_kernel, count, high),
        arrays,
        [jax.ShapeDtypeStruct((2, high, 2, rows, rest), x.dtype) for x in arrays],
        [ANY] * count,
        [ANY] * count,
        [DMA((count, 4 * high)), DMA((count, 4 * high)), DMA((count,))],
        comm_params(collective_id),
        name,
        riders,
    )
    return [x.reshape(2 * grp * rows, rest) for x in result], arrived


def sum_rows_kernel(high, riders, src, out, recv0, mid0, last0, recv1, mid1, last1, own0, own1, send_sems, recv_sems, local_sems):
    a, b, across, along = plane_peers(high)
    greet([across] + along + riders.peers())
    riders.start()
    slots = iter(range(2 * high))

    def push(what, where, peer):
        k = next(slots)
        return send(what, where, send_sems.at[k], recv_sems.at[k], peer)

    over0 = push(src.at[0, :, 1 - b], recv0, across)
    up1 = [
        push(src.at[1, lax.rem(a + k, high)], recv1.at[k - 1], along[k - 1]) for k in range(1, high)
    ]
    load0 = pltpu.make_async_copy(src.at[0, :, b], own0, local_sems.at[0])
    load1 = pltpu.make_async_copy(src.at[1, a], own1, local_sems.at[1])
    load0.start()
    load1.start()
    load0.wait()
    load1.wait()
    over0.wait_recv()
    mid0[...] = (own0[...].astype(F32) + recv0[...].astype(F32)).astype(BF16)
    up0 = [
        push(mid0.at[lax.rem(a + k, high)], last0.at[k - 1], along[k - 1]) for k in range(1, high)
    ]
    for copy in up1:
        copy.wait_recv()
    joined = own1[...].astype(F32)
    for k in range(1, high):
        joined = joined + recv1[k - 1].astype(F32)
    mid1[...] = joined.astype(BF16)
    over1 = push(mid1.at[1 - b], last1, across)
    for copy in up0:
        copy.wait_recv()
    result = own0[pl.ds(a, 1)][0].astype(F32) + recv0[pl.ds(a, 1)][0].astype(F32)
    for k in range(1, high):
        result = result + last0[k - 1].astype(F32)
    out[0] = result
    over1.wait_recv()
    result = own1[pl.ds(b, 1)][0].astype(F32)
    for k in range(1, high):
        result = result + recv1[k - 1, pl.ds(b, 1)][0].astype(F32)
    out[1] = result + last1[...].astype(F32)
    for copy in [over0, over1] + up0 + up1:
        copy.wait_send()
    riders.finish()


def sum_rows(partial_sums, grp, collective_id, name, riders=()):
    high = grp // 2
    tokens, width = partial_sums.shape
    rows = tokens // (2 * grp)
    parts = partial_sums.astype(BF16).reshape(2, high, 2, rows, width)
    (result,), arrived = carried_call(
        partial(sum_rows_kernel, high),
        [parts],
        [jax.ShapeDtypeStruct((2, rows, width), F32)],
        [ANY],
        [VMEM],
        [
            pltpu.VMEM((high, rows, width), BF16),
            pltpu.VMEM((high, rows, width), BF16),
            pltpu.VMEM((high - 1, rows, width), BF16),
            pltpu.VMEM((high - 1, 2, rows, width), BF16),
            pltpu.VMEM((2, rows, width), BF16),
            pltpu.VMEM((rows, width), BF16),
            pltpu.VMEM((high, rows, width), BF16),
            pltpu.VMEM((2, rows, width), BF16),
            DMA((2 * high,)),
            DMA((2 * high,)),
            DMA((2,)),
        ],
        comm_params(collective_id),
        name,
        riders,
    )
    return result, arrived


def pair_peer():
    s, g = lax.axis_index("seq"), lax.axis_index("grp")
    side = lax.rem(s // 2, 2)
    return side, (s + 2 - 4 * side, g)


def gather_pair_kernel(high, src, dst, send_sems, recv_sems, pair_sems, local_sem):
    a, b, across, along = plane_peers(high)
    side, pair = pair_peer()
    greet([across, pair] + along)
    over_pair = send(src, dst.at[side, :, a, b], pair_sems.at[0], pair_sems.at[1], pair)
    local = pltpu.make_async_copy(src, dst.at[side, :, a, b], local_sem)
    local.start()

    def spread_plane(i, side, first, second):
        slots = iter(range(4 * high))

        def push(what, where, peer):
            k = next(slots)
            return send(what, where, send_sems.at[i, k], recv_sems.at[i, k], peer)

        over0 = push(first, dst.at[side, 0, a, b], across)
        up1 = [push(second, dst.at[side, 1, a, b], peer) for peer in along]
        over1 = push(second, dst.at[side, 1, a, b], across)
        up0 = [push(first, dst.at[side, 0, a, b], peer) for peer in along]
        over0.wait_recv()
        passed = dst.at[side, 0, a, 1 - b]
        later = [push(passed, passed, peer) for peer in along]
        for k in range(1, high):
            up1[k - 1].wait_recv()
            passed = dst.at[side, 1, lax.rem(a + high - k, high), b]
            later.append(push(passed, passed, across))
        return [over1] + up0 + later, [over0] + up1

    late0, early0 = spread_plane(0, side, src.at[0], src.at[1])
    over_pair.wait_recv()
    other = 1 - side
    late1, early1 = spread_plane(1, other, dst.at[other, 0, a, b], dst.at[other, 1, a, b])
    for copy in late0 + late1:
        copy.wait_recv()
    for copy in early0 + early1 + late0 + late1 + [over_pair]:
        copy.wait_send()
    local.wait()


def gather_pair(array, grp, collective_id, name):
    high = grp // 2
    rows, width = array.shape[1:]
    result = pl.pallas_call(
        partial(gather_pair_kernel, high),
        name=name,
        out_shape=jax.ShapeDtypeStruct((2, 2, high, 2, rows, width), array.dtype),
        in_specs=[ANY],
        out_specs=ANY,
        scratch_shapes=[DMA((2, 4 * high)), DMA((2, 4 * high)), DMA((2,)), DMA],
        compiler_params=comm_params(collective_id),
    )(array)
    return result.reshape(4 * grp * rows, width)


def sum_pair_kernel(
    high, riders, src, out, recv0, mid0, last0, recv1, mid1, last1, own0, own1, given, taken, send_sems, recv_sems, pair_sems, local_sems
):
    a, b, across, along = plane_peers(high)
    side, pair = pair_peer()
    greet([across, pair] + along + riders.peers())
    riders.start()

    def pusher(i):
        slots = iter(range(2 * high))

        def push(what, where, peer):
            k = next(slots)
            return send(what, where, send_sems.at[i, k], recv_sems.at[i, k], peer)

        return push

    parts = []
    for i, part in ((0, 1 - side), (1, side)):
        push = pusher(i)
        over0 = push(src.at[part, 0, :, 1 - b], recv0.at[i], across)
        up1 = [
            push(src.at[part, 1, lax.rem(a + k, high)], recv1.at[i, k - 1], along[k - 1])
            for k in range(1, high)
        ]
        load0 = pltpu.make_async_copy(src.at[part, 0, :, b], own0.at[i], local_sems.at[i, 0])
        load1 = pltpu.make_async_copy(src.at[part, 1, a], own1.at[i], local_sems.at[i, 1])
        load0.start()
        load1.start()
        parts.append((push, over0, up1, load0, load1))
    started = []
    for i in range(2):
        push, over0, up1, load0, load1 = parts[i]
        load0.wait()
        load1.wait()
        over0.wait_recv()
        mid0[i] = (own0[i].astype(F32) + recv0[i].astype(F32)).astype(BF16)
        up0 = [
            push(mid0.at[i, lax.rem(a + k, high)], last0.at[i, k - 1], along[k - 1])
            for k in range(1, high)
        ]
        for copy in up1:
            copy.wait_recv()
        joined = own1[i].astype(F32)
        for k in range(1, high):
            joined = joined + recv1[i, k - 1].astype(F32)
        mid1[i] = joined.astype(BF16)
        over1 = push(mid1.at[i, 1 - b], last1.at[i], across)
        started.append((up0, over1))
    over_pair = None
    for i in range(2):
        up0, over1 = started[i]
        for copy in up0:
            copy.wait_recv()
        result0 = own0[i, pl.ds(a, 1)][0].astype(F32) + recv0[i, pl.ds(a, 1)][0].astype(F32)
        for k in range(1, high):
            result0 = result0 + last0[i, k - 1].astype(F32)
        over1.wait_recv()
        result1 = own1[i, pl.ds(b, 1)][0].astype(F32) + last1[i].astype(F32)
        for k in range(1, high):
            result1 = result1 + recv1[i, k - 1, pl.ds(b, 1)][0].astype(F32)
        if i == 0:
            given[0] = result0.astype(BF16)
            given[1] = result1.astype(BF16)
            over_pair = send(given, taken, pair_sems.at[0], pair_sems.at[1], pair)
        else:
            out[0] = result0
            out[1] = result1
    over_pair.wait_recv()
    out[...] += taken[...].astype(F32)
    over_pair.wait_send()
    for i in range(2):
        push, over0, up1, load0, load1 = parts[i]
        up0, over1 = started[i]
        for copy in [over0, over1] + up0 + up1:
            copy.wait_send()
    riders.finish()


def sum_pair(partial_sums, grp, collective_id, name, riders=()):
    high = grp // 2
    tokens, width = partial_sums.shape
    rows = tokens // (4 * grp)
    parts = partial_sums.astype(BF16).reshape(2, 2, high, 2, rows, width)
    (result,), arrived = carried_call(
        partial(sum_pair_kernel, high),
        [parts],
        [jax.ShapeDtypeStruct((2, rows, width), F32)],
        [ANY],
        [VMEM],
        [
            pltpu.VMEM((2, high, rows, width), BF16),
            pltpu.VMEM((2, high, rows, width), BF16),
            pltpu.VMEM((2, high - 1, rows, width), BF16),
            pltpu.VMEM((2, high - 1, 2, rows, width), BF16),
            pltpu.VMEM((2, 2, rows, width), BF16),
            pltpu.VMEM((2, rows, width), BF16),
            pltpu.VMEM((2, high, rows, width), BF16),
            pltpu.VMEM((2, 2, rows, width), BF16),
            pltpu.VMEM((2, rows, width), BF16),
            pltpu.VMEM((2, rows, width), BF16),
            DMA((2, 2 * high)),
            DMA((2, 2 * high)),
            DMA((2,)),
            DMA((2, 2)),
        ],
        comm_params(collective_id),
        name,
        riders,
    )
    return result, arrived


def turn_half(values):
    half = values.shape[-1] // 2
    return jnp.concatenate([-values[:, half:], values[:, :half]], axis=-1)


def heads_kernel(queries, keys, raw, gains, cosine, sine, out):
    head = pl.program_id(0)

    @pl.when(head < queries + keys)
    def _():
        unit, _ = normalize(raw[...])
        scaled = unit * jnp.where(head < queries, gains[0:1], gains[1:2])
        out[...] = (scaled * cosine[...] + turn_half(scaled) * sine[...]).astype(BF16)

    @pl.when(head >= queries + keys)
    def _():
        out[...] = raw[...].astype(BF16)


def heads_forward(raw, gains, cosine, sine, queries, keys, dim):
    tokens, width = raw.shape
    column = pl.BlockSpec((tokens, dim), lambda h: (0, h))
    table = pl.BlockSpec((tokens, dim), lambda h: (0, 0))
    return pl.pallas_call(
        partial(heads_kernel, queries, keys),
        name="heads_forward",
        grid=(width // dim,),
        out_shape=jax.ShapeDtypeStruct((tokens, width), BF16),
        in_specs=[column, pl.BlockSpec((8, dim), lambda h: (0, 0)), table, table],
        out_specs=column,
    )(raw, gains, cosine, sine)


def heads_back_kernel(queries, keys, raw, grads, gains, cosine, sine, out, gain_out):
    head = pl.program_id(0)

    @pl.when(head < queries + keys)
    def _():
        unit, inverse = normalize(raw[...])
        given = grads[...]
        turned = given * cosine[...] - turn_half(given * sine[...])
        gain_out[...] = jnp.broadcast_to(
            jnp.sum(turned * unit, axis=0, keepdims=True)[None], gain_out.shape
        )
        scaled = turned * jnp.where(head < queries, gains[0:1], gains[1:2])
        out[...] = norm_back(scaled, unit, inverse).astype(BF16)

    @pl.when(head >= queries + keys)
    def _():
        gain_out[...] = jnp.zeros_like(gain_out)
        out[...] = grads[...].astype(BF16)


def heads_backward(raw, grads, gains, cosine, sine, queries, keys, dim):
    tokens, width = raw.shape
    column = pl.BlockSpec((tokens, dim), lambda h: (0, h))
    table = pl.BlockSpec((tokens, dim), lambda h: (0, 0))
    return pl.pallas_call(
        partial(heads_back_kernel, queries, keys),
        name="heads_backward",
        grid=(width // dim,),
        out_shape=[
            jax.ShapeDtypeStruct((tokens, width), BF16),
            jax.ShapeDtypeStruct((width // dim, 8, dim), F32),
        ],
        in_specs=[column, column, pl.BlockSpec((8, dim), lambda h: (0, 0)), table, table],
        out_specs=[column, pl.BlockSpec((1, 8, dim), lambda h: (h, 0, 0))],
    )(raw, grads, gains, cosine, sine)


def half_line_peers(chips):
    s, g = lax.axis_index("seq"), lax.axis_index("grp")
    chip, core = s // 2, lax.rem(s, 2)
    place = lax.rem(chip, chips)
    others = [((chip - place + lax.rem(place + k, chips)) * 2 + core, g) for k in range(1, chips)]
    return place, core, (s + 1 - 2 * core, g), others


def remote(src, dst, send_sem, recv_sem, peer):
    return pltpu.make_async_remote_copy(
        src_ref=src,
        dst_ref=dst,
        send_sem=send_sem,
        recv_sem=recv_sem,
        device_id=peer,
        device_id_type=MESH,
    )


def allowed_pairs(query_block, key_block, length, rows, repeat, diagonal):
    key_pos = key_block * rows + lax.broadcasted_iota(jnp.int32, (rows, repeat * rows), 0)
    allowed = key_pos < length
    if diagonal:
        query_pos = lax.broadcasted_iota(jnp.int32, (rows, repeat * rows), 1)
        allowed = allowed & (key_pos <= query_block * rows + lax.rem(query_pos, rows))
    return allowed


def stacked(ref, part, rows, first, repeat, dim):
    return jnp.concatenate(
        [
            ref[part * rows : (part + 1) * rows, (first + r) * dim : (first + r + 1) * dim]
            for r in range(repeat)
        ],
        axis=0,
    )


def attend_kernel(
    shape,
    chips,
    riders,
    length,
    q,
    kv_home,
    mixed,
    mixed_low,
    log_total,
    kv_all,
    kv_buf,
    acc,
    sums,
    lane_send,
    lane_recv,
    cross_send,
    cross_recv,
    local_sems,
):
    rows, keys, repeat, dim = shape
    scale = 1.0 / math.sqrt(dim)
    place, core, cross, others = half_line_peers(chips)
    me = place * 2 + core
    greet([cross] + others + riders.peers())
    home = pltpu.make_async_copy(kv_home, kv_all.at[me], local_sems.at[0])
    home.start()

    def over(i, src, owner):
        return remote(src, kv_all.at[owner], cross_send.at[i], cross_recv.at[i], cross)

    lanes = [
        remote(kv_home, kv_all.at[me], lane_send.at[k], lane_recv.at[k], peer)
        for k, peer in enumerate(others)
    ]
    crossed = [over(0, kv_home, me)]
    for copy in lanes + crossed:
        copy.start()
    riders.start()
    acc[...] = jnp.zeros_like(acc)
    sums[...] = jnp.zeros_like(sums)

    def piece(owner, query_part, key_part, diagonal):
        query_block, key_block = me + query_part * 2 * chips, owner + key_part * 2 * chips
        allowed = allowed_pairs(query_block, key_block, length[0], rows, repeat, diagonal)
        here = slice(key_part * rows, (key_part + 1) * rows)
        for k in range(keys):
            unit = query_part * keys + k
            kk = kv_buf[here, k * dim : (k + 1) * dim]
            vv = kv_buf[here, (keys + k) * dim : (keys + k + 1) * dim]
            scores = nt(kk, stacked(q, query_part, rows, k * repeat, repeat, dim)) * scale
            weights = jnp.where(allowed, jnp.exp(scores), 0.0)
            sums[unit] += jnp.sum(weights, axis=0, keepdims=True)
            acc[unit] += tn(vv, weights.astype(BF16))

    def work(src, owner, own):
        load = pltpu.make_async_copy(src, kv_buf, local_sems.at[1])
        load.start()
        load.wait()
        piece(owner, 1, 0, False)
        if own:
            piece(owner, 0, 0, True)
            piece(owner, 1, 1, True)
        else:

            @pl.when(owner < me)
            def _():
                piece(owner, 0, 0, False)
                piece(owner, 1, 1, False)

    work(kv_home, me, True)
    for k in range(chips):
        near = lax.rem(place + chips - k, chips) * 2
        if k:
            owner = near + core
            lanes[k - 1].wait_recv()
            crossed.append(over(k, kv_all.at[owner], owner))
            crossed[k].start()
            work(kv_all.at[owner], owner, False)
        owner = near + 1 - core
        crossed[k].wait_recv()
        work(kv_all.at[owner], owner, False)
    for part in range(2):
        for k in range(keys):
            unit = part * keys + k
            log_total[unit] = jnp.log(sums[unit])
            result = (acc[unit] / sums[unit]).T
            for r in range(repeat):
                cut = result[r * rows : (r + 1) * rows]
                h = k * repeat + r
                mixed[part * rows : (part + 1) * rows, h * dim : (h + 1) * dim] = cut
                mixed_low[part * rows : (part + 1) * rows, h * dim : (h + 1) * dim] = cut.astype(BF16)
    home.wait()
    for copy in lanes + crossed:
        copy.wait_send()
    riders.finish()


def attend(length, q, kv_home, seq, keys, repeat, dim, collective_id, riders=()):
    tokens, kv_width = kv_home.shape
    rows, width = tokens // 2, keys * repeat * dim
    chips = seq // 4
    return carried_call(
        partial(attend_kernel, (rows, keys, repeat, dim), chips),
        [length, q, kv_home],
        [
            jax.ShapeDtypeStruct((tokens, width), F32),
            jax.ShapeDtypeStruct((tokens, width), BF16),
            jax.ShapeDtypeStruct((2 * keys, 1, repeat * rows), F32),
            jax.ShapeDtypeStruct((2 * chips, tokens, kv_width), BF16),
        ],
        [pl.BlockSpec(memory_space=pltpu.SMEM), VMEM, ANY],
        [VMEM, VMEM, VMEM, ANY],
        [
            pltpu.VMEM((tokens, kv_width), BF16),
            pltpu.VMEM((2 * keys, dim, repeat * rows), F32),
            pltpu.VMEM((2 * keys, 1, repeat * rows), F32),
            DMA((chips,)),
            DMA((chips,)),
            DMA((chips,)),
            DMA((chips,)),
            DMA((2,)),
        ],
        comm_params(collective_id),
        "attend",
        riders,
    )


def attend_back_kernel(
    shape,
    chips,
    length,
    q,
    mixed,
    grad_mixed,
    log_total,
    kv_all,
    grad_q,
    grad_kv,
    kv_buf,
    acc,
    delta,
    mine,
    lane_out,
    lane_in,
    cross_out,
    cross_in,
    lane_send,
    lane_recv,
    cross_send,
    cross_recv,
    local_sem,
):
    rows, keys, repeat, dim = shape
    scale = 1.0 / math.sqrt(dim)
    place, core, cross, others = half_line_peers(chips)
    me = place * 2 + core
    greet([cross] + others)
    acc[...] = jnp.zeros_like(acc)
    for part in range(2):
        for k in range(keys):
            product = stacked(mixed, part, rows, k * repeat, repeat, dim) * stacked(
                grad_mixed, part, rows, k * repeat, repeat, dim
            ).astype(F32)
            delta[part * keys + k] = jnp.sum(product.T, axis=0, keepdims=True)

    def piece(owner, query_part, key_part, diagonal, first):
        query_block, key_block = me + query_part * 2 * chips, owner + key_part * 2 * chips
        allowed = allowed_pairs(query_block, key_block, length[0], rows, repeat, diagonal)
        here = slice(key_part * rows, (key_part + 1) * rows)
        for k in range(keys):
            unit = query_part * keys + k
            key_cut, value_cut = slice(k * dim, (k + 1) * dim), slice((keys + k) * dim, (keys + k + 1) * dim)
            kk, vv = kv_buf[here, key_cut], kv_buf[here, value_cut]
            qq = stacked(q, query_part, rows, k * repeat, repeat, dim)
            gg = stacked(grad_mixed, query_part, rows, k * repeat, repeat, dim)
            weights = jnp.where(allowed, jnp.exp(nt(kk, qq) * scale - log_total[unit]), 0.0)
            grad_scores = (weights * (nt(vv, gg) - delta[unit])).astype(BF16)
            grad_k, grad_v = nn(grad_scores, qq) * scale, nn(weights.astype(BF16), gg)
            if first:
                mine[here, key_cut] = grad_k
                mine[here, value_cut] = grad_v
            else:
                mine[here, key_cut] += grad_k
                mine[here, value_cut] += grad_v
            acc[unit] += tn(grad_scores, kk)

    def work(owner, own):
        load = pltpu.make_async_copy(kv_all.at[owner], kv_buf, local_sem)
        load.start()
        load.wait()
        piece(owner, 1, 0, False, True)
        if own:
            piece(owner, 0, 0, True, False)
            piece(owner, 1, 1, True, True)
        else:

            @pl.when(owner < me)
            def _():
                piece(owner, 0, 0, False, False)
                piece(owner, 1, 1, False, True)

            @pl.when(owner > me)
            def _():
                mine[rows:, :] = jnp.zeros_like(mine[rows:, :])

    lanes, crossed = [], []
    for k in list(range(1, chips)) + [0]:
        near = lax.rem(place + k, chips) * 2
        work(near + 1 - core, False)
        cross_out[k] = mine[...].astype(BF16)
        copy = remote(cross_out.at[k], cross_in.at[k], cross_send.at[k], cross_recv.at[k], cross)
        copy.start()
        crossed.append(copy)
        work(near + core, k == 0)
        copy.wait_recv()
        mine[...] += cross_in[k].astype(F32)
        if k:
            lane_out[k - 1] = mine[...].astype(BF16)
            copy = remote(
                lane_out.at[k - 1], lane_in.at[k - 1], lane_send.at[k - 1], lane_recv.at[k - 1], others[k - 1]
            )
            copy.start()
            lanes.append(copy)
    for k, copy in enumerate(lanes):
        copy.wait_recv()
        mine[...] += lane_in[k].astype(F32)
    grad_kv[...] = mine[...]
    for part in range(2):
        for k in range(keys):
            for r in range(repeat):
                h = k * repeat + r
                grad_q[part * rows : (part + 1) * rows, h * dim : (h + 1) * dim] = (
                    acc[part * keys + k, r * rows : (r + 1) * rows] * scale
                )
    for copy in lanes + crossed:
        copy.wait_send()


def attend_back(length, q, kv_all, mixed, grad_mixed, log_total, keys, repeat, dim, collective_id):
    owners, tokens, kv_width = kv_all.shape
    rows, width = tokens // 2, keys * repeat * dim
    chips = owners // 2
    slots = pltpu.VMEM((chips, tokens, kv_width), BF16)
    return pl.pallas_call(
        partial(attend_back_kernel, (rows, keys, repeat, dim), chips),
        name="attend_back",
        in_specs=[pl.BlockSpec(memory_space=pltpu.SMEM), VMEM, VMEM, VMEM, VMEM, ANY],
        out_specs=[VMEM, VMEM],
        scratch_shapes=[
            pltpu.VMEM((tokens, kv_width), BF16),
            pltpu.VMEM((2 * keys, repeat * rows, dim), F32),
            pltpu.VMEM((2 * keys, 1, repeat * rows), F32),
            pltpu.VMEM((tokens, kv_width), F32),
            slots,
            slots,
            slots,
            slots,
            DMA((chips,)),
            DMA((chips,)),
            DMA((chips,)),
            DMA((chips,)),
            DMA,
        ],
        out_shape=[
            jax.ShapeDtypeStruct((tokens, width), F32),
            jax.ShapeDtypeStruct((tokens, kv_width), F32),
        ],
        compiler_params=comm_params(collective_id, 48),
    )(length, q, mixed, grad_mixed, log_total, kv_all)


def load_weights(own, other, first, weights, sems):
    side = lax.rem(lax.axis_index("seq") // 2, 2)
    members = sems.shape[1]
    depth, width = own.shape[0] // members, weights.shape[1]
    copies = []
    for i in range(members):
        for k, (src, which) in enumerate(((own, side), (other, 1 - side))):
            block = ((i // 2) * 2 + which) * 2 + i % 2
            copy = pltpu.make_async_copy(
                src.at[pl.ds(i * depth, depth), pl.ds(first, width)],
                weights.at[pl.ds(block * depth, depth)],
                sems.at[k, i],
            )
            copy.start()
            copies.append(copy)
    for copy in copies:
        copy.wait()
    return depth


def member_place(block):
    return (block // 4) * 4 + lax.rem(block, 2) * 2 + lax.rem(block // 2, 2)


def mlp_kernel(own, other, rows, cot, inner, grad_pre, grad_down, weights, sems):
    depth = load_weights(own, other, 0, weights, sems)
    units = inner.shape[1]
    step = 256 if units % 256 == 0 else 128
    tile = 256
    tiles = rows.shape[0] // tile

    def one(t, carry):
        here = pl.ds(pl.multiple_of(lax.rem(t, tiles) * tile, tile), tile)
        first = pl.multiple_of((t // tiles) * step, step)
        cols = pl.ds(first, step)
        x = rows[here, :]
        gate = nn(x, weights[:, cols])
        up = nn(x, weights[:, pl.ds(units + first, step)])
        grad = nn(cot[here, :], weights[:, pl.ds(2 * units + first, step)])
        sigmoid = jax.nn.sigmoid(gate)
        silu = gate * sigmoid
        inner[here, cols] = (silu * up).astype(BF16)
        grad_pre[here, cols] = (grad * up * sigmoid * (1.0 + gate * (1.0 - sigmoid))).astype(BF16)
        grad_pre[here, pl.ds(units + first, step)] = (grad * silu).astype(BF16)
        return carry

    lax.fori_loop(0, tiles * (units // step), one, 0)

    def down(j, carry):
        x = cot[:, pl.ds(pl.multiple_of(j * depth, depth), depth)]
        place = pl.multiple_of(member_place(j) * depth, depth)
        grad_down[pl.ds(place, depth), :] = tn(x, inner[...]).astype(BF16)
        return carry

    lax.fori_loop(0, rows.shape[1] // depth, down, 0)


def mlp(own, other, rows, cot):
    (tokens, width), columns = rows.shape, own.shape[1]
    units, members = columns // 3, lax.axis_size("seq") // 2
    return pl.pallas_call(
        mlp_kernel,
        name="mlp",
        in_specs=[ANY, ANY, VMEM, VMEM],
        out_specs=[VMEM, VMEM, VMEM],
        out_shape=[
            jax.ShapeDtypeStruct((tokens, units), BF16),
            jax.ShapeDtypeStruct((tokens, 2 * units), BF16),
            jax.ShapeDtypeStruct((width, units), BF16),
        ],
        scratch_shapes=[pltpu.VMEM((width, columns), BF16), DMA((2, members))],
        compiler_params=pltpu.CompilerParams(vmem_limit_bytes=52 * 2**20),
    )(own, other, rows, cot)


def mlp_back_kernel(own, other, rows, grad_pre, grad_w, grad_rows, weights, sems):
    depth = load_weights(own, other, 0, weights, sems)
    tile = 256

    def one(j, carry):
        x = rows[:, pl.ds(pl.multiple_of(j * depth, depth), depth)]
        place = pl.multiple_of(member_place(j) * depth, depth)
        grad_w[pl.ds(place, depth), :] = tn(x, grad_pre[...]).astype(BF16)
        return carry

    lax.fori_loop(0, rows.shape[1] // depth, one, 0)

    def two(t, carry):
        here = pl.ds(pl.multiple_of(t * tile, tile), tile)
        grad_rows[here, :] = nt(grad_pre[here, :], weights[...]).astype(BF16)
        return carry

    lax.fori_loop(0, rows.shape[0] // tile, two, 0)


def mlp_back(own, other, rows, grad_pre):
    (tokens, width), columns = rows.shape, grad_pre.shape[1]
    return pl.pallas_call(
        mlp_back_kernel,
        name="mlp_back",
        in_specs=[ANY, ANY, VMEM, VMEM],
        out_specs=[VMEM, VMEM],
        out_shape=[
            jax.ShapeDtypeStruct((width, columns), BF16),
            jax.ShapeDtypeStruct((tokens, width), BF16),
        ],
        scratch_shapes=[pltpu.VMEM((width, columns), BF16), DMA((2, lax.axis_size("seq") // 2))],
        compiler_params=pltpu.CompilerParams(vmem_limit_bytes=52 * 2**20),
    )(own, other, rows, grad_pre)


def mlp_out_kernel(own, other, inner, out, weights, sems):
    load_weights(own, other, 2 * inner.shape[1], weights, sems)
    tile = 256

    def one(t, carry):
        here = pl.ds(pl.multiple_of(t * tile, tile), tile)
        out[here, :] = nt(inner[here, :], weights[...]).astype(BF16)
        return carry

    lax.fori_loop(0, inner.shape[0] // tile, one, 0)


def mlp_out(own, other, inner, width):
    tokens, units = inner.shape
    return pl.pallas_call(
        mlp_out_kernel,
        name="mlp_out",
        in_specs=[ANY, ANY, VMEM],
        out_specs=VMEM,
        out_shape=jax.ShapeDtypeStruct((tokens, width), BF16),
        scratch_shapes=[pltpu.VMEM((width, units), BF16), DMA((2, lax.axis_size("seq") // 2))],
        compiler_params=pltpu.CompilerParams(vmem_limit_bytes=52 * 2**20),
    )(own, other, inner)


def shards(
    tokens,
    lengths,
    attn_gain,
    w_query,
    w_key,
    w_value,
    query_gain,
    key_gain,
    w_out,
    mlp_gain,
    w_gate,
    w_up,
    w_down,
    cotangent,
):
    seq, grp = lax.axis_size("seq"), lax.axis_size("grp")
    seq_index, grp_index = lax.axis_index("seq"), lax.axis_index("grp")
    local_rows, width = tokens.shape[1:]
    rows = local_rows * grp
    dim = query_gain.shape[0]
    queries, keys = w_query.shape[1] // dim, w_key.shape[1] // dim
    repeat = queries // keys
    hidden_units = w_gate.shape[1]
    chunk = attn_gain.shape[0]
    depth = width // seq

    line = seq // 2
    row = seq_index // line

    def to_give(values):
        return lax.dynamic_index_in_dim(values, 1 - row, 0, keepdims=False)

    def both_rows(values, taken):
        kept = lax.dynamic_index_in_dim(values, row, 0, keepdims=False)
        return jnp.stack([jnp.where(row == 0, kept, taken), jnp.where(row == 0, taken, kept)])

    blocks = lax.rem(seq_index, line) + jnp.arange(2, dtype=jnp.int32) * line
    length = lax.dynamic_slice(lengths, (row,), (1,))

    side = lax.rem(seq_index // 2, 2)
    half_units = hidden_units // 2
    pairs = [(s, s ^ 2) for s in range(seq)]
    same_side = [[s for s in range(seq) if s // 2 % 2 == k] for k in range(2)]

    def half(which):
        cut = [
            lax.dynamic_slice_in_dim(w, which * half_units, half_units, 1)
            for w in (w_gate, w_up, w_down.T)
        ]
        return jnp.concatenate(cut, axis=1)

    def gather_side(weights):
        return lax.all_gather(weights, "seq", axis=0, tiled=True, axis_index_groups=same_side)

    def sum_side(grads):
        return lax.psum_scatter(
            grads, "seq", scatter_dimension=0, tiled=True, axis_index_groups=same_side
        )

    def half_to_give(sums):
        return lax.dynamic_slice_in_dim(sums, (1 - side) * depth, depth, 0)

    def from_halves(sums, taken, count):
        kept = lax.dynamic_slice_in_dim(sums, side * depth, depth, 0)
        low = jnp.where(side == 0, kept, taken).astype(F32).reshape(depth, count, half_units)
        high = jnp.where(side == 0, taken, kept).astype(F32).reshape(depth, count, half_units)
        return [jnp.concatenate([low[:, i], high[:, i]], axis=1) for i in range(count)]

    projections = jnp.concatenate([w_query, w_key, w_value], axis=1)
    full_qkv = lax.all_gather(projections, "seq", axis=0, tiled=True)
    lane = max(128, chunk)
    packed = jnp.zeros((8, lane), F32).at[0, :chunk].set(attn_gain).at[1, :chunk].set(mlp_gain)
    spread_gains, (taken_tokens,) = spread(packed, seq, grp, 1, [("opposite", to_give(tokens))])
    spread_gains = spread_gains[:, :, :, :chunk].transpose(2, 1, 0, 3)
    gain_attn = spread_gains[0].reshape(-1)
    gain_mlp = spread_gains[1].reshape(-1)
    full_out = lax.all_gather(after(w_out.T, taken_tokens), "seq", axis=0, tiled=True)
    residual = both_rows(tokens, taken_tokens).astype(F32)
    attn_unit, attn_inverse = normalize(residual)
    (attn_rows,), _ = gather_rows([(attn_unit * gain_attn).astype(BF16)], grp, 2, "gather_inputs")
    token_pos = (blocks[:, None] * grp + grp_index) * local_rows
    token_pos = token_pos + jnp.arange(local_rows, dtype=jnp.int32)[None, :]
    valid_rows = (token_pos < length).astype(F32)
    kept_half, given_half = after((half(side), half(1 - side)), attn_rows)

    raw = nn(attn_rows, full_qkv)
    positions = (blocks[:, None] * rows + jnp.arange(rows, dtype=jnp.int32)[None, :]).reshape(-1)
    frequency = ROPE_BASE ** (-jnp.arange(dim // 2, dtype=F32) * 2.0 / dim)
    angles = positions.astype(F32)[:, None] * frequency[None, :]
    cosine = jnp.tile(jnp.cos(angles), (1, 2))
    sine = jnp.tile(jnp.sin(angles), (1, 2))
    head_gains = jnp.zeros((8, dim), F32).at[0].set(query_gain).at[1].set(key_gain)
    heads = heads_forward(raw, head_gains, cosine, sine, queries, keys, dim)
    q, kv_home = heads[:, : queries * dim], heads[:, queries * dim :]

    (mixed, mixed_low, log_total, kv_all), (taken_cotangent,) = attend(
        length, q, kv_home, seq, keys, repeat, dim, 3, [("opposite", to_give(cotangent))]
    )
    own_side = gather_side(after(kept_half, mixed))
    taken_half = lax.ppermute(after(given_half, mixed), "seq", pairs)
    cot_rows = both_rows(cotangent, taken_cotangent).astype(F32) * valid_rows[:, :, None]
    summed, _ = sum_rows(nt(mixed_low, full_out), grp, 4, "sum_attention")
    hidden = residual + summed

    mlp_unit, mlp_inverse = normalize(hidden)
    taken_half, hidden_in = after((taken_half, (mlp_unit * gain_mlp).astype(BF16)), summed)
    other_side = gather_side(taken_half)
    mlp_rows = gather_pair(hidden_in, grp, 5, "gather_mlp")
    grad_out_rows = gather_pair(after(cot_rows.astype(BF16), mlp_rows), grp, 6, "gather_cotangent")
    inner_low, grad_pre, grad_w_down = mlp(own_side, other_side, mlp_rows, grad_out_rows)
    sum_down = sum_side(grad_w_down)
    grad_w_pre, grad_mlp_part = mlp_back(own_side, other_side, mlp_rows, grad_pre)
    sum_pre = sum_side(grad_w_pre)
    grad_mlp_in, _ = sum_pair(grad_mlp_part, grp, 7, "sum_mlp_back")
    grad_gain_mlp = jnp.sum(grad_mlp_in * mlp_unit, axis=(0, 1))
    grad_hidden = cot_rows + norm_back(grad_mlp_in * gain_mlp, mlp_unit, mlp_inverse)
    (grad_branch,), _ = gather_rows([grad_hidden.astype(BF16)], grp, 8, "gather_branch")

    grad_w_out = tn(grad_branch, mixed_low).astype(BF16)
    sum_out = lax.psum_scatter(grad_w_out, "seq", scatter_dimension=0, tiled=True)
    grad_mixed = nn(after(grad_branch, grad_w_out), full_out).astype(BF16)
    grad_q, grad_kv = attend_back(
        length, q, kv_all, mixed, grad_mixed, log_total, keys, repeat, dim, 9
    )
    grad_heads = jnp.concatenate([grad_q, grad_kv], axis=1)
    grad_raw, head_gain_parts = heads_backward(
        raw, grad_heads, head_gains, cosine, sine, queries, keys, dim
    )
    grad_w_qkv = tn(attn_rows, grad_raw).astype(BF16)
    sum_qkv = lax.psum_scatter(grad_w_qkv, "seq", scatter_dimension=0, tiled=True)
    grad_attn_part = nt(after(grad_raw, grad_w_qkv), full_qkv)
    grad_attn_in, _ = sum_rows(grad_attn_part, grp, 10, "sum_attention_back")
    grad_gain_attn = jnp.sum(grad_attn_in * attn_unit, axis=(0, 1))
    grad_tokens = grad_hidden + norm_back(grad_attn_in * gain_attn, attn_unit, attn_inverse)

    out_part = mlp_out(own_side, other_side, after(inner_low, grad_attn_in), width)
    summed, (taken_grads,) = sum_pair(
        out_part, grp, 11, "sum_output", [("opposite", to_give(grad_tokens).astype(BF16))]
    )
    grad_tokens = both_rows(grad_tokens, taken_grads.astype(F32))
    taken_down = lax.ppermute(half_to_give(sum_down), "seq", pairs)
    taken_pre = lax.ppermute(half_to_give(sum_pre), "seq", pairs)
    (out_down,) = from_halves(sum_down, taken_down, 1)
    out_gate, out_up = from_halves(sum_pre, taken_pre, 2)
    output = (hidden + summed).astype(BF16)

    head_gain_grads = jnp.stack(
        [
            jnp.sum(head_gain_parts[:queries, 0], axis=0),
            jnp.sum(head_gain_parts[queries : queries + keys, 0], axis=0),
        ]
    )
    vector = jnp.concatenate([grad_gain_attn, grad_gain_mlp, head_gain_grads.reshape(-1)])
    padded = -(-vector.shape[0] // 1024) * 1024
    vector = jnp.pad(vector, (0, padded - vector.shape[0])).reshape(-1, 128)
    sums, (taken_output,) = total(after(vector, (taken_down, taken_pre)), seq, grp, 12, [("opposite", to_give(output))])
    sums = sums.reshape(-1)
    output = both_rows(output, taken_output)
    place = (seq_index * grp + grp_index) * chunk
    out_attn_gain = lax.dynamic_slice(sums, (place,), (chunk,))
    out_mlp_gain = lax.dynamic_slice(sums, (width + place,), (chunk,))
    out_query_gain = sums[2 * width : 2 * width + dim]
    out_key_gain = sums[2 * width + dim : 2 * width + 2 * dim]

    sum_qkv = sum_qkv.astype(F32)
    cuts = (queries * dim, (queries + keys) * dim)
    return (
        output,
        grad_tokens,
        out_attn_gain,
        sum_qkv[:, : cuts[0]],
        sum_qkv[:, cuts[0] : cuts[1]],
        sum_qkv[:, cuts[1] :],
        out_query_gain,
        out_key_gain,
        sum_out.astype(F32).T,
        out_mlp_gain,
        out_gate,
        out_up,
        out_down.T,
    )


def solution(mesh):
    rows = P(None, ("seq", "grp"), None)
    vector = P(("seq", "grp"))
    wide, tall = P("seq", "grp"), P("grp", "seq")
    return jax.shard_map(
        shards,
        mesh=mesh,
        in_specs=(
            rows,
            P(),
            vector,
            wide,
            wide,
            wide,
            P(),
            P(),
            tall,
            vector,
            wide,
            wide,
            tall,
            rows,
        ),
        out_specs=(
            rows,
            rows,
            vector,
            wide,
            wide,
            wide,
            P(),
            P(),
            tall,
            vector,
            wide,
            wide,
            tall,
        ),
        check_vma=False,
    )
```

```python
from functools import partial
import math

import jax
import jax.numpy as jnp
from jax import lax
from jax.experimental import pallas as pl
from jax.experimental.pallas import tpu as pltpu
from jax.sharding import PartitionSpec as P

EPSILON = 1e-06
ROPE_BASE = 1000000.0
MESH = pl.DeviceIdType.MESH
ANY = pl.BlockSpec(memory_space=pltpu.HBM)
VMEM = pl.BlockSpec(memory_space=pltpu.VMEM)
DMA = pltpu.SemaphoreType.DMA
F32 = jnp.float32
BF16 = jnp.bfloat16


def normalize(values):
    inverse = lax.rsqrt(jnp.mean(values * values, axis=-1, keepdims=True) + EPSILON)
    return (values * inverse, inverse)


def norm_back(gradient, unit_values, inverse):
    return inverse * (
        gradient - unit_values * jnp.mean(gradient * unit_values, axis=-1, keepdims=True)
    )


def after(value, earlier):
    return lax.optimization_barrier((value, earlier))[0]


def nt(a, b):
    return lax.dot_general(a, b, (((1,), (1,)), ((), ())), preferred_element_type=F32)


def tn(a, b):
    return lax.dot_general(a, b, (((0,), (0,)), ((), ())), preferred_element_type=F32)


def nn(a, b):
    return jnp.dot(a, b, preferred_element_type=F32)


NO_COST = pl.CostEstimate(flops=1, bytes_accessed=1, transcendentals=0)


def comm_params(collective_id, mib=32):
    return pltpu.CompilerParams(
        collective_id=collective_id, has_side_effects=True, vmem_limit_bytes=mib * 2**20
    )


def greet(peers):
    barrier = pltpu.get_barrier_semaphore()
    for peer in peers:
        pl.semaphore_signal(barrier, inc=1, device_id=peer, device_id_type=MESH)
    pl.semaphore_wait(barrier, len(peers))


def send(src, dst, send_sem, recv_sem, peer):
    copy = pltpu.make_async_remote_copy(
        src_ref=src,
        dst_ref=dst,
        send_sem=send_sem,
        recv_sem=recv_sem,
        device_id=peer,
        device_id_type=MESH,
    )
    copy.start()
    return copy


def peer_of(kind):
    s, g = lax.axis_index("seq"), lax.axis_index("grp")
    line = lax.axis_size("seq") // 2
    if kind == "opposite":
        return lax.rem(s + line, 2 * line), g
    if kind == "core":
        return s + 1 - 2 * lax.rem(s, 2), g
    place = lax.rem(s, line)
    return s - place + lax.rem(place + 2 * kind, line), g


def part_of(kind, part):
    s = lax.axis_index("seq")
    line = lax.axis_size("seq") // 2
    if part == "row":
        return 1 - s // line
    return lax.rem(lax.rem(s, line) + 2 * kind, line) // 2


class Riders:
    def __init__(self, kinds, parts, sources, targets, send_sems, recv_sems):
        self.kinds, self.parts, self.sources, self.targets = kinds, parts, sources, targets
        self.send_sems, self.recv_sems = send_sems, recv_sems
        self.copies = []

    def peers(self):
        return [peer_of(kind) for kind in dict.fromkeys(self.kinds)]

    def start(self):
        for i, (kind, part) in enumerate(zip(self.kinds, self.parts)):
            src = self.sources[i] if part is None else self.sources[i].at[part_of(kind, part)]
            self.copies.append(
                send(src, self.targets[i], self.send_sems.at[i], self.recv_sems.at[i], peer_of(kind))
            )

    def finish(self):
        for copy in self.copies:
            copy.wait()


def carried_call(kernel, operands, out_shape, in_specs, out_specs, scratch, params, name, riders=()):
    riders = [rider if len(rider) == 3 else rider + (None,) for rider in riders]
    kinds, parts = [rider[0] for rider in riders], [rider[2] for rider in riders]
    arrays = [rider[1] for rider in riders]
    carried = [x.shape if part is None else x.shape[1:] for x, part in zip(arrays, parts)]
    count, ins, outs = len(arrays), len(in_specs), len(out_specs)

    def body(*refs):
        sources, refs = refs[:count], refs[count:]
        own_in, refs = refs[:ins], refs[ins:]
        targets, refs = refs[:count], refs[count:]
        own_out, refs = refs[:outs], refs[outs:]
        sems, refs = (refs[:2], refs[2:]) if count else ((None, None), refs)
        kernel(Riders(kinds, parts, sources, targets, *sems), *own_in, *own_out, *refs)

    results = pl.pallas_call(
        body,
        name=name,
        cost_estimate=NO_COST,
        out_shape=[jax.ShapeDtypeStruct(shape, x.dtype) for shape, x in zip(carried, arrays)]
        + list(out_shape),
        in_specs=[ANY] * count + list(in_specs),
        out_specs=[ANY] * count + list(out_specs),
        scratch_shapes=([DMA((count,)), DMA((count,))] if count else []) + list(scratch),
        compiler_params=params,
    )(*arrays, *operands)
    return list(results[count:]), list(results[:count])


def spread_kernel(seq, grp, riders, x_ref, out_ref, send1, recv1, send2, recv2):
    s, g = lax.axis_index("seq"), lax.axis_index("grp")
    line = [(lax.rem(s + k, seq), g) for k in range(1, seq)]
    plane = [(s, lax.rem(g + k, grp)) for k in range(1, grp)]
    greet(line + plane + riders.peers())
    out_ref[pl.ds(g, 1), pl.ds(s, 1)] = x_ref[...][None, None]
    first = [
        send(x_ref, out_ref.at[g, s], send1.at[k], recv1.at[k], peer) for k, peer in enumerate(line)
    ]
    riders.start()
    for copy in first:
        copy.wait()
    second = [
        send(out_ref.at[g], out_ref.at[g], send2.at[k], recv2.at[k], peer)
        for k, peer in enumerate(plane)
    ]
    for copy in second:
        copy.wait()
    riders.finish()


def spread(block, seq, grp, collective_id, riders=()):
    (result,), arrived = carried_call(
        partial(spread_kernel, seq, grp),
        [block],
        [jax.ShapeDtypeStruct((grp, seq) + block.shape, block.dtype)],
        [VMEM],
        [VMEM],
        [DMA((seq - 1,)), DMA((seq - 1,)), DMA((grp - 1,)), DMA((grp - 1,))],
        comm_params(collective_id),
        "gather_gains",
        riders,
    )
    return result, arrived


def total_kernel(
    seq, grp, riders, x_ref, out_ref, line_buf, part, plane_buf, send1, recv1, send2, recv2
):
    s, g = lax.axis_index("seq"), lax.axis_index("grp")
    line = [(lax.rem(s + k, seq), g) for k in range(1, seq)]
    plane = [(s, lax.rem(g + k, grp)) for k in range(1, grp)]
    greet(line + plane + riders.peers())
    riders.start()
    line_buf[pl.ds(s, 1)] = x_ref[...][None]
    first = [
        send(x_ref, line_buf.at[s], send1.at[k], recv1.at[k], peer) for k, peer in enumerate(line)
    ]
    for copy in first:
        copy.wait()
    part[...] = jnp.sum(line_buf[...], axis=0)
    plane_buf[pl.ds(g, 1)] = part[...][None]
    second = [
        send(part, plane_buf.at[g], send2.at[k], recv2.at[k], peer) for k, peer in enumerate(plane)
    ]
    for copy in second:
        copy.wait()
    out_ref[...] = jnp.sum(plane_buf[...], axis=0)
    riders.finish()


def total(block, seq, grp, collective_id, riders=()):
    (result,), arrived = carried_call(
        partial(total_kernel, seq, grp),
        [block],
        [jax.ShapeDtypeStruct(block.shape, block.dtype)],
        [VMEM],
        [VMEM],
        [
            pltpu.VMEM((seq,) + block.shape, block.dtype),
            pltpu.VMEM(block.shape, block.dtype),
            pltpu.VMEM((grp,) + block.shape, block.dtype),
            DMA((seq - 1,)),
            DMA((seq - 1,)),
            DMA((grp - 1,)),
            DMA((grp - 1,)),
        ],
        comm_params(collective_id),
        "sum_gains",
        riders,
    )
    return result, arrived


def plane_peers(high):
    s, g = lax.axis_index("seq"), lax.axis_index("grp")
    a, b = g // 2, lax.rem(g, 2)
    across = (s, a * 2 + 1 - b)
    along = [(s, lax.rem(a + k, high) * 2 + b) for k in range(1, high)]
    return a, b, across, along


class PlaneGather:
    def __init__(self, high, first, second, target, send_sems, recv_sems):
        self.high, self.first, self.second, self.target = high, first, second, target
        self.send_sems, self.recv_sems = send_sems, recv_sems
        self.slots = iter(range(4 * high))
        self.place = plane_peers(high)

    def push(self, what, where, peer):
        k = next(self.slots)
        return send(what, where, self.send_sems.at[k], self.recv_sems.at[k], peer)

    def start(self):
        a, b, across, along = self.place
        here0, here1 = self.target.at[0, a, b], self.target.at[1, a, b]
        self.early = [self.push(self.first, here0, across)]
        self.early += [self.push(self.second, here1, peer) for peer in along]
        self.late = [self.push(self.second, here1, across)]
        self.late += [self.push(self.first, here0, peer) for peer in along]

    def forward(self):
        a, b, across, along = self.place
        self.early[0].wait_recv()
        passed = self.target.at[0, a, 1 - b]
        self.late += [self.push(passed, passed, peer) for peer in along]
        for k in range(1, self.high):
            self.early[k].wait_recv()
            passed = self.target.at[1, lax.rem(a + self.high - k, self.high), b]
            self.late.append(self.push(passed, passed, across))

    def finish(self):
        for copy in self.late:
            copy.wait_recv()
        for copy in self.early + self.late:
            copy.wait_send()


def gather_rows_kernel(high, riders, src, dst, send_sems, recv_sems, local_sem):
    a, b, across, along = plane_peers(high)
    greet([across] + along + riders.peers())
    riders.start()
    home = pltpu.make_async_copy(src, dst.at[:, a, b], local_sem)
    home.start()
    plane = PlaneGather(high, src.at[0], src.at[1], dst, send_sems, recv_sems)
    plane.start()
    plane.forward()
    plane.finish()
    home.wait()
    riders.finish()


def plane_shape(array, grp):
    rows, width = array.shape[1:]
    return jax.ShapeDtypeStruct((2, grp // 2, 2, rows, width), array.dtype)


def gather_rows(array, grp, collective_id, name, riders=()):
    high = grp // 2
    (result,), arrived = carried_call(
        partial(gather_rows_kernel, high),
        [array],
        [plane_shape(array, grp)],
        [ANY],
        [ANY],
        [DMA((4 * high,)), DMA((4 * high,)), DMA],
        comm_params(collective_id),
        name,
        riders,
    )
    return result.reshape(2 * grp * array.shape[1], array.shape[2]), arrived


def sum_rows_kernel(high, riders, src, out, recv0, mid0, last0, recv1, mid1, last1, own0, own1, send_sems, recv_sems, local_sems):
    a, b, across, along = plane_peers(high)
    greet([across] + along + riders.peers())
    riders.start()
    slots = iter(range(2 * high))

    def push(what, where, peer):
        k = next(slots)
        return send(what, where, send_sems.at[k], recv_sems.at[k], peer)

    over0 = push(src.at[0, :, 1 - b], recv0, across)
    up1 = [
        push(src.at[1, lax.rem(a + k, high)], recv1.at[k - 1], along[k - 1]) for k in range(1, high)
    ]
    load0 = pltpu.make_async_copy(src.at[0, :, b], own0, local_sems.at[0])
    load1 = pltpu.make_async_copy(src.at[1, a], own1, local_sems.at[1])
    load0.start()
    load1.start()
    load0.wait()
    load1.wait()
    over0.wait_recv()
    mid0[...] = (own0[...].astype(F32) + recv0[...].astype(F32)).astype(BF16)
    up0 = [
        push(mid0.at[lax.rem(a + k, high)], last0.at[k - 1], along[k - 1]) for k in range(1, high)
    ]
    for copy in up1:
        copy.wait_recv()
    joined = own1[...].astype(F32)
    for k in range(1, high):
        joined = joined + recv1[k - 1].astype(F32)
    mid1[...] = joined.astype(BF16)
    over1 = push(mid1.at[1 - b], last1, across)
    for copy in up0:
        copy.wait_recv()
    result = own0[pl.ds(a, 1)][0].astype(F32) + recv0[pl.ds(a, 1)][0].astype(F32)
    for k in range(1, high):
        result = result + last0[k - 1].astype(F32)
    out[0] = result
    over1.wait_recv()
    result = own1[pl.ds(b, 1)][0].astype(F32)
    for k in range(1, high):
        result = result + recv1[k - 1, pl.ds(b, 1)][0].astype(F32)
    out[1] = result + last1[...].astype(F32)
    for copy in [over0, over1] + up0 + up1:
        copy.wait_send()
    riders.finish()


def sum_rows(partial_sums, grp, collective_id, name, riders=()):
    high = grp // 2
    tokens, width = partial_sums.shape
    rows = tokens // (2 * grp)
    parts = partial_sums.astype(BF16).reshape(2, high, 2, rows, width)
    (result,), arrived = carried_call(
        partial(sum_rows_kernel, high),
        [parts],
        [jax.ShapeDtypeStruct((2, rows, width), F32)],
        [ANY],
        [VMEM],
        [
            pltpu.VMEM((high, rows, width), BF16),
            pltpu.VMEM((high, rows, width), BF16),
            pltpu.VMEM((high - 1, rows, width), BF16),
            pltpu.VMEM((high - 1, 2, rows, width), BF16),
            pltpu.VMEM((2, rows, width), BF16),
            pltpu.VMEM((rows, width), BF16),
            pltpu.VMEM((high, rows, width), BF16),
            pltpu.VMEM((2, rows, width), BF16),
            DMA((2 * high,)),
            DMA((2 * high,)),
            DMA((2,)),
        ],
        comm_params(collective_id),
        name,
        riders,
    )
    return result, arrived


def pair_peer():
    s, g = lax.axis_index("seq"), lax.axis_index("grp")
    line = lax.axis_size("seq") // 2
    return s // line, (lax.rem(s + line, 2 * line), g)


def gather_pair_kernel(
    high, riders, src, beside, dst, beside_dst, send_sems, recv_sems, pair_sems, local_sems
):
    a, b, across, along = plane_peers(high)
    _, pair = pair_peer()
    greet([across, pair] + along + riders.peers())
    over_pair = send(src, dst.at[1, :, a, b], pair_sems.at[0], pair_sems.at[1], pair)
    riders.start()
    homes = [
        pltpu.make_async_copy(src, dst.at[0, :, a, b], local_sems.at[0]),
        pltpu.make_async_copy(beside, beside_dst.at[:, a, b], local_sems.at[1]),
    ]
    for copy in homes:
        copy.start()
    given = dst.at[1, :, a, b]
    planes = [
        PlaneGather(high, first, second, target, send_sems.at[i], recv_sems.at[i])
        for i, (first, second, target) in enumerate(
            (
                (src.at[0], src.at[1], dst.at[0]),
                (beside.at[0], beside.at[1], beside_dst),
                (given.at[0], given.at[1], dst.at[1]),
            )
        )
    ]
    planes[0].start()
    planes[1].start()
    planes[0].forward()
    over_pair.wait_recv()
    planes[2].start()
    planes[1].forward()
    planes[2].forward()
    for plane in planes:
        plane.finish()
    over_pair.wait_send()
    for copy in homes:
        copy.wait()
    riders.finish()


def gather_pair(array, beside, grp, collective_id, name, riders=()):
    high = grp // 2
    rows, width = array.shape[1:]
    both = jax.ShapeDtypeStruct((2,) + plane_shape(array, grp).shape, array.dtype)
    (result, beside), arrived = carried_call(
        partial(gather_pair_kernel, high),
        [array, beside],
        [both, plane_shape(beside, grp)],
        [ANY, ANY],
        [ANY, ANY],
        [DMA((3, 4 * high)), DMA((3, 4 * high)), DMA((2,)), DMA((2,))],
        comm_params(collective_id, 60),
        name,
        riders,
    )
    result, beside = result.reshape(4 * grp * rows, width), beside.reshape(2, grp * rows, width)
    return result, beside, arrived


class PairSum:
    def __init__(self, high, src, out, scratch):
        self.high, self.src, self.out = high, src, out
        self.recv0, self.mid0, self.last0, self.recv1, self.mid1, self.last1 = scratch[:6]
        self.own0, self.own1, self.given, self.taken = scratch[6:10]
        self.send_sems, self.recv_sems, self.pair_sems, self.local_sems = scratch[10:]
        self.place = plane_peers(high)
        self.pair = pair_peer()[1]
        self.slots = [iter(range(2 * high)), iter(range(2 * high))]
        self.sent, self.first, self.second = [[], []], [None, None], [None, None]

    @staticmethod
    def scratch(high, rows, width):
        return [
            pltpu.VMEM((2, high, rows, width), BF16),
            pltpu.VMEM((2, high, rows, width), BF16),
            pltpu.VMEM((2, high - 1, rows, width), BF16),
            pltpu.VMEM((2, high - 1, 2, rows, width), BF16),
            pltpu.VMEM((2, 2, rows, width), BF16),
            pltpu.VMEM((2, rows, width), BF16),
            pltpu.VMEM((2, high, rows, width), BF16),
            pltpu.VMEM((2, 2, rows, width), BF16),
            pltpu.VMEM((2, rows, width), BF16),
            pltpu.VMEM((2, rows, width), BF16),
            DMA((2, 2 * high)),
            DMA((2, 2 * high)),
            DMA((2,)),
            DMA((2, 2)),
        ]

    def push(self, i, what, where, peer):
        k = next(self.slots[i])
        copy = send(what, where, self.send_sems.at[i, k], self.recv_sems.at[i, k], peer)
        self.sent[i].append(copy)
        return copy

    def start(self, i):
        a, b, across, along = self.place
        part = self.src.at[1 - i]
        over0 = self.push(i, part.at[0, :, 1 - b], self.recv0.at[i], across)
        up1 = [
            self.push(i, part.at[1, lax.rem(a + k, self.high)], self.recv1.at[i, k - 1], along[k - 1])
            for k in range(1, self.high)
        ]
        loads = [
            pltpu.make_async_copy(part.at[0, :, b], self.own0.at[i], self.local_sems.at[i, 0]),
            pltpu.make_async_copy(part.at[1, a], self.own1.at[i], self.local_sems.at[i, 1]),
        ]
        for load in loads:
            load.start()
        self.first[i] = (over0, up1, loads)

    def middle(self, i):
        a, b, across, along = self.place
        over0, up1, loads = self.first[i]
        for load in loads:
            load.wait()
        over0.wait_recv()
        self.mid0[i] = (self.own0[i].astype(F32) + self.recv0[i].astype(F32)).astype(BF16)
        up0 = [
            self.push(
                i, self.mid0.at[i, lax.rem(a + k, self.high)], self.last0.at[i, k - 1], along[k - 1]
            )
            for k in range(1, self.high)
        ]
        for copy in up1:
            copy.wait_recv()
        joined = self.own1[i].astype(F32)
        for k in range(1, self.high):
            joined = joined + self.recv1[i, k - 1].astype(F32)
        self.mid1[i] = joined.astype(BF16)
        over1 = self.push(i, self.mid1.at[i, 1 - b], self.last1.at[i], across)
        self.second[i] = (up0, over1)

    def last(self, i):
        a, b, across, along = self.place
        up0, over1 = self.second[i]
        for copy in up0:
            copy.wait_recv()
        result0 = self.own0[i, pl.ds(a, 1)][0].astype(F32) + self.recv0[i, pl.ds(a, 1)][0].astype(F32)
        for k in range(1, self.high):
            result0 = result0 + self.last0[i, k - 1].astype(F32)
        over1.wait_recv()
        result1 = self.own1[i, pl.ds(b, 1)][0].astype(F32) + self.last1[i].astype(F32)
        for k in range(1, self.high):
            result1 = result1 + self.recv1[i, k - 1, pl.ds(b, 1)][0].astype(F32)
        if i == 0:
            self.given[0] = result0.astype(BF16)
            self.given[1] = result1.astype(BF16)
            self.over_pair = send(
                self.given, self.taken, self.pair_sems.at[0], self.pair_sems.at[1], self.pair
            )
        else:
            self.out[0] = result0
            self.out[1] = result1

    def finish(self):
        self.over_pair.wait_recv()
        self.out[...] += self.taken[...].astype(F32)
        self.over_pair.wait_send()
        for copy in self.sent[0] + self.sent[1]:
            copy.wait_send()


def sum_pair_kernel(high, count, riders, src, inner, *refs):
    blocks, (out, product, weights, sems, *scratch) = refs[:count], refs[count:]
    a, b, across, along = plane_peers(high)
    greet([across, pair_peer()[1]] + along + riders.peers())
    riders.start()
    whole = PairSum(high, src, out, scratch)
    whole.start(0)
    whole.middle(0)
    whole.start(1)
    mlp_out_kernel(blocks, inner, product, weights, sems)
    whole.last(0)
    whole.middle(1)
    whole.last(1)
    whole.finish()
    riders.finish()


def pair_parts(partial_sums, grp):
    tokens, width = partial_sums.shape
    return partial_sums.reshape(2, 2, grp // 2, 2, tokens // (4 * grp), width)


def sum_pair(partial_sums, blocks, inner, grp, collective_id, name, riders=()):
    parts = pair_parts(partial_sums, grp)
    high, _, rows, width = parts.shape[2:]
    (result, product), arrived = carried_call(
        partial(sum_pair_kernel, high, len(blocks)),
        [parts, inner, *blocks],
        [
            jax.ShapeDtypeStruct((2, rows, width), F32),
            jax.ShapeDtypeStruct(partial_sums.shape, BF16),
        ],
        [ANY, VMEM] + [ANY] * len(blocks),
        [VMEM, VMEM],
        [pltpu.VMEM((width, inner.shape[1]), BF16), DMA((len(blocks),))] + PairSum.scratch(high, rows, width),
        comm_params(collective_id, 48),
        name,
        riders,
    )
    return result, product, arrived


def turn_half(values):
    half = values.shape[-1] // 2
    return jnp.concatenate([-values[:, half:], values[:, :half]], axis=-1)


def fill_tables(frequency, cosine, sine):
    line = lax.axis_size("seq") // 2
    rows, dim = cosine.shape[0] // 2, cosine.shape[1]
    for part in range(2):
        first = (lax.rem(lax.axis_index("seq"), line) + part * line) * rows
        position = first + lax.broadcasted_iota(jnp.int32, (rows, dim), 0)
        angles = position.astype(F32) * frequency[...]
        cosine[part * rows : (part + 1) * rows] = jnp.cos(angles)
        sine[part * rows : (part + 1) * rows] = jnp.sin(angles)


def heads_kernel(queries, keys, x, w, frequency, query_gain, key_gain, raw, out, cosine, sine):
    step, dim = pl.program_id(0), cosine.shape[1]
    pl.when(step == 0)(lambda: fill_tables(frequency, cosine, sine))
    raw[...] = nn(x[...], w[...])
    for i in range(raw.shape[1] // dim):
        head, cut = step * (raw.shape[1] // dim) + i, slice(i * dim, (i + 1) * dim)

        @pl.when(head < queries + keys)
        def _():
            unit, _ = normalize(raw[:, cut])
            scaled = unit * jnp.where(head < queries, query_gain[...], key_gain[...])
            out[:, cut] = (scaled * cosine[...] + turn_half(scaled) * sine[...]).astype(BF16)

        @pl.when(head >= queries + keys)
        def _():
            out[:, cut] = raw[:, cut].astype(BF16)


def heads_forward(x, w, small, queries, keys):
    (tokens, depth), width, dim = x.shape, w.shape[1], small[0].shape[1]
    step = 2 * dim
    column = pl.BlockSpec((tokens, step), lambda h: (0, h))
    one = pl.BlockSpec((1, dim), lambda h: (0, 0))
    return pl.pallas_call(
        partial(heads_kernel, queries, keys),
        cost_estimate=NO_COST,
        name="heads_forward",
        grid=(width // step,),
        out_shape=[
            jax.ShapeDtypeStruct((tokens, width), F32),
            jax.ShapeDtypeStruct((tokens, width), BF16),
        ],
        in_specs=[
            pl.BlockSpec((tokens, depth), lambda h: (0, 0)),
            pl.BlockSpec((depth, step), lambda h: (0, h)),
            one,
            one,
            one,
        ],
        out_specs=[column, column],
        scratch_shapes=[pltpu.VMEM((tokens, dim), F32), pltpu.VMEM((tokens, dim), F32)],
        compiler_params=pltpu.CompilerParams(vmem_limit_bytes=60 * 2**20),
    )(x, w, *small)


def heads_back_kernel(
    queries, keys, raw, grad_q, grad_kv, frequency, query_gain, key_gain, out, gain_out, cosine, sine
):
    head = pl.program_id(0)
    pl.when(head == 0)(lambda: fill_tables(frequency, cosine, sine))

    def turned_back(given):
        unit, inverse = normalize(raw[...])
        turned = given * cosine[...] - turn_half(given * sine[...])
        gain_out[...] = jnp.broadcast_to(
            jnp.sum(turned * unit, axis=0, keepdims=True)[None], gain_out.shape
        )
        scaled = turned * jnp.where(head < queries, query_gain[...], key_gain[...])
        out[...] = norm_back(scaled, unit, inverse).astype(BF16)

    pl.when(head < queries)(lambda: turned_back(grad_q[...]))
    pl.when((head >= queries) & (head < queries + keys))(lambda: turned_back(grad_kv[...]))

    @pl.when(head >= queries + keys)
    def _():
        gain_out[...] = jnp.zeros_like(gain_out)
        out[...] = grad_kv[...].astype(BF16)


def heads_backward(raw, grad_q, grad_kv, small, queries, keys):
    (tokens, width), dim = raw.shape, small[0].shape[1]
    column = pl.BlockSpec((tokens, dim), lambda h: (0, h))
    one = pl.BlockSpec((1, dim), lambda h: (0, 0))
    return pl.pallas_call(
        partial(heads_back_kernel, queries, keys),
        cost_estimate=NO_COST,
        name="heads_backward",
        grid=(width // dim,),
        out_shape=[
            jax.ShapeDtypeStruct((tokens, width), BF16),
            jax.ShapeDtypeStruct((width // dim, 8, dim), F32),
        ],
        in_specs=[
            column,
            pl.BlockSpec((tokens, dim), lambda h: (0, jnp.minimum(h, queries - 1))),
            pl.BlockSpec((tokens, dim), lambda h: (0, jnp.maximum(h - queries, 0))),
            one,
            one,
            one,
        ],
        out_specs=[column, pl.BlockSpec((1, 8, dim), lambda h: (h, 0, 0))],
        scratch_shapes=[pltpu.VMEM((tokens, dim), F32), pltpu.VMEM((tokens, dim), F32)],
        compiler_params=pltpu.CompilerParams(vmem_limit_bytes=32 * 2**20),
    )(raw, grad_q, grad_kv, *small)


def half_line_peers(chips):
    s, g = lax.axis_index("seq"), lax.axis_index("grp")
    chip, core = s // 2, lax.rem(s, 2)
    place = lax.rem(chip, chips)
    others = [((chip - place + lax.rem(place + k, chips)) * 2 + core, g) for k in range(1, chips)]
    return place, core, (s + 1 - 2 * core, g), others


def remote(src, dst, send_sem, recv_sem, peer):
    return pltpu.make_async_remote_copy(
        src_ref=src,
        dst_ref=dst,
        send_sem=send_sem,
        recv_sem=recv_sem,
        device_id=peer,
        device_id_type=MESH,
    )


def allowed_pairs(query_block, key_block, length, rows, repeat, diagonal):
    key_pos = key_block * rows + lax.broadcasted_iota(jnp.int32, (rows, repeat * rows), 0)
    allowed = key_pos < length
    if diagonal:
        query_pos = lax.broadcasted_iota(jnp.int32, (rows, repeat * rows), 1)
        allowed = allowed & (key_pos <= query_block * rows + lax.rem(query_pos, rows))
    return allowed


def stacked(ref, part, rows, first, repeat, dim):
    return jnp.concatenate(
        [
            ref[part * rows : (part + 1) * rows, (first + r) * dim : (first + r + 1) * dim]
            for r in range(repeat)
        ],
        axis=0,
    )


def attend_kernel(
    shape,
    chips,
    high,
    riders,
    length,
    q,
    kv_home,
    beside,
    mixed,
    mixed_low,
    log_total,
    kv_all,
    beside_dst,
    plane_send,
    plane_recv,
    kv_buf,
    acc,
    sums,
    lane_send,
    lane_recv,
    cross_send,
    cross_recv,
    local_sems,
):
    rows, keys, repeat, dim = shape
    scale = 1.0 / math.sqrt(dim)
    place, core, cross, others = half_line_peers(chips)
    me = place * 2 + core
    a, b, across, along = plane_peers(high)
    greet([cross] + others + [across] + along + riders.peers())
    home = pltpu.make_async_copy(kv_home, kv_all.at[me], local_sems.at[0])
    home.start()
    beside_home = pltpu.make_async_copy(beside, beside_dst.at[:, a, b], local_sems.at[2])
    beside_home.start()
    plane = PlaneGather(high, beside.at[0], beside.at[1], beside_dst, plane_send, plane_recv)

    def over(i, src, owner):
        return remote(src, kv_all.at[owner], cross_send.at[i], cross_recv.at[i], cross)

    lanes = [
        remote(kv_home, kv_all.at[me], lane_send.at[k], lane_recv.at[k], peer)
        for k, peer in enumerate(others)
    ]
    crossed = [over(0, kv_home, me)]
    for copy in lanes + crossed:
        copy.start()
    plane.start()
    riders.start()
    acc[...] = jnp.zeros_like(acc)
    sums[...] = jnp.zeros_like(sums)

    def piece(owner, query_part, key_part, diagonal):
        query_block, key_block = me + query_part * 2 * chips, owner + key_part * 2 * chips
        allowed = allowed_pairs(query_block, key_block, length[0], rows, repeat, diagonal)
        here = slice(key_part * rows, (key_part + 1) * rows)
        for k in range(keys):
            unit = query_part * keys + k
            kk = kv_buf[here, k * dim : (k + 1) * dim]
            vv = kv_buf[here, (keys + k) * dim : (keys + k + 1) * dim]
            scores = nt(kk, stacked(q, query_part, rows, k * repeat, repeat, dim)) * scale
            weights = jnp.where(allowed, jnp.exp(scores), 0.0)
            sums[unit] += jnp.sum(weights, axis=0, keepdims=True)
            acc[unit] += tn(vv, weights.astype(BF16))

    def work(src, owner, own):
        load = pltpu.make_async_copy(src, kv_buf, local_sems.at[1])
        load.start()
        load.wait()
        piece(owner, 1, 0, False)
        if own:
            piece(owner, 0, 0, True)
            piece(owner, 1, 1, True)
        else:

            @pl.when(owner < me)
            def _():
                piece(owner, 0, 0, False)
                piece(owner, 1, 1, False)

    work(kv_home, me, True)
    for k in range(chips):
        near = lax.rem(place + chips - k, chips) * 2
        if k:
            owner = near + core
            lanes[k - 1].wait_recv()
            crossed.append(over(k, kv_all.at[owner], owner))
            crossed[k].start()
            work(kv_all.at[owner], owner, False)
        owner = near + 1 - core
        crossed[k].wait_recv()
        work(kv_all.at[owner], owner, False)
        if k == 0:
            plane.forward()
    for part in range(2):
        for k in range(keys):
            unit = part * keys + k
            log_total[unit] = jnp.log(sums[unit])
            result = (acc[unit] / sums[unit]).T
            for r in range(repeat):
                cut = result[r * rows : (r + 1) * rows]
                h = k * repeat + r
                mixed[part * rows : (part + 1) * rows, h * dim : (h + 1) * dim] = cut
                mixed_low[part * rows : (part + 1) * rows, h * dim : (h + 1) * dim] = cut.astype(BF16)
    home.wait()
    for copy in lanes + crossed:
        copy.wait_send()
    plane.finish()
    beside_home.wait()
    riders.finish()


def attend(length, q, kv_home, beside, seq, grp, keys, repeat, dim, collective_id, riders=()):
    tokens, kv_width = kv_home.shape
    rows, width = tokens // 2, keys * repeat * dim
    chips = seq // 4
    return carried_call(
        partial(attend_kernel, (rows, keys, repeat, dim), chips, grp // 2),
        [length, q, kv_home, beside],
        [
            jax.ShapeDtypeStruct((tokens, width), F32),
            jax.ShapeDtypeStruct((tokens, width), BF16),
            jax.ShapeDtypeStruct((2 * keys, 1, repeat * rows), F32),
            jax.ShapeDtypeStruct((2 * chips, tokens, kv_width), BF16),
            plane_shape(beside, grp),
        ],
        [pl.BlockSpec(memory_space=pltpu.SMEM), VMEM, ANY, ANY],
        [VMEM, VMEM, VMEM, ANY, ANY],
        [
            DMA((2 * grp,)),
            DMA((2 * grp,)),
            pltpu.VMEM((tokens, kv_width), BF16),
            pltpu.VMEM((2 * keys, dim, repeat * rows), F32),
            pltpu.VMEM((2 * keys, 1, repeat * rows), F32),
            DMA((chips,)),
            DMA((chips,)),
            DMA((chips,)),
            DMA((chips,)),
            DMA((3,)),
        ],
        comm_params(collective_id, 60),
        "attend",
        riders,
    )


def attend_back_kernel(
    shape,
    chips,
    high,
    riders,
    length,
    q,
    mixed,
    grad_mixed,
    log_total,
    kv_all,
    beside,
    grad_q,
    grad_kv,
    beside_out,
    kv_buf,
    acc,
    delta,
    mine,
    lane_out,
    lane_in,
    cross_out,
    cross_in,
    lane_send,
    lane_recv,
    cross_send,
    cross_recv,
    local_sem,
    *beside_scratch,
):
    rows, keys, repeat, dim = shape
    scale = 1.0 / math.sqrt(dim)
    place, core, cross, others = half_line_peers(chips)
    me = place * 2 + core
    _, _, across, along = plane_peers(high)
    greet([cross] + others + [across, pair_peer()[1]] + along + riders.peers())
    whole = PairSum(high, beside, beside_out, beside_scratch)
    whole.start(0)
    riders.start()
    acc[...] = jnp.zeros_like(acc)
    for part in range(2):
        for k in range(keys):
            product = stacked(mixed, part, rows, k * repeat, repeat, dim) * stacked(
                grad_mixed, part, rows, k * repeat, repeat, dim
            ).astype(F32)
            delta[part * keys + k] = jnp.sum(product.T, axis=0, keepdims=True)

    def piece(owner, query_part, key_part, diagonal, first):
        query_block, key_block = me + query_part * 2 * chips, owner + key_part * 2 * chips
        allowed = allowed_pairs(query_block, key_block, length[0], rows, repeat, diagonal)
        here = slice(key_part * rows, (key_part + 1) * rows)
        for k in range(keys):
            unit = query_part * keys + k
            key_cut, value_cut = slice(k * dim, (k + 1) * dim), slice((keys + k) * dim, (keys + k + 1) * dim)
            kk, vv = kv_buf[here, key_cut], kv_buf[here, value_cut]
            qq = stacked(q, query_part, rows, k * repeat, repeat, dim)
            gg = stacked(grad_mixed, query_part, rows, k * repeat, repeat, dim)
            weights = jnp.where(allowed, jnp.exp(nt(kk, qq) * scale - log_total[unit]), 0.0)
            grad_scores = (weights * (nt(vv, gg) - delta[unit])).astype(BF16)
            grad_k, grad_v = nn(grad_scores, qq) * scale, nn(weights.astype(BF16), gg)
            if first:
                mine[here, key_cut] = grad_k
                mine[here, value_cut] = grad_v
            else:
                mine[here, key_cut] += grad_k
                mine[here, value_cut] += grad_v
            acc[unit] += tn(grad_scores, kk)

    def work(owner, own):
        load = pltpu.make_async_copy(kv_all.at[owner], kv_buf, local_sem)
        load.start()
        load.wait()
        piece(owner, 1, 0, False, True)
        if own:
            piece(owner, 0, 0, True, False)
            piece(owner, 1, 1, True, True)
        else:

            @pl.when(owner < me)
            def _():
                piece(owner, 0, 0, False, False)
                piece(owner, 1, 1, False, True)

            @pl.when(owner > me)
            def _():
                mine[rows:, :] = jnp.zeros_like(mine[rows:, :])

    lanes, crossed = [], []
    for k in list(range(1, chips)) + [0]:
        near = lax.rem(place + k, chips) * 2
        work(near + 1 - core, False)
        if k == 1:
            whole.middle(0)
            whole.start(1)
        if k == 0:
            whole.middle(1)
        cross_out[k] = mine[...].astype(BF16)
        copy = remote(cross_out.at[k], cross_in.at[k], cross_send.at[k], cross_recv.at[k], cross)
        copy.start()
        crossed.append(copy)
        work(near + core, k == 0)
        if k == 1:
            whole.last(0)
        if k == 0:
            whole.last(1)
        copy.wait_recv()
        mine[...] += cross_in[k].astype(F32)
        if k:
            lane_out[k - 1] = mine[...].astype(BF16)
            copy = remote(
                lane_out.at[k - 1], lane_in.at[k - 1], lane_send.at[k - 1], lane_recv.at[k - 1], others[k - 1]
            )
            copy.start()
            lanes.append(copy)
    for k, copy in enumerate(lanes):
        copy.wait_recv()
        mine[...] += lane_in[k].astype(F32)
    grad_kv[...] = mine[...]
    for part in range(2):
        for k in range(keys):
            for r in range(repeat):
                h = k * repeat + r
                grad_q[part * rows : (part + 1) * rows, h * dim : (h + 1) * dim] = (
                    acc[part * keys + k, r * rows : (r + 1) * rows] * scale
                )
    for copy in lanes + crossed:
        copy.wait_send()
    whole.finish()
    riders.finish()


def attend_back(
    length, q, kv_all, mixed, grad_mixed, log_total, beside, grp, keys, repeat, dim, collective_id, riders=()
):
    owners, tokens, kv_width = kv_all.shape
    rows, width = tokens // 2, keys * repeat * dim
    chips = owners // 2
    parts = pair_parts(beside, grp)
    high, _, beside_rows, beside_width = parts.shape[2:]
    slots = pltpu.VMEM((chips, tokens, kv_width), BF16)
    return carried_call(
        partial(attend_back_kernel, (rows, keys, repeat, dim), chips, high),
        [length, q, mixed, grad_mixed, log_total, kv_all, parts],
        [
            jax.ShapeDtypeStruct((tokens, width), F32),
            jax.ShapeDtypeStruct((tokens, kv_width), F32),
            jax.ShapeDtypeStruct((2, beside_rows, beside_width), F32),
        ],
        [pl.BlockSpec(memory_space=pltpu.SMEM), VMEM, VMEM, VMEM, VMEM, ANY, ANY],
        [VMEM, VMEM, VMEM],
        [
            pltpu.VMEM((tokens, kv_width), BF16),
            pltpu.VMEM((2 * keys, repeat * rows, dim), F32),
            pltpu.VMEM((2 * keys, 1, repeat * rows), F32),
            pltpu.VMEM((tokens, kv_width), F32),
            slots,
            slots,
            slots,
            slots,
            DMA((chips,)),
            DMA((chips,)),
            DMA((chips,)),
            DMA((chips,)),
            DMA,
        ]
        + PairSum.scratch(high, beside_rows, beside_width),
        comm_params(collective_id, 48),
        "attend_back",
        riders,
    )


def attention_grads_kernel(rows, grad_raw, branch, mixed_low, out):
    width = grad_raw.shape[1]
    out[:, :width] = tn(rows[...], grad_raw[...]).astype(BF16)
    out[:, width:] = tn(branch[...], mixed_low[...]).astype(BF16)


def attention_grads(rows, grad_raw, branch, mixed_low):
    (tokens, depth), width, inner = rows.shape, grad_raw.shape[1], mixed_low.shape[1]
    step = 512
    column = pl.BlockSpec((tokens, step), lambda d: (0, d))
    return pl.pallas_call(
        attention_grads_kernel,
        cost_estimate=NO_COST,
        name="attention_grads",
        grid=(depth // step,),
        out_shape=jax.ShapeDtypeStruct((depth, width + inner), BF16),
        in_specs=[
            column,
            pl.BlockSpec((tokens, width), lambda d: (0, 0)),
            column,
            pl.BlockSpec((tokens, inner), lambda d: (0, 0)),
        ],
        out_specs=pl.BlockSpec((step, width + inner), lambda d: (d, 0)),
        compiler_params=pltpu.CompilerParams(vmem_limit_bytes=32 * 2**20),
    )(rows, grad_raw, branch, mixed_low)


def write_attention_kernel(sums, *outs):
    first = 0
    for out in outs[:-1]:
        last = first + out.shape[1]
        out[...] = sums[:, first:last].astype(F32)
        first = last
    outs[-1][...] = sums[:, first:].astype(F32).T


def write_attention(sums, widths):
    depth, columns = sums.shape
    shapes = [(depth, width) for width in widths] + [(columns - sum(widths), depth)]
    return pl.pallas_call(
        write_attention_kernel,
        cost_estimate=NO_COST,
        name="write_attention",
        in_specs=[VMEM],
        out_specs=[VMEM] * len(shapes),
        out_shape=[jax.ShapeDtypeStruct(shape, F32) for shape in shapes],
        compiler_params=pltpu.CompilerParams(vmem_limit_bytes=32 * 2**20),
    )(sums)


def load_weights(blocks, first, weights, sems):
    s = lax.axis_index("seq")
    line = lax.axis_size("seq") // 2
    chips = line // 2
    row, place, core = s // line, lax.rem(s, line) // 2, lax.rem(s, 2)
    depth, width = blocks[0].shape[0], weights.shape[1]
    copies = []
    for i, src in enumerate(blocks):
        which = row if i // chips % 2 == 0 else 1 - row
        back = lax.rem(place + chips - i % chips, chips)
        owner = which * line + back * 2 + (core if i < 2 * chips else 1 - core)
        copy = pltpu.make_async_copy(
            src.at[:, pl.ds(first, width)], weights.at[pl.ds(owner * depth, depth)], sems.at[i]
        )
        copy.start()
        copies.append(copy)
    for copy in copies:
        copy.wait()
    return depth


def weight_grads(x, grads, keep, give):
    chips, halves, depth, _ = keep.shape
    core = lax.rem(lax.axis_index("seq"), 2)

    def one(t, carry):
        cut = pl.ds(pl.multiple_of(t * 2 * depth, 2 * depth), 2 * depth)
        both = tn(x[:, cut], grads[...]).astype(BF16)
        chip, which = lax.rem(t, chips), t // chips

        @pl.when(core == 0)
        def _():
            keep[chip, which] = both[:depth]
            give[chip, which] = both[depth:]

        @pl.when(core == 1)
        def _():
            keep[chip, which] = both[depth:]
            give[chip, which] = both[:depth]

        return carry

    lax.fori_loop(0, halves * chips, one, 0)


def mlp_kernel(rows, cot_home, cot_away, *refs):
    *blocks, inner, grad_pre, keep, give, weights, cot, sems, cot_sems = refs
    block = cot_home.shape[1]
    row = lax.axis_index("seq") // (lax.axis_size("seq") // 2)

    def load(i, src):
        return pltpu.make_async_copy(src, cot.at[pl.ds(i * block, block)], cot_sems.at[i])

    for k, order in enumerate(
        (
            (cot_home.at[0], cot_away.at[0], cot_home.at[1], cot_away.at[1]),
            (cot_away.at[1], cot_home.at[1], cot_away.at[0], cot_home.at[0]),
        )
    ):

        @pl.when(row == k)
        def _():
            for i, src in enumerate(order):
                load(i, src).start()

    depth = load_weights(blocks, 0, weights, sems)
    for i in range(4):
        load(i, cot_home.at[0]).wait()
    units = inner.shape[1]
    step = 256 if units % 256 == 0 else 128
    tile = 512
    tiles = rows.shape[0] // tile

    def one(t, carry):
        here = pl.ds(pl.multiple_of(lax.rem(t, tiles) * tile, tile), tile)
        first = pl.multiple_of((t // tiles) * step, step)
        cols = pl.ds(first, step)
        x = rows[here, :]
        gate = nn(x, weights[:, cols])
        up = nn(x, weights[:, pl.ds(units + first, step)])
        grad = nn(cot[here, :], weights[:, pl.ds(2 * units + first, step)])
        sigmoid = jax.nn.sigmoid(gate)
        silu = gate * sigmoid
        inner[here, cols] = (silu * up).astype(BF16)
        grad_pre[here, cols] = (grad * up * sigmoid * (1.0 + gate * (1.0 - sigmoid))).astype(BF16)
        grad_pre[here, pl.ds(units + first, step)] = (grad * silu).astype(BF16)
        return carry

    lax.fori_loop(0, tiles * (units // step), one, 0)

    weight_grads(cot, inner, keep, give)


def grads_shape(width, columns):
    chips = lax.axis_size("seq") // 4
    return jax.ShapeDtypeStruct((chips, 2, width // chips // 4, columns), BF16)


def mlp(blocks, rows, cot_home, cot_away):
    (tokens, width), columns = rows.shape, blocks[0].shape[1]
    units = columns // 3
    return pl.pallas_call(
        mlp_kernel,
        cost_estimate=NO_COST,
        name="mlp",
        in_specs=[VMEM, ANY, ANY] + [ANY] * len(blocks),
        out_specs=[VMEM] * 4,
        out_shape=[
            jax.ShapeDtypeStruct((tokens, units), BF16),
            jax.ShapeDtypeStruct((tokens, 2 * units), BF16),
            grads_shape(width, units),
            grads_shape(width, units),
        ],
        scratch_shapes=[
            pltpu.VMEM((width, columns), BF16),
            pltpu.VMEM((tokens, width), BF16),
            DMA((len(blocks),)),
            DMA((4,)),
        ],
        compiler_params=pltpu.CompilerParams(vmem_limit_bytes=52 * 2**20),
    )(rows, cot_home, cot_away, *blocks)


def mlp_back_kernel(riders, rows, grad_pre, keep_down, give_down, *refs):
    *blocks, down, gate, up, grad_rows, keep, give, got, got_down, weights, sems, core_sems = refs
    core = peer_of("core")
    greet([core])
    over_down = send(give_down, got_down, core_sems.at[0, 0], core_sems.at[0, 1], core)
    load_weights(blocks, 0, weights, sems)
    weight_grads(rows, grad_pre, keep, give)
    over = send(give, got, core_sems.at[1, 0], core_sems.at[1, 1], core)
    tile = 512

    def one(t, carry):
        here = pl.ds(pl.multiple_of(t * tile, tile), tile)
        grad_rows[here, :] = nt(grad_pre[here, :], weights[...]).astype(BF16)
        return carry

    lax.fori_loop(0, rows.shape[0] // tile, one, 0)
    units = gate.shape[-1]
    over_down.wait()
    over.wait()

    def add(t, carry):
        at = (lax.rem(t, keep.shape[0]), t // keep.shape[0])
        down[at] = (keep_down[at].astype(F32) + got_down[at].astype(F32)).astype(BF16)
        both = (keep[at].astype(F32) + got[at].astype(F32)).astype(BF16)
        gate[at] = both[:, :units]
        up[at] = both[:, units:]
        return carry

    lax.fori_loop(0, 2 * keep.shape[0], add, 0)


def mlp_back(blocks, rows, grad_pre, keep_down, give_down, collective_id):
    (tokens, width), columns = rows.shape, grad_pre.shape[1]
    one, two = grads_shape(width, columns // 2), grads_shape(width, columns)
    results, _ = carried_call(
        mlp_back_kernel,
        [rows, grad_pre, keep_down, give_down, *blocks],
        [one, one, one, jax.ShapeDtypeStruct((tokens, width), BF16)],
        [VMEM, VMEM, VMEM, ANY] + [ANY] * len(blocks),
        [VMEM] * 4,
        [pltpu.VMEM(two.shape, BF16)] * 3
        + [
            pltpu.VMEM(one.shape, BF16),
            pltpu.VMEM((width, columns), BF16),
            DMA((len(blocks),)),
            DMA((2, 2)),
        ],
        comm_params(collective_id, 60),
        "mlp_back",
    )
    return results


def mlp_out_kernel(blocks, inner, out, weights, sems):
    load_weights(blocks, 2 * inner.shape[1], weights, sems)
    tile = 512

    def one(t, carry):
        here = pl.ds(pl.multiple_of(t * tile, tile), tile)
        out[here, :] = nt(inner[here, :], weights[...]).astype(BF16)
        return carry

    lax.fori_loop(0, inner.shape[0] // tile, one, 0)


def write_kernel(sums, taken, out):
    units = taken.shape[1]
    row = lax.axis_index("seq") // (lax.axis_size("seq") // 2)
    kept, other = sums[row].astype(F32), taken[...].astype(F32)
    out[:, :units] = jnp.where(row == 0, kept, other)
    out[:, units:] = jnp.where(row == 0, other, kept)


def write_down_kernel(sums, taken, out):
    units = taken.shape[1]
    row = lax.axis_index("seq") // (lax.axis_size("seq") // 2)
    kept, other = sums[row].astype(F32), taken[...].astype(F32)
    out[:units] = jnp.where(row == 0, kept, other).T
    out[units:] = jnp.where(row == 0, other, kept).T


def write(kernel, sums, taken, shape, name):
    return pl.pallas_call(
        kernel,
        cost_estimate=NO_COST,
        name=name,
        in_specs=[VMEM, VMEM],
        out_specs=VMEM,
        out_shape=jax.ShapeDtypeStruct(shape, F32),
        compiler_params=pltpu.CompilerParams(vmem_limit_bytes=32 * 2**20),
    )(sums, taken)


def shards(
    tokens,
    lengths,
    attn_gain,
    w_query,
    w_key,
    w_value,
    query_gain,
    key_gain,
    w_out,
    mlp_gain,
    w_gate,
    w_up,
    w_down,
    cotangent,
):
    seq, grp = lax.axis_size("seq"), lax.axis_size("grp")
    seq_index, grp_index = lax.axis_index("seq"), lax.axis_index("grp")
    local_rows, width = tokens.shape[1:]
    rows = local_rows * grp
    dim = query_gain.shape[0]
    queries, keys = w_query.shape[1] // dim, w_key.shape[1] // dim
    repeat = queries // keys
    hidden_units = w_gate.shape[1]
    chunk = attn_gain.shape[0]
    depth = width // seq

    line = seq // 2
    row = seq_index // line

    def to_give(values):
        return lax.dynamic_index_in_dim(values, 1 - row, 0, keepdims=False)

    def both_rows(values, taken):
        kept = lax.dynamic_index_in_dim(values, row, 0, keepdims=False)
        return jnp.stack([jnp.where(row == 0, kept, taken), jnp.where(row == 0, taken, kept)])

    length = lax.dynamic_slice(lengths, (row,), (1,))

    half_units = hidden_units // 2
    opposite = [(s, (s + line) % seq) for s in range(seq)]

    def half(which):
        cut = [
            lax.dynamic_slice_in_dim(w, which * half_units, half_units, 1)
            for w in (w_gate, w_up, w_down.T)
        ]
        return jnp.concatenate(cut, axis=1)

    chips = line // 2
    steps = range(1, chips)
    place = lax.rem(seq_index, line) // 2

    def chips_sum(parts, arrived):
        mine = lax.dynamic_index_in_dim(parts, place, 0, keepdims=False)
        return sum([x.astype(F32) for x in arrived], mine.astype(F32)).astype(BF16)

    def to_chips(parts):
        return [(k, parts, "chip") for k in steps]

    projections = jnp.concatenate([w_query, w_key, w_value], axis=1)
    full_qkv = lax.all_gather(projections, "seq", axis=0, tiled=True)
    lane = max(128, chunk)
    packed = jnp.pad(jnp.stack([attn_gain, mlp_gain]), ((0, 6), (0, lane - chunk)))
    spread_gains, (taken_tokens,) = spread(packed, seq, grp, 1, [("opposite", to_give(tokens))])
    spread_gains = spread_gains[:, :, :, :chunk].transpose(2, 1, 0, 3)
    gain_attn = spread_gains[0].reshape(-1)
    gain_mlp = spread_gains[1].reshape(-1)
    full_out = lax.all_gather(after(w_out.T, taken_tokens), "seq", axis=0, tiled=True)
    residual = both_rows(tokens, taken_tokens).astype(F32)
    attn_unit, attn_inverse = normalize(residual)
    attn_rows, _ = gather_rows((attn_unit * gain_attn).astype(BF16), grp, 2, "gather_inputs")
    kept_half, given_half = after((half(row), half(1 - row)), attn_rows)
    taken_half = lax.ppermute(given_half, "seq", opposite)
    token_pos = (seq_index * grp + grp_index) * local_rows + jnp.arange(local_rows, dtype=jnp.int32)
    valid_rows = (token_pos[None, :] < lengths[:, None]).astype(BF16)
    cot_home = cotangent * valid_rows[:, :, None]

    frequency = ROPE_BASE ** (-jnp.arange(dim // 2, dtype=F32) * 2.0 / dim)
    small = [jnp.tile(frequency, 2)[None], query_gain[None], key_gain[None]]
    raw, heads = heads_forward(attn_rows, full_qkv, small, queries, keys)
    q, kv_home = heads[:, : queries * dim], heads[:, queries * dim :]

    (mixed, mixed_low, log_total, kv_all, cot_gathered), _ = attend(
        length, q, kv_home, cot_home, seq, grp, keys, repeat, dim, 3
    )
    cot_gathered = cot_gathered.reshape(2, rows, width)
    summed, (taken_cotangent, *passed) = sum_rows(
        nt(mixed_low, full_out),
        grp,
        4,
        "sum_attention",
        [("opposite", cot_home)] + [(k, kept_half) for k in steps],
    )
    own_half = [kept_half] + passed
    early = jnp.where(row == 0, cot_home[0], taken_cotangent[1])
    late = jnp.where(row == 0, taken_cotangent[0], cot_home[1])
    cot_rows = jnp.stack([early, late]).astype(F32)
    hidden = residual + summed

    mlp_unit, mlp_inverse = normalize(hidden)
    first_blocks = own_half + [taken_half]
    mlp_rows, cot_away, arrived = gather_pair(
        (mlp_unit * gain_mlp).astype(BF16),
        taken_cotangent,
        grp,
        5,
        "gather_mlp",
        [(k, taken_half) for k in steps] + [("core", x) for x in first_blocks],
    )
    passed, core_blocks = arrived[: len(steps)], arrived[len(steps) :]
    core_swap = [(s, s ^ 1) for s in range(seq)]
    core_blocks += [lax.ppermute(x, "seq", core_swap) for x in passed]
    blocks_w = first_blocks + passed + core_blocks
    inner_low, grad_pre, keep_down, give_down = mlp(blocks_w, mlp_rows, cot_gathered, cot_away)
    down, gate, up, grad_mlp_part = mlp_back(blocks_w, mlp_rows, grad_pre, keep_down, give_down, 13)
    grad_mlp_in, out_part, arrived = sum_pair(
        grad_mlp_part,
        blocks_w,
        inner_low,
        grp,
        7,
        "sum_mlp_back",
        to_chips(down) + to_chips(gate),
    )
    down = chips_sum(down, arrived[: len(steps)])
    gate = chips_sum(gate, arrived[len(steps) :])
    grad_gain_mlp = jnp.sum(grad_mlp_in * mlp_unit, axis=(0, 1))
    grad_hidden = cot_rows + norm_back(grad_mlp_in * gain_mlp, mlp_unit, mlp_inverse)
    grad_branch, (taken_down, taken_gate, *arrived) = gather_rows(
        grad_hidden.astype(BF16),
        grp,
        8,
        "gather_branch",
        [("opposite", down, "row"), ("opposite", gate, "row")] + to_chips(up),
    )
    up = chips_sum(up, arrived)

    grad_mixed = nn(grad_branch, full_out).astype(BF16)
    (grad_q, grad_kv, summed), (taken_up,) = attend_back(
        length,
        q,
        kv_all,
        mixed,
        grad_mixed,
        log_total,
        out_part,
        grp,
        keys,
        repeat,
        dim,
        9,
        [("opposite", up, "row")],
    )
    output = (hidden + summed).astype(BF16)
    grad_raw, head_gain_parts = heads_backward(raw, grad_q, grad_kv, small, queries, keys)
    grad_w_attn = attention_grads(attn_rows, grad_raw, grad_branch, mixed_low)
    sum_attn = lax.psum_scatter(grad_w_attn, "seq", scatter_dimension=0, tiled=True)
    grad_attn_part = nt(after(grad_raw, grad_w_attn), full_qkv)
    grad_attn_in, (taken_output,) = sum_rows(
        grad_attn_part,
        grp,
        10,
        "sum_attention_back",
        [("opposite", to_give(output))],
    )
    output = both_rows(output, taken_output)
    wide_shape = (depth, hidden_units)
    taken_down, taken_gate, taken_up = after((taken_down, taken_gate, taken_up), grad_attn_in)
    out_down = write(write_down_kernel, down, taken_down, wide_shape[::-1], "write_down")
    out_gate = write(write_kernel, gate, taken_gate, wide_shape, "write_gate")
    out_up = write(write_kernel, up, taken_up, wide_shape, "write_up")
    grad_gain_attn = jnp.sum(grad_attn_in * attn_unit, axis=(0, 1))
    grad_tokens = grad_hidden + norm_back(grad_attn_in * gain_attn, attn_unit, attn_inverse)

    head_gain_grads = jnp.stack(
        [
            jnp.sum(head_gain_parts[:queries, 0], axis=0),
            jnp.sum(head_gain_parts[queries : queries + keys, 0], axis=0),
        ]
    )
    vector = jnp.concatenate([grad_gain_attn, grad_gain_mlp, head_gain_grads.reshape(-1)])
    padded = -(-vector.shape[0] // 1024) * 1024
    vector = jnp.pad(vector, (0, padded - vector.shape[0])).reshape(-1, 128)
    sums, (taken_grads,) = total(vector, seq, grp, 12, [("opposite", to_give(grad_tokens).astype(BF16))])
    sums = sums.reshape(-1)
    grad_tokens = both_rows(grad_tokens, taken_grads.astype(F32))
    place = (seq_index * grp + grp_index) * chunk
    out_attn_gain = lax.dynamic_slice(sums, (place,), (chunk,))
    out_mlp_gain = lax.dynamic_slice(sums, (width + place,), (chunk,))
    out_query_gain = sums[2 * width : 2 * width + dim]
    out_key_gain = sums[2 * width + dim : 2 * width + 2 * dim]

    out_query, out_key, out_value, out_out = write_attention(
        sum_attn, (queries * dim, keys * dim, keys * dim)
    )
    return (
        output,
        grad_tokens,
        out_attn_gain,
        out_query,
        out_key,
        out_value,
        out_query_gain,
        out_key_gain,
        out_out,
        out_mlp_gain,
        out_gate,
        out_up,
        out_down,
    )


def solution(mesh):
    rows = P(None, ("seq", "grp"), None)
    vector = P(("seq", "grp"))
    wide, tall = P("seq", "grp"), P("grp", "seq")
    return jax.shard_map(
        shards,
        mesh=mesh,
        in_specs=(
            rows,
            P(),
            vector,
            wide,
            wide,
            wide,
            P(),
            P(),
            tall,
            vector,
            wide,
            wide,
            tall,
            rows,
        ),
        out_specs=(
            rows,
            rows,
            vector,
            wide,
            wide,
            wide,
            P(),
            P(),
            tall,
            vector,
            wide,
            wide,
            tall,
        ),
        check_vma=False,
    )
```

```python
from functools import partial
import math

import jax
import jax.numpy as jnp
from jax import lax
from jax.experimental import pallas as pl
from jax.experimental.pallas import tpu as pltpu
from jax.sharding import PartitionSpec as P

EPSILON = 1e-06
ROPE_BASE = 1000000.0
MESH = pl.DeviceIdType.MESH
ANY = pl.BlockSpec(memory_space=pltpu.HBM)
VMEM = pl.BlockSpec(memory_space=pltpu.VMEM)
DMA = pltpu.SemaphoreType.DMA
F32 = jnp.float32
BF16 = jnp.bfloat16


def normalize(values):
    inverse = lax.rsqrt(jnp.mean(values * values, axis=-1, keepdims=True) + EPSILON)
    return (values * inverse, inverse)


def norm_back(gradient, unit_values, inverse):
    return inverse * (
        gradient - unit_values * jnp.mean(gradient * unit_values, axis=-1, keepdims=True)
    )


def after(value, earlier):
    return lax.optimization_barrier((value, earlier))[0]


def nt(a, b):
    return lax.dot_general(a, b, (((1,), (1,)), ((), ())), preferred_element_type=F32)


def tn(a, b):
    return lax.dot_general(a, b, (((0,), (0,)), ((), ())), preferred_element_type=F32)


def nn(a, b):
    return jnp.dot(a, b, preferred_element_type=F32)


NO_COST = pl.CostEstimate(flops=1, bytes_accessed=1, transcendentals=0)


def comm_params(collective_id, mib=32):
    return pltpu.CompilerParams(
        collective_id=collective_id, has_side_effects=True, vmem_limit_bytes=mib * 2**20
    )


def greet(peers):
    barrier = pltpu.get_barrier_semaphore()
    for peer in peers:
        pl.semaphore_signal(barrier, inc=1, device_id=peer, device_id_type=MESH)
    pl.semaphore_wait(barrier, len(peers))


def send(src, dst, send_sem, recv_sem, peer):
    copy = pltpu.make_async_remote_copy(
        src_ref=src,
        dst_ref=dst,
        send_sem=send_sem,
        recv_sem=recv_sem,
        device_id=peer,
        device_id_type=MESH,
    )
    copy.start()
    return copy


def peer_of(kind):
    s, g = lax.axis_index("seq"), lax.axis_index("grp")
    line = lax.axis_size("seq") // 2
    if kind == "opposite":
        return lax.rem(s + line, 2 * line), g
    if kind == "core":
        return s + 1 - 2 * lax.rem(s, 2), g
    place = lax.rem(s, line)
    return s - place + lax.rem(place + 2 * kind, line), g


def part_of(kind, part):
    s = lax.axis_index("seq")
    line = lax.axis_size("seq") // 2
    if part == "row":
        return 1 - s // line
    return lax.rem(lax.rem(s, line) + 2 * kind, line) // 2


class Riders:
    def __init__(self, kinds, parts, sources, targets, send_sems, recv_sems):
        self.kinds, self.parts, self.sources, self.targets = kinds, parts, sources, targets
        self.send_sems, self.recv_sems = send_sems, recv_sems
        self.copies = []

    def peers(self):
        return [peer_of(kind) for kind in dict.fromkeys(self.kinds)]

    def start(self):
        for i, (kind, part) in enumerate(zip(self.kinds, self.parts)):
            src = self.sources[i] if part is None else self.sources[i].at[part_of(kind, part)]
            self.copies.append(
                send(src, self.targets[i], self.send_sems.at[i], self.recv_sems.at[i], peer_of(kind))
            )

    def finish(self):
        for copy in self.copies:
            copy.wait()


def carried_call(kernel, operands, out_shape, in_specs, out_specs, scratch, params, name, riders=()):
    riders = [rider if len(rider) == 3 else rider + (None,) for rider in riders]
    kinds, parts = [rider[0] for rider in riders], [rider[2] for rider in riders]
    arrays = [rider[1] for rider in riders]
    carried = [x.shape if part is None else x.shape[1:] for x, part in zip(arrays, parts)]
    count, ins, outs = len(arrays), len(in_specs), len(out_specs)

    def body(*refs):
        sources, refs = refs[:count], refs[count:]
        own_in, refs = refs[:ins], refs[ins:]
        targets, refs = refs[:count], refs[count:]
        own_out, refs = refs[:outs], refs[outs:]
        sems, refs = (refs[:2], refs[2:]) if count else ((None, None), refs)
        kernel(Riders(kinds, parts, sources, targets, *sems), *own_in, *own_out, *refs)

    results = pl.pallas_call(
        body,
        name=name,
        cost_estimate=NO_COST,
        out_shape=[jax.ShapeDtypeStruct(shape, x.dtype) for shape, x in zip(carried, arrays)]
        + list(out_shape),
        in_specs=[ANY] * count + list(in_specs),
        out_specs=[ANY] * count + list(out_specs),
        scratch_shapes=([DMA((count,)), DMA((count,))] if count else []) + list(scratch),
        compiler_params=params,
    )(*arrays, *operands)
    return list(results[count:]), list(results[:count])


def spread_kernel(seq, grp, riders, x_ref, out_ref, send1, recv1, send2, recv2):
    s, g = lax.axis_index("seq"), lax.axis_index("grp")
    line = [(lax.rem(s + k, seq), g) for k in range(1, seq)]
    plane = [(s, lax.rem(g + k, grp)) for k in range(1, grp)]
    greet(line + plane + riders.peers())
    out_ref[pl.ds(g, 1), pl.ds(s, 1)] = x_ref[...][None, None]
    first = [
        send(x_ref, out_ref.at[g, s], send1.at[k], recv1.at[k], peer) for k, peer in enumerate(line)
    ]
    riders.start()
    for copy in first:
        copy.wait()
    second = [
        send(out_ref.at[g], out_ref.at[g], send2.at[k], recv2.at[k], peer)
        for k, peer in enumerate(plane)
    ]
    for copy in second:
        copy.wait()
    riders.finish()


def spread(block, seq, grp, collective_id, riders=()):
    (result,), arrived = carried_call(
        partial(spread_kernel, seq, grp),
        [block],
        [jax.ShapeDtypeStruct((grp, seq) + block.shape, block.dtype)],
        [VMEM],
        [VMEM],
        [DMA((seq - 1,)), DMA((seq - 1,)), DMA((grp - 1,)), DMA((grp - 1,))],
        comm_params(collective_id),
        "gather_gains",
        riders,
    )
    return result, arrived


def total_kernel(
    seq, grp, riders, x_ref, out_ref, line_buf, part, plane_buf, send1, recv1, send2, recv2
):
    s, g = lax.axis_index("seq"), lax.axis_index("grp")
    line = [(lax.rem(s + k, seq), g) for k in range(1, seq)]
    plane = [(s, lax.rem(g + k, grp)) for k in range(1, grp)]
    greet(line + plane + riders.peers())
    riders.start()
    line_buf[pl.ds(s, 1)] = x_ref[...][None]
    first = [
        send(x_ref, line_buf.at[s], send1.at[k], recv1.at[k], peer) for k, peer in enumerate(line)
    ]
    for copy in first:
        copy.wait()
    part[...] = jnp.sum(line_buf[...], axis=0)
    plane_buf[pl.ds(g, 1)] = part[...][None]
    second = [
        send(part, plane_buf.at[g], send2.at[k], recv2.at[k], peer) for k, peer in enumerate(plane)
    ]
    for copy in second:
        copy.wait()
    out_ref[...] = jnp.sum(plane_buf[...], axis=0)
    riders.finish()


def total(block, seq, grp, collective_id, riders=()):
    (result,), arrived = carried_call(
        partial(total_kernel, seq, grp),
        [block],
        [jax.ShapeDtypeStruct(block.shape, block.dtype)],
        [VMEM],
        [VMEM],
        [
            pltpu.VMEM((seq,) + block.shape, block.dtype),
            pltpu.VMEM(block.shape, block.dtype),
            pltpu.VMEM((grp,) + block.shape, block.dtype),
            DMA((seq - 1,)),
            DMA((seq - 1,)),
            DMA((grp - 1,)),
            DMA((grp - 1,)),
        ],
        comm_params(collective_id),
        "sum_gains",
        riders,
    )
    return result, arrived


def plane_peers(high):
    s, g = lax.axis_index("seq"), lax.axis_index("grp")
    a, b = g // 2, lax.rem(g, 2)
    across = (s, a * 2 + 1 - b)
    along = [(s, lax.rem(a + k, high) * 2 + b) for k in range(1, high)]
    return a, b, across, along


class PlaneGather:
    def __init__(self, high, first, second, target, send_sems, recv_sems):
        self.high, self.first, self.second, self.target = high, first, second, target
        self.send_sems, self.recv_sems = send_sems, recv_sems
        self.slots = iter(range(4 * high))
        self.place = plane_peers(high)

    def push(self, what, where, peer):
        k = next(self.slots)
        return send(what, where, self.send_sems.at[k], self.recv_sems.at[k], peer)

    def start(self):
        a, b, across, along = self.place
        here0, here1 = self.target.at[0, a, b], self.target.at[1, a, b]
        self.early = [self.push(self.first, here0, across)]
        self.early += [self.push(self.second, here1, peer) for peer in along]
        self.late = [self.push(self.second, here1, across)]
        self.late += [self.push(self.first, here0, peer) for peer in along]

    def forward(self):
        a, b, across, along = self.place
        self.early[0].wait_recv()
        passed = self.target.at[0, a, 1 - b]
        self.late += [self.push(passed, passed, peer) for peer in along]
        for k in range(1, self.high):
            self.early[k].wait_recv()
            passed = self.target.at[1, lax.rem(a + self.high - k, self.high), b]
            self.late.append(self.push(passed, passed, across))

    def finish(self):
        for copy in self.late:
            copy.wait_recv()
        for copy in self.early + self.late:
            copy.wait_send()


def gather_rows_kernel(high, riders, src, dst, send_sems, recv_sems, local_sem):
    a, b, across, along = plane_peers(high)
    greet([across] + along + riders.peers())
    riders.start()
    home = pltpu.make_async_copy(src, dst.at[:, a, b], local_sem)
    home.start()
    plane = PlaneGather(high, src.at[0], src.at[1], dst, send_sems, recv_sems)
    plane.start()
    plane.forward()
    plane.finish()
    home.wait()
    riders.finish()


def plane_shape(array, grp):
    rows, width = array.shape[1:]
    return jax.ShapeDtypeStruct((2, grp // 2, 2, rows, width), array.dtype)


def gather_rows(array, grp, collective_id, name, riders=()):
    high = grp // 2
    (result,), arrived = carried_call(
        partial(gather_rows_kernel, high),
        [array],
        [plane_shape(array, grp)],
        [ANY],
        [ANY],
        [DMA((4 * high,)), DMA((4 * high,)), DMA],
        comm_params(collective_id),
        name,
        riders,
    )
    return result.reshape(2 * grp * array.shape[1], array.shape[2]), arrived


def sum_rows_kernel(high, riders, src, out, recv0, mid0, last0, recv1, mid1, last1, own0, own1, send_sems, recv_sems, local_sems):
    a, b, across, along = plane_peers(high)
    greet([across] + along + riders.peers())
    riders.start()
    slots = iter(range(2 * high))

    def push(what, where, peer):
        k = next(slots)
        return send(what, where, send_sems.at[k], recv_sems.at[k], peer)

    over0 = push(src.at[0, :, 1 - b], recv0, across)
    up1 = [
        push(src.at[1, lax.rem(a + k, high)], recv1.at[k - 1], along[k - 1]) for k in range(1, high)
    ]
    load0 = pltpu.make_async_copy(src.at[0, :, b], own0, local_sems.at[0])
    load1 = pltpu.make_async_copy(src.at[1, a], own1, local_sems.at[1])
    load0.start()
    load1.start()
    load0.wait()
    load1.wait()
    over0.wait_recv()
    mid0[...] = (own0[...].astype(F32) + recv0[...].astype(F32)).astype(BF16)
    up0 = [
        push(mid0.at[lax.rem(a + k, high)], last0.at[k - 1], along[k - 1]) for k in range(1, high)
    ]
    for copy in up1:
        copy.wait_recv()
    joined = own1[...].astype(F32)
    for k in range(1, high):
        joined = joined + recv1[k - 1].astype(F32)
    mid1[...] = joined.astype(BF16)
    over1 = push(mid1.at[1 - b], last1, across)
    for copy in up0:
        copy.wait_recv()
    result = own0[pl.ds(a, 1)][0].astype(F32) + recv0[pl.ds(a, 1)][0].astype(F32)
    for k in range(1, high):
        result = result + last0[k - 1].astype(F32)
    out[0] = result
    over1.wait_recv()
    result = own1[pl.ds(b, 1)][0].astype(F32)
    for k in range(1, high):
        result = result + recv1[k - 1, pl.ds(b, 1)][0].astype(F32)
    out[1] = result + last1[...].astype(F32)
    for copy in [over0, over1] + up0 + up1:
        copy.wait_send()
    riders.finish()


def sum_rows(partial_sums, grp, collective_id, name, riders=()):
    high = grp // 2
    tokens, width = partial_sums.shape
    rows = tokens // (2 * grp)
    parts = partial_sums.astype(BF16).reshape(2, high, 2, rows, width)
    (result,), arrived = carried_call(
        partial(sum_rows_kernel, high),
        [parts],
        [jax.ShapeDtypeStruct((2, rows, width), F32)],
        [ANY],
        [VMEM],
        [
            pltpu.VMEM((high, rows, width), BF16),
            pltpu.VMEM((high, rows, width), BF16),
            pltpu.VMEM((high - 1, rows, width), BF16),
            pltpu.VMEM((high - 1, 2, rows, width), BF16),
            pltpu.VMEM((2, rows, width), BF16),
            pltpu.VMEM((rows, width), BF16),
            pltpu.VMEM((high, rows, width), BF16),
            pltpu.VMEM((2, rows, width), BF16),
            DMA((2 * high,)),
            DMA((2 * high,)),
            DMA((2,)),
        ],
        comm_params(collective_id),
        name,
        riders,
    )
    return result, arrived


def pair_peer():
    s, g = lax.axis_index("seq"), lax.axis_index("grp")
    line = lax.axis_size("seq") // 2
    return s // line, (lax.rem(s + line, 2 * line), g)


def gather_pair_kernel(
    high, riders, src, beside, dst, beside_dst, send_sems, recv_sems, pair_sems, local_sems
):
    a, b, across, along = plane_peers(high)
    _, pair = pair_peer()
    greet([across, pair] + along + riders.peers())
    over_pair = send(src, dst.at[1, :, a, b], pair_sems.at[0], pair_sems.at[1], pair)
    homes = [
        pltpu.make_async_copy(src, dst.at[0, :, a, b], local_sems.at[0]),
        pltpu.make_async_copy(beside, beside_dst.at[:, a, b], local_sems.at[1]),
    ]
    for copy in homes:
        copy.start()
    given = dst.at[1, :, a, b]
    planes = [
        PlaneGather(high, first, second, target, send_sems.at[i], recv_sems.at[i])
        for i, (first, second, target) in enumerate(
            (
                (src.at[0], src.at[1], dst.at[0]),
                (beside.at[0], beside.at[1], beside_dst),
                (given.at[0], given.at[1], dst.at[1]),
            )
        )
    ]
    planes[0].start()
    planes[1].start()
    planes[0].forward()
    over_pair.wait_recv()
    riders.start()
    planes[2].start()
    planes[1].forward()
    planes[2].forward()
    for plane in planes:
        plane.finish()
    over_pair.wait_send()
    for copy in homes:
        copy.wait()
    riders.finish()


def gather_pair(array, beside, grp, collective_id, name, riders=()):
    high = grp // 2
    rows, width = array.shape[1:]
    both = jax.ShapeDtypeStruct((2,) + plane_shape(array, grp).shape, array.dtype)
    (result, beside), arrived = carried_call(
        partial(gather_pair_kernel, high),
        [array, beside],
        [both, plane_shape(beside, grp)],
        [ANY, ANY],
        [ANY, ANY],
        [DMA((3, 4 * high)), DMA((3, 4 * high)), DMA((2,)), DMA((2,))],
        comm_params(collective_id, 60),
        name,
        riders,
    )
    result, beside = result.reshape(4 * grp * rows, width), beside.reshape(2, grp * rows, width)
    return result, beside, arrived


class PairSum:
    def __init__(self, high, src, out, scratch, base=None):
        self.high, self.src, self.out, self.base = high, src, out, base
        self.recv0, self.mid0, self.last0, self.recv1, self.mid1, self.last1 = scratch[:6]
        self.own0, self.own1, self.given, self.taken = scratch[6:10]
        self.send_sems, self.recv_sems, self.pair_sems, self.local_sems = scratch[10:]
        self.place = plane_peers(high)
        self.pair = pair_peer()[1]
        self.slots = [iter(range(2 * high)), iter(range(2 * high))]
        self.sent, self.first, self.second = [[], []], [None, None], [None, None]

    @staticmethod
    def scratch(high, rows, width):
        return [
            pltpu.VMEM((2, high, rows, width), BF16),
            pltpu.VMEM((2, high, rows, width), BF16),
            pltpu.VMEM((2, high - 1, rows, width), BF16),
            pltpu.VMEM((2, high - 1, 2, rows, width), BF16),
            pltpu.VMEM((2, 2, rows, width), BF16),
            pltpu.VMEM((2, rows, width), BF16),
            pltpu.VMEM((2, high, rows, width), BF16),
            pltpu.VMEM((2, 2, rows, width), BF16),
            pltpu.VMEM((2, rows, width), BF16),
            pltpu.VMEM((2, rows, width), BF16),
            DMA((2, 2 * high)),
            DMA((2, 2 * high)),
            DMA((2,)),
            DMA((2, 2)),
        ]

    def push(self, i, what, where, peer):
        k = next(self.slots[i])
        copy = send(what, where, self.send_sems.at[i, k], self.recv_sems.at[i, k], peer)
        self.sent[i].append(copy)
        return copy

    def block(self, i):
        row = pair_peer()[0]
        return row if i else 1 - row

    def start(self, i):
        a, b, across, along = self.place
        if self.base is None:
            first, second = self.src.at[1 - i, 0], self.src.at[1 - i, 1]
        else:
            first, second = self.src.at[0, self.block(i)], self.src.at[1, self.block(i)]
        over0 = self.push(i, first.at[:, 1 - b], self.recv0.at[i], across)
        up1 = [
            self.push(i, second.at[lax.rem(a + k, self.high)], self.recv1.at[i, k - 1], along[k - 1])
            for k in range(1, self.high)
        ]
        loads = [
            pltpu.make_async_copy(first.at[:, b], self.own0.at[i], self.local_sems.at[i, 0]),
            pltpu.make_async_copy(second.at[a], self.own1.at[i], self.local_sems.at[i, 1]),
        ]
        for load in loads:
            load.start()
        self.first[i] = (over0, up1, loads)

    def middle(self, i):
        a, b, across, along = self.place
        over0, up1, loads = self.first[i]
        for load in loads:
            load.wait()
        over0.wait_recv()
        self.mid0[i] = (self.own0[i].astype(F32) + self.recv0[i].astype(F32)).astype(BF16)
        up0 = [
            self.push(
                i, self.mid0.at[i, lax.rem(a + k, self.high)], self.last0.at[i, k - 1], along[k - 1]
            )
            for k in range(1, self.high)
        ]
        for copy in up1:
            copy.wait_recv()
        joined = self.own1[i].astype(F32)
        for k in range(1, self.high):
            joined = joined + self.recv1[i, k - 1].astype(F32)
        self.mid1[i] = joined.astype(BF16)
        over1 = self.push(i, self.mid1.at[i, 1 - b], self.last1.at[i], across)
        self.second[i] = (up0, over1)

    def last(self, i):
        a, b, across, along = self.place
        up0, over1 = self.second[i]
        for copy in up0:
            copy.wait_recv()
        result0 = self.own0[i, pl.ds(a, 1)][0].astype(F32) + self.recv0[i, pl.ds(a, 1)][0].astype(F32)
        for k in range(1, self.high):
            result0 = result0 + self.last0[i, k - 1].astype(F32)
        if self.base is not None:
            result0 = result0 + self.base[pl.ds(self.block(i), 1)][0]
        over1.wait_recv()
        result1 = self.own1[i, pl.ds(b, 1)][0].astype(F32) + self.last1[i].astype(F32)
        for k in range(1, self.high):
            result1 = result1 + self.recv1[i, k - 1, pl.ds(b, 1)][0].astype(F32)
        if i == 0:
            self.given[0] = result0.astype(BF16)
            self.given[1] = result1.astype(BF16)
            self.over_pair = send(
                self.given, self.taken, self.pair_sems.at[0], self.pair_sems.at[1], self.pair
            )
        else:
            self.out[0] = result0
            self.out[1] = result1

    def finish(self):
        self.over_pair.wait_recv()
        for k in range(2):
            self.out[k] += self.taken[k if self.base is None else 1 - k].astype(F32)
        self.over_pair.wait_send()
        for copy in self.sent[0] + self.sent[1]:
            copy.wait_send()


def sum_pair_kernel(high, riders, src, inner, weights, out, product, *scratch):
    a, b, across, along = plane_peers(high)
    greet([across, pair_peer()[1]] + along + riders.peers())
    riders.start()
    whole = PairSum(high, src, out, scratch)
    whole.start(0)
    whole.middle(0)
    whole.start(1)
    tile = 512

    def one(t, carry):
        here = pl.ds(pl.multiple_of(t * tile, tile), tile)
        product[here, :] = nt(inner[here, :], weights[...]).astype(BF16)
        return carry

    lax.fori_loop(0, inner.shape[0] // tile, one, 0)
    whole.last(0)
    whole.middle(1)
    whole.last(1)
    whole.finish()
    riders.finish()


def pair_parts(partial_sums, grp):
    tokens, width = partial_sums.shape
    return partial_sums.reshape(2, 2, grp // 2, 2, tokens // (4 * grp), width)


def sum_pair(partial_sums, inner, weights, grp, collective_id, name, riders=()):
    parts = pair_parts(partial_sums, grp)
    high, _, rows, width = parts.shape[2:]
    (result, product), arrived = carried_call(
        partial(sum_pair_kernel, high),
        [parts, inner, weights],
        [
            jax.ShapeDtypeStruct((2, rows, width), F32),
            jax.ShapeDtypeStruct(partial_sums.shape, BF16),
        ],
        [ANY, VMEM, VMEM],
        [VMEM, VMEM],
        PairSum.scratch(high, rows, width),
        comm_params(collective_id, 48),
        name,
        riders,
    )
    return result, product, arrived


def turn_half(values):
    half = values.shape[-1] // 2
    return jnp.concatenate([-values[:, half:], values[:, :half]], axis=-1)


def fill_tables(frequency, cosine, sine):
    line = lax.axis_size("seq") // 2
    rows, dim = cosine.shape[0] // 2, cosine.shape[1]
    for part in range(2):
        first = (lax.rem(lax.axis_index("seq"), line) + part * line) * rows
        position = first + lax.broadcasted_iota(jnp.int32, (rows, dim), 0)
        angles = position.astype(F32) * frequency[...]
        cosine[part * rows : (part + 1) * rows] = jnp.cos(angles)
        sine[part * rows : (part + 1) * rows] = jnp.sin(angles)


def heads_kernel(queries, keys, x, w, frequency, query_gain, key_gain, raw, q, kv, cosine, sine):
    step, dim = pl.program_id(0), cosine.shape[1]
    pl.when(step == 0)(lambda: fill_tables(frequency, cosine, sine))
    raw[...] = nn(x[...], w[...])
    for i in range(raw.shape[1] // dim):
        head, cut = step * (raw.shape[1] // dim) + i, slice(i * dim, (i + 1) * dim)

        def turned(gain):
            unit, _ = normalize(raw[:, cut])
            scaled = unit * gain[...]
            return (scaled * cosine[...] + turn_half(scaled) * sine[...]).astype(BF16)

        @pl.when(head < queries)
        def _():
            q[:, cut] = turned(query_gain)

        @pl.when((head >= queries) & (head < queries + keys))
        def _():
            kv[:, cut] = turned(key_gain)

        @pl.when(head >= queries + keys)
        def _():
            kv[:, cut] = raw[:, cut].astype(BF16)


def heads_forward(x, w, small, queries, keys):
    (tokens, depth), width, dim = x.shape, w.shape[1], small[0].shape[1]
    step = 2 * dim
    column = pl.BlockSpec((tokens, step), lambda h: (0, h))
    one = pl.BlockSpec((1, dim), lambda h: (0, 0))
    return pl.pallas_call(
        partial(heads_kernel, queries, keys),
        cost_estimate=NO_COST,
        name="heads_forward",
        grid=(width // step,),
        out_shape=[
            jax.ShapeDtypeStruct((tokens, width), F32),
            jax.ShapeDtypeStruct((tokens, queries * dim), BF16),
            jax.ShapeDtypeStruct((tokens, 2 * keys * dim), BF16),
        ],
        in_specs=[
            pl.BlockSpec((tokens, depth), lambda h: (0, 0)),
            pl.BlockSpec((depth, step), lambda h: (0, h)),
            one,
            one,
            one,
        ],
        out_specs=[
            column,
            pl.BlockSpec((tokens, step), lambda h: (0, jnp.minimum(h, queries // 2 - 1))),
            pl.BlockSpec((tokens, step), lambda h: (0, jnp.maximum(h - queries // 2, 0))),
        ],
        scratch_shapes=[pltpu.VMEM((tokens, dim), F32), pltpu.VMEM((tokens, dim), F32)],
        compiler_params=pltpu.CompilerParams(vmem_limit_bytes=60 * 2**20),
    )(x, w, *small)


def heads_back_kernel(
    queries, keys, raw, grad_q, grad_kv, frequency, query_gain, key_gain, out, gain_out, cosine, sine
):
    head = pl.program_id(0)
    pl.when(head == 0)(lambda: fill_tables(frequency, cosine, sine))

    def turned_back(given):
        unit, inverse = normalize(raw[...])
        turned = given * cosine[...] - turn_half(given * sine[...])
        gain_out[...] = jnp.broadcast_to(
            jnp.sum(turned * unit, axis=0, keepdims=True)[None], gain_out.shape
        )
        scaled = turned * jnp.where(head < queries, query_gain[...], key_gain[...])
        out[...] = norm_back(scaled, unit, inverse).astype(BF16)

    pl.when(head < queries)(lambda: turned_back(grad_q[...]))
    pl.when((head >= queries) & (head < queries + keys))(lambda: turned_back(grad_kv[...]))

    @pl.when(head >= queries + keys)
    def _():
        gain_out[...] = jnp.zeros_like(gain_out)
        out[...] = grad_kv[...].astype(BF16)


def heads_backward(raw, grad_q, grad_kv, small, queries, keys):
    (tokens, width), dim = raw.shape, small[0].shape[1]
    column = pl.BlockSpec((tokens, dim), lambda h: (0, h))
    one = pl.BlockSpec((1, dim), lambda h: (0, 0))
    return pl.pallas_call(
        partial(heads_back_kernel, queries, keys),
        cost_estimate=NO_COST,
        name="heads_backward",
        grid=(width // dim,),
        out_shape=[
            jax.ShapeDtypeStruct((tokens, width), BF16),
            jax.ShapeDtypeStruct((width // dim, 8, dim), F32),
        ],
        in_specs=[
            column,
            pl.BlockSpec((tokens, dim), lambda h: (0, jnp.minimum(h, queries - 1))),
            pl.BlockSpec((tokens, dim), lambda h: (0, jnp.maximum(h - queries, 0))),
            one,
            one,
            one,
        ],
        out_specs=[column, pl.BlockSpec((1, 8, dim), lambda h: (h, 0, 0))],
        scratch_shapes=[pltpu.VMEM((tokens, dim), F32), pltpu.VMEM((tokens, dim), F32)],
        compiler_params=pltpu.CompilerParams(vmem_limit_bytes=32 * 2**20),
    )(raw, grad_q, grad_kv, *small)


def half_line_peers(chips):
    s, g = lax.axis_index("seq"), lax.axis_index("grp")
    chip, core = s // 2, lax.rem(s, 2)
    place = lax.rem(chip, chips)
    others = [((chip - place + lax.rem(place + k, chips)) * 2 + core, g) for k in range(1, chips)]
    return place, core, (s + 1 - 2 * core, g), others


def remote(src, dst, send_sem, recv_sem, peer):
    return pltpu.make_async_remote_copy(
        src_ref=src,
        dst_ref=dst,
        send_sem=send_sem,
        recv_sem=recv_sem,
        device_id=peer,
        device_id_type=MESH,
    )


def allowed_pairs(query_block, key_block, length, rows, repeat, diagonal):
    key_pos = key_block * rows + lax.broadcasted_iota(jnp.int32, (rows, repeat * rows), 0)
    allowed = key_pos < length
    if diagonal:
        query_pos = lax.broadcasted_iota(jnp.int32, (rows, repeat * rows), 1)
        allowed = allowed & (key_pos <= query_block * rows + lax.rem(query_pos, rows))
    return allowed


def stacked(ref, part, rows, first, repeat, dim):
    return jnp.concatenate(
        [
            ref[part * rows : (part + 1) * rows, (first + r) * dim : (first + r + 1) * dim]
            for r in range(repeat)
        ],
        axis=0,
    )


def attend_kernel(
    shape,
    chips,
    high,
    riders,
    length,
    q,
    kv_home,
    beside,
    mixed,
    mixed_low,
    log_total,
    kv_all,
    beside_dst,
    plane_send,
    plane_recv,
    kv_buf,
    acc,
    sums,
    lane_send,
    lane_recv,
    cross_send,
    cross_recv,
    local_sems,
):
    rows, keys, repeat, dim = shape
    scale = 1.0 / math.sqrt(dim)
    place, core, cross, others = half_line_peers(chips)
    me = place * 2 + core
    a, b, across, along = plane_peers(high)
    greet([cross] + others + [across] + along + riders.peers())
    home = pltpu.make_async_copy(kv_home, kv_all.at[me], local_sems.at[0])
    home.start()
    beside_home = pltpu.make_async_copy(beside, beside_dst.at[:, a, b], local_sems.at[2])
    beside_home.start()
    plane = PlaneGather(high, beside.at[0], beside.at[1], beside_dst, plane_send, plane_recv)

    def over(i, src, owner):
        return remote(src, kv_all.at[owner], cross_send.at[i], cross_recv.at[i], cross)

    lanes = [
        remote(kv_home, kv_all.at[me], lane_send.at[k], lane_recv.at[k], peer)
        for k, peer in enumerate(others)
    ]
    crossed = [over(0, kv_home, me)]
    for copy in lanes + crossed:
        copy.start()
    plane.start()
    riders.start()
    acc[...] = jnp.zeros_like(acc)
    sums[...] = jnp.zeros_like(sums)

    def piece(owner, query_part, key_part, diagonal):
        query_block, key_block = me + query_part * 2 * chips, owner + key_part * 2 * chips
        allowed = allowed_pairs(query_block, key_block, length[0], rows, repeat, diagonal)
        here = slice(key_part * rows, (key_part + 1) * rows)
        for k in range(keys):
            unit = query_part * keys + k
            kk = kv_buf[here, k * dim : (k + 1) * dim]
            vv = kv_buf[here, (keys + k) * dim : (keys + k + 1) * dim]
            scores = nt(kk, stacked(q, query_part, rows, k * repeat, repeat, dim)) * scale
            weights = jnp.where(allowed, jnp.exp(scores), 0.0)
            sums[unit] += jnp.sum(weights, axis=0, keepdims=True)
            acc[unit] += tn(vv, weights.astype(BF16))

    def work(src, owner, own):
        load = pltpu.make_async_copy(src, kv_buf, local_sems.at[1])
        load.start()
        load.wait()
        piece(owner, 1, 0, False)
        if own:
            piece(owner, 0, 0, True)
            piece(owner, 1, 1, True)
        else:

            @pl.when(owner < me)
            def _():
                piece(owner, 0, 0, False)
                piece(owner, 1, 1, False)

    work(kv_home, me, True)
    for k in range(chips):
        near = lax.rem(place + chips - k, chips) * 2
        if k:
            owner = near + core
            lanes[k - 1].wait_recv()
            crossed.append(over(k, kv_all.at[owner], owner))
            crossed[k].start()
            work(kv_all.at[owner], owner, False)
        owner = near + 1 - core
        crossed[k].wait_recv()
        work(kv_all.at[owner], owner, False)
        if k == 0:
            plane.forward()
    for part in range(2):
        for k in range(keys):
            unit = part * keys + k
            log_total[unit] = jnp.log(sums[unit])
            result = (acc[unit] / sums[unit]).T
            for r in range(repeat):
                cut = result[r * rows : (r + 1) * rows]
                h = k * repeat + r
                mixed[part * rows : (part + 1) * rows, h * dim : (h + 1) * dim] = cut
                mixed_low[part * rows : (part + 1) * rows, h * dim : (h + 1) * dim] = cut.astype(BF16)
    home.wait()
    for copy in lanes + crossed:
        copy.wait_send()
    plane.finish()
    beside_home.wait()
    riders.finish()


def attend(length, q, kv_home, beside, seq, grp, keys, repeat, dim, collective_id, riders=()):
    tokens, kv_width = kv_home.shape
    rows, width = tokens // 2, keys * repeat * dim
    chips = seq // 4
    return carried_call(
        partial(attend_kernel, (rows, keys, repeat, dim), chips, grp // 2),
        [length, q, kv_home, beside],
        [
            jax.ShapeDtypeStruct((tokens, width), F32),
            jax.ShapeDtypeStruct((tokens, width), BF16),
            jax.ShapeDtypeStruct((2 * keys, 1, repeat * rows), F32),
            jax.ShapeDtypeStruct((2 * chips, tokens, kv_width), BF16),
            plane_shape(beside, grp),
        ],
        [pl.BlockSpec(memory_space=pltpu.SMEM), VMEM, ANY, ANY],
        [VMEM, VMEM, VMEM, ANY, ANY],
        [
            DMA((2 * grp,)),
            DMA((2 * grp,)),
            pltpu.VMEM((tokens, kv_width), BF16),
            pltpu.VMEM((2 * keys, dim, repeat * rows), F32),
            pltpu.VMEM((2 * keys, 1, repeat * rows), F32),
            DMA((chips,)),
            DMA((chips,)),
            DMA((chips,)),
            DMA((chips,)),
            DMA((3,)),
        ],
        comm_params(collective_id, 60),
        "attend",
        riders,
    )


def attend_back_kernel(
    shape,
    chips,
    high,
    riders,
    length,
    q,
    mixed,
    grad_mixed,
    log_total,
    kv_all,
    beside,
    base,
    grad_q,
    grad_kv,
    beside_out,
    kv_buf,
    acc,
    delta,
    mine,
    lane_out,
    lane_in,
    cross_out,
    cross_in,
    lane_send,
    lane_recv,
    cross_send,
    cross_recv,
    local_sem,
    *beside_scratch,
):
    rows, keys, repeat, dim = shape
    scale = 1.0 / math.sqrt(dim)
    place, core, cross, others = half_line_peers(chips)
    me = place * 2 + core
    _, _, across, along = plane_peers(high)
    greet([cross] + others + [across, pair_peer()[1]] + along + riders.peers())
    whole = PairSum(high, beside, beside_out, beside_scratch, base)
    whole.start(0)
    riders.start()
    acc[...] = jnp.zeros_like(acc)
    for part in range(2):
        for k in range(keys):
            product = stacked(mixed, part, rows, k * repeat, repeat, dim) * stacked(
                grad_mixed, part, rows, k * repeat, repeat, dim
            ).astype(F32)
            delta[part * keys + k] = jnp.sum(product.T, axis=0, keepdims=True)

    def piece(owner, query_part, key_part, diagonal, first):
        query_block, key_block = me + query_part * 2 * chips, owner + key_part * 2 * chips
        allowed = allowed_pairs(query_block, key_block, length[0], rows, repeat, diagonal)
        here = slice(key_part * rows, (key_part + 1) * rows)
        for k in range(keys):
            unit = query_part * keys + k
            key_cut, value_cut = slice(k * dim, (k + 1) * dim), slice((keys + k) * dim, (keys + k + 1) * dim)
            kk, vv = kv_buf[here, key_cut], kv_buf[here, value_cut]
            qq = stacked(q, query_part, rows, k * repeat, repeat, dim)
            gg = stacked(grad_mixed, query_part, rows, k * repeat, repeat, dim)
            weights = jnp.where(allowed, jnp.exp(nt(kk, qq) * scale - log_total[unit]), 0.0)
            grad_scores = (weights * (nt(vv, gg) - delta[unit])).astype(BF16)
            grad_k, grad_v = nn(grad_scores, qq) * scale, nn(weights.astype(BF16), gg)
            if first:
                mine[here, key_cut] = grad_k
                mine[here, value_cut] = grad_v
            else:
                mine[here, key_cut] += grad_k
                mine[here, value_cut] += grad_v
            acc[unit] += tn(grad_scores, kk)

    def work(owner, own):
        load = pltpu.make_async_copy(kv_all.at[owner], kv_buf, local_sem)
        load.start()
        load.wait()
        piece(owner, 1, 0, False, True)
        if own:
            piece(owner, 0, 0, True, False)
            piece(owner, 1, 1, True, True)
        else:

            @pl.when(owner < me)
            def _():
                piece(owner, 0, 0, False, False)
                piece(owner, 1, 1, False, True)

            @pl.when(owner > me)
            def _():
                mine[rows:, :] = jnp.zeros_like(mine[rows:, :])

    lanes, crossed = [], []
    for k in list(range(1, chips)) + [0]:
        near = lax.rem(place + k, chips) * 2
        work(near + 1 - core, False)
        if k == 1:
            whole.middle(0)
            whole.start(1)
        if k == 0:
            whole.middle(1)
        cross_out[k] = mine[...].astype(BF16)
        copy = remote(cross_out.at[k], cross_in.at[k], cross_send.at[k], cross_recv.at[k], cross)
        copy.start()
        crossed.append(copy)
        work(near + core, k == 0)
        if k == 1:
            whole.last(0)
        if k == 0:
            whole.last(1)
        copy.wait_recv()
        mine[...] += cross_in[k].astype(F32)
        if k:
            lane_out[k - 1] = mine[...].astype(BF16)
            copy = remote(
                lane_out.at[k - 1], lane_in.at[k - 1], lane_send.at[k - 1], lane_recv.at[k - 1], others[k - 1]
            )
            copy.start()
            lanes.append(copy)
    for k, copy in enumerate(lanes):
        copy.wait_recv()
        mine[...] += lane_in[k].astype(F32)
    grad_kv[...] = mine[...]
    for part in range(2):
        for k in range(keys):
            for r in range(repeat):
                h = k * repeat + r
                grad_q[part * rows : (part + 1) * rows, h * dim : (h + 1) * dim] = (
                    acc[part * keys + k, r * rows : (r + 1) * rows] * scale
                )
    for copy in lanes + crossed:
        copy.wait_send()
    whole.finish()
    riders.finish()


def attend_back(
    length, q, kv_all, mixed, grad_mixed, log_total, beside, base, grp, keys, repeat, dim, collective_id, riders=()
):
    owners, tokens, kv_width = kv_all.shape
    rows, width = tokens // 2, keys * repeat * dim
    chips = owners // 2
    parts = pair_parts(beside, grp)
    high, _, beside_rows, beside_width = parts.shape[2:]
    slots = pltpu.VMEM((chips, tokens, kv_width), BF16)
    return carried_call(
        partial(attend_back_kernel, (rows, keys, repeat, dim), chips, high),
        [length, q, mixed, grad_mixed, log_total, kv_all, parts, base],
        [
            jax.ShapeDtypeStruct((tokens, width), F32),
            jax.ShapeDtypeStruct((tokens, kv_width), F32),
            jax.ShapeDtypeStruct((2, beside_rows, beside_width), F32),
        ],
        [pl.BlockSpec(memory_space=pltpu.SMEM), VMEM, VMEM, VMEM, VMEM, ANY, ANY, VMEM],
        [VMEM, VMEM, VMEM],
        [
            pltpu.VMEM((tokens, kv_width), BF16),
            pltpu.VMEM((2 * keys, repeat * rows, dim), F32),
            pltpu.VMEM((2 * keys, 1, repeat * rows), F32),
            pltpu.VMEM((tokens, kv_width), F32),
            slots,
            slots,
            slots,
            slots,
            DMA((chips,)),
            DMA((chips,)),
            DMA((chips,)),
            DMA((chips,)),
            DMA,
        ]
        + PairSum.scratch(high, beside_rows, beside_width),
        comm_params(collective_id, 48),
        "attend_back",
        riders,
    )


def attention_grads_kernel(rows, grad_raw, branch, mixed_low, out):
    width = grad_raw.shape[1]
    out[:, :width] = tn(rows[...], grad_raw[...]).astype(BF16)
    out[:, width:] = tn(branch[...], mixed_low[...]).astype(BF16)


def attention_grads(rows, grad_raw, branch, mixed_low):
    (tokens, depth), width, inner = rows.shape, grad_raw.shape[1], mixed_low.shape[1]
    step = 512
    column = pl.BlockSpec((tokens, step), lambda d: (0, d))
    return pl.pallas_call(
        attention_grads_kernel,
        cost_estimate=NO_COST,
        name="attention_grads",
        grid=(depth // step,),
        out_shape=jax.ShapeDtypeStruct((depth, width + inner), BF16),
        in_specs=[
            column,
            pl.BlockSpec((tokens, width), lambda d: (0, 0)),
            column,
            pl.BlockSpec((tokens, inner), lambda d: (0, 0)),
        ],
        out_specs=pl.BlockSpec((step, width + inner), lambda d: (d, 0)),
        compiler_params=pltpu.CompilerParams(vmem_limit_bytes=32 * 2**20),
    )(rows, grad_raw, branch, mixed_low)


def write_attention_kernel(sums, *outs):
    first = 0
    for out in outs[:-1]:
        last = first + out.shape[1]
        out[...] = sums[:, first:last].astype(F32)
        first = last
    outs[-1][...] = sums[:, first:].astype(F32).T


def write_attention(sums, widths):
    depth, columns = sums.shape
    shapes = [(depth, width) for width in widths] + [(columns - sum(widths), depth)]
    return pl.pallas_call(
        write_attention_kernel,
        cost_estimate=NO_COST,
        name="write_attention",
        in_specs=[VMEM],
        out_specs=[VMEM] * len(shapes),
        out_shape=[jax.ShapeDtypeStruct(shape, F32) for shape in shapes],
        compiler_params=pltpu.CompilerParams(vmem_limit_bytes=32 * 2**20),
    )(sums)


def owner_of(kind, core):
    s = lax.axis_index("seq")
    line = lax.axis_size("seq") // 2
    other, back = kind
    half = 1 - s // line if other else s // line
    place = lax.rem(lax.rem(s, line) // 2 + line // 2 - back, line // 2)
    return half * line + place * 2 + core


def weight_grads(x, grads, keep, give, first=0, last=None):
    chips, halves, depth, _ = keep.shape
    core = lax.rem(lax.axis_index("seq"), 2)

    def one(t, carry):
        cut = pl.ds(pl.multiple_of(t * 2 * depth, 2 * depth), 2 * depth)
        both = tn(x[:, cut], grads[...]).astype(BF16)
        chip, which = lax.rem(t, chips), t // chips

        @pl.when(core == 0)
        def _():
            keep[chip, which] = both[:depth]
            give[chip, which] = both[depth:]

        @pl.when(core == 1)
        def _():
            keep[chip, which] = both[depth:]
            give[chip, which] = both[:depth]

        return carry

    lax.fori_loop(first, halves * chips if last is None else last, one, 0)


def mlp_kernel(shared, alone, rows, cot_home, cot_away, *refs):
    count = 2 * len(shared) + len(alone)
    blocks, refs = refs[:count], refs[count:]
    inner, out_weights, down, gate, up, grad_rows, refs = *refs[:6], refs[6:]
    weights, cot, grad_pre, keep_down, give_down, got_down, keep, give, got, *refs = refs
    *far_down, weight_sems, over_sems, cot_sems, core_sems, chip_sems = refs
    core, mate = lax.rem(lax.axis_index("seq"), 2), peer_of("core")
    depth, chips = blocks[0].shape[0], keep.shape[0]
    greet([mate] + [peer_of(k) for k in range(1, chips)])

    def place(kind, which):
        return weights.at[pl.ds(pl.multiple_of(owner_of(kind, which) * depth, depth), depth)]

    over = [
        send(src, place(kind, core), over_sems.at[0, i], over_sems.at[1, i], mate)
        for i, (kind, src) in enumerate(zip(alone, blocks[2 * len(shared) :]))
    ]
    kinds = [(kind, core) for kind in shared] + [(kind, 1 - core) for kind in shared]
    kinds += [(kind, core) for kind in alone]
    loads = []
    for i, ((kind, which), src) in enumerate(zip(kinds, blocks)):
        loads.append(pltpu.make_async_copy(src, place(kind, which), weight_sems.at[i]))
        loads[i].start()

    block = cot_home.shape[1]
    row = lax.axis_index("seq") // (lax.axis_size("seq") // 2)

    def load(i, src):
        return pltpu.make_async_copy(src, cot.at[pl.ds(i * block, block)], cot_sems.at[i])

    for k, order in enumerate(
        (
            (cot_home.at[0], cot_away.at[0], cot_home.at[1], cot_away.at[1]),
            (cot_away.at[1], cot_home.at[1], cot_away.at[0], cot_home.at[0]),
        )
    ):

        @pl.when(row == k)
        def _():
            for i, src in enumerate(order):
                load(i, src).start()

    for copy in loads:
        copy.wait()
    for i in range(4):
        load(i, cot_home.at[0]).wait()
    for copy in over:
        copy.wait()

    units = inner.shape[1]
    step = 256 if units % 256 == 0 else 128
    tile = 512
    tiles = rows.shape[0] // tile

    def one(t, carry):
        here = pl.ds(pl.multiple_of(lax.rem(t, tiles) * tile, tile), tile)
        first = pl.multiple_of((t // tiles) * step, step)
        cols = pl.ds(first, step)
        x = rows[here, :]
        gate_pre = nn(x, weights[:, cols])
        up_pre = nn(x, weights[:, pl.ds(units + first, step)])
        grad = nn(cot[here, :], weights[:, pl.ds(2 * units + first, step)])
        sigmoid = jax.nn.sigmoid(gate_pre)
        silu = gate_pre * sigmoid
        inner[here, cols] = (silu * up_pre).astype(BF16)
        grad_gate = grad * up_pre * sigmoid * (1.0 + gate_pre * (1.0 - sigmoid))
        grad_pre[here, cols] = grad_gate.astype(BF16)
        grad_pre[here, pl.ds(units + first, step)] = (grad * silu).astype(BF16)
        return carry

    lax.fori_loop(0, tiles * (units // step), one, 0)
    weight_grads(cot, inner, keep_down, give_down)
    over_down = send(give_down, got_down, core_sems.at[0, 0], core_sems.at[0, 1], mate)
    weight_grads(rows, grad_pre, keep, give, 0, chips)
    over_down.wait()

    def add_down(t, carry):
        at = (lax.rem(t, chips), t // chips)
        keep_down[at] = (keep_down[at].astype(F32) + got_down[at].astype(F32)).astype(BF16)
        return carry

    lax.fori_loop(0, 2 * chips, add_down, 0)
    to_chips = [
        send(
            keep_down.at[part_of(k, "chip")],
            far_down[k - 1],
            chip_sems.at[0, k - 1],
            chip_sems.at[1, k - 1],
            peer_of(k),
        )
        for k in range(1, chips)
    ]
    weight_grads(rows, grad_pre, keep, give, chips, None)
    over_pre = send(give, got, core_sems.at[1, 0], core_sems.at[1, 1], mate)

    def two(t, carry):
        here = pl.ds(pl.multiple_of(t * tile, tile), tile)
        grad_rows[here, :] = nt(grad_pre[here, :], weights[:, : 2 * units]).astype(BF16)
        return carry

    lax.fori_loop(0, tiles, two, 0)
    out_weights[...] = weights[:, 2 * units :]
    over_pre.wait()

    def add(t, carry):
        at = (lax.rem(t, chips), t // chips)
        both = (keep[at].astype(F32) + got[at].astype(F32)).astype(BF16)
        gate[at] = both[:, :units]
        up[at] = both[:, units:]
        return carry

    lax.fori_loop(0, 2 * chips, add, 0)
    total_down = keep_down[pl.ds(part_of(0, "chip"), 1)][0].astype(F32)
    for k, copy in enumerate(to_chips):
        copy.wait()
        total_down = total_down + far_down[k][...].astype(F32)
    down[...] = total_down.astype(BF16)


def grads_shape(width, columns):
    chips = lax.axis_size("seq") // 4
    return jax.ShapeDtypeStruct((chips, 2, width // chips // 4, columns), BF16)


def mlp(shared, alone, rows, cot_home, cot_away, collective_id):
    blocks = [x for x, _ in shared.values()] + [x for _, x in shared.values()] + list(alone.values())
    (tokens, width), columns = rows.shape, blocks[0].shape[1]
    units = columns // 3
    one, two = grads_shape(width, units), grads_shape(width, 2 * units)
    far, others = jax.ShapeDtypeStruct(one.shape[1:], BF16), one.shape[0] - 1
    results, _ = carried_call(
        lambda riders, *refs: mlp_kernel(list(shared), list(alone), *refs),
        [rows, cot_home, cot_away, *blocks],
        [
            jax.ShapeDtypeStruct((tokens, units), BF16),
            jax.ShapeDtypeStruct((width, units), BF16),
            far,
            one,
            one,
            jax.ShapeDtypeStruct((tokens, width), BF16),
        ],
        [VMEM, ANY, ANY] + [ANY] * len(blocks),
        [VMEM] * 6,
        [
            pltpu.VMEM((width, columns), BF16),
            pltpu.VMEM((tokens, width), BF16),
            pltpu.VMEM((tokens, 2 * units), BF16),
        ]
        + [pltpu.VMEM(one.shape, BF16)] * 3
        + [pltpu.VMEM(two.shape, BF16)] * 3
        + [pltpu.VMEM(far.shape, BF16)] * others
        + [DMA((len(blocks),)), DMA((2, len(alone))), DMA((4,)), DMA((2, 2)), DMA((2, others))],
        comm_params(collective_id, 60),
        "mlp",
    )
    return results


def write_kernel(sums, taken, out):
    units = taken.shape[1]
    row = lax.axis_index("seq") // (lax.axis_size("seq") // 2)
    kept, other = sums[row].astype(F32), taken[...].astype(F32)
    out[:, :units] = jnp.where(row == 0, kept, other)
    out[:, units:] = jnp.where(row == 0, other, kept)


def write_down_kernel(sums, taken, out):
    units = taken.shape[1]
    row = lax.axis_index("seq") // (lax.axis_size("seq") // 2)
    kept, other = sums[row].astype(F32), taken[...].astype(F32)
    out[:units] = jnp.where(row == 0, kept, other).T
    out[units:] = jnp.where(row == 0, other, kept).T


def write(kernel, sums, taken, shape, name):
    return pl.pallas_call(
        kernel,
        cost_estimate=NO_COST,
        name=name,
        in_specs=[VMEM, VMEM],
        out_specs=VMEM,
        out_shape=jax.ShapeDtypeStruct(shape, F32),
        compiler_params=pltpu.CompilerParams(vmem_limit_bytes=32 * 2**20),
    )(sums, taken)


def shards(
    tokens,
    lengths,
    attn_gain,
    w_query,
    w_key,
    w_value,
    query_gain,
    key_gain,
    w_out,
    mlp_gain,
    w_gate,
    w_up,
    w_down,
    cotangent,
):
    seq, grp = lax.axis_size("seq"), lax.axis_size("grp")
    seq_index, grp_index = lax.axis_index("seq"), lax.axis_index("grp")
    local_rows, width = tokens.shape[1:]
    rows = local_rows * grp
    dim = query_gain.shape[0]
    queries, keys = w_query.shape[1] // dim, w_key.shape[1] // dim
    repeat = queries // keys
    hidden_units = w_gate.shape[1]
    chunk = attn_gain.shape[0]
    depth = width // seq

    line = seq // 2
    row = seq_index // line

    def to_give(values):
        return lax.dynamic_index_in_dim(values, 1 - row, 0, keepdims=False)

    def both_rows(values, taken):
        kept = lax.dynamic_index_in_dim(values, row, 0, keepdims=False)
        return jnp.stack([jnp.where(row == 0, kept, taken), jnp.where(row == 0, taken, kept)])

    length = lax.dynamic_slice(lengths, (row,), (1,))

    half_units = hidden_units // 2
    opposite = [(s, (s + line) % seq) for s in range(seq)]

    def half(which):
        cut = [
            lax.dynamic_slice_in_dim(w, which * half_units, half_units, 1)
            for w in (w_gate, w_up, w_down.T)
        ]
        return jnp.concatenate(cut, axis=1)

    chips = line // 2
    steps = range(1, chips)
    place = lax.rem(seq_index, line) // 2

    def next_chip(k):
        return [(s, s - s % line + (s % line + 2 * k) % line) for s in range(seq)]

    def chips_sum(parts, arrived):
        mine = lax.dynamic_index_in_dim(parts, place, 0, keepdims=False)
        return sum([x.astype(F32) for x in arrived], mine.astype(F32)).astype(BF16)

    def to_chips(parts):
        return [(k, parts, "chip") for k in steps]

    projections = jnp.concatenate([w_query, w_key, w_value], axis=1)
    full_qkv = lax.all_gather(projections, "seq", axis=0, tiled=True)
    lane = max(128, chunk)
    packed = jnp.pad(jnp.stack([attn_gain, mlp_gain]), ((0, 6), (0, lane - chunk)))
    spread_gains, (taken_tokens,) = spread(packed, seq, grp, 1, [("opposite", to_give(tokens))])
    spread_gains = spread_gains[:, :, :, :chunk].transpose(2, 1, 0, 3)
    gain_attn = spread_gains[0].reshape(-1)
    gain_mlp = spread_gains[1].reshape(-1)
    full_out = lax.all_gather(after(w_out.T, taken_tokens), "seq", axis=0, tiled=True)
    residual = both_rows(tokens, taken_tokens).astype(F32)
    attn_unit, attn_inverse = normalize(residual)
    attn_rows, _ = gather_rows((attn_unit * gain_attn).astype(BF16), grp, 2, "gather_inputs")
    kept_half, given_half = after((half(row), half(1 - row)), attn_rows)
    taken_half = lax.ppermute(given_half, "seq", opposite)
    token_pos = (seq_index * grp + grp_index) * local_rows + jnp.arange(local_rows, dtype=jnp.int32)
    valid_rows = (token_pos[None, :] < lengths[:, None]).astype(BF16)
    cot_home = cotangent * valid_rows[:, :, None]

    frequency = ROPE_BASE ** (-jnp.arange(dim // 2, dtype=F32) * 2.0 / dim)
    small = [jnp.tile(frequency, 2)[None], query_gain[None], key_gain[None]]
    raw, q, kv_home = heads_forward(attn_rows, full_qkv, small, queries, keys)

    (mixed, mixed_low, log_total, kv_all, cot_gathered), _ = attend(
        length, q, kv_home, cot_home, seq, grp, keys, repeat, dim, 3
    )
    cot_gathered = cot_gathered.reshape(2, rows, width)
    near = after(kept_half, mixed)
    kept_passed = [lax.ppermute(near, "seq", next_chip(k)) for k in steps]
    summed, (taken_cotangent,) = sum_rows(
        nt(mixed_low, full_out), grp, 4, "sum_attention", [("opposite", cot_home)]
    )
    early = jnp.where(row == 0, cot_home[0], taken_cotangent[1])
    late = jnp.where(row == 0, taken_cotangent[0], cot_home[1])
    cot_rows = jnp.stack([early, late]).astype(F32)
    hidden = residual + summed

    mlp_unit, mlp_inverse = normalize(hidden)
    mlp_rows, cot_away, (core_kept, core_taken, *taken_passed) = gather_pair(
        (mlp_unit * gain_mlp).astype(BF16),
        taken_cotangent,
        grp,
        5,
        "gather_mlp",
        [("core", kept_half), ("core", taken_half)] + [(k, taken_half) for k in steps],
    )
    shared = {(False, 0): (kept_half, core_kept), (True, 0): (taken_half, core_taken)}
    alone = {(False, k): x for k, x in zip(steps, kept_passed)}
    alone.update({(True, k): x for k, x in zip(steps, taken_passed)})
    inner_low, down_weights, down, gate, up, grad_mlp_part = mlp(
        shared, alone, mlp_rows, cot_gathered, cot_away, 13
    )
    grad_mlp_in, out_part, arrived = sum_pair(
        grad_mlp_part,
        inner_low,
        down_weights,
        grp,
        7,
        "sum_mlp_back",
        [("opposite", down, "row")] + to_chips(gate),
    )
    taken_down, *arrived = arrived
    gate = chips_sum(gate, arrived)
    grad_gain_mlp = jnp.sum(grad_mlp_in * mlp_unit, axis=(0, 1))
    grad_hidden = cot_rows + norm_back(grad_mlp_in * gain_mlp, mlp_unit, mlp_inverse)
    grad_branch, (taken_gate, *arrived) = gather_rows(
        grad_hidden.astype(BF16),
        grp,
        8,
        "gather_branch",
        [("opposite", gate, "row")] + to_chips(up),
    )
    up = chips_sum(up, arrived)

    grad_mixed = nn(grad_branch, full_out).astype(BF16)
    (grad_q, grad_kv, summed), (taken_up,) = attend_back(
        length,
        q,
        kv_all,
        mixed,
        grad_mixed,
        log_total,
        out_part,
        hidden,
        grp,
        keys,
        repeat,
        dim,
        9,
        [("opposite", up, "row")],
    )
    output = jnp.where(row == 0, summed, summed[::-1]).astype(BF16)
    grad_raw, head_gain_parts = heads_backward(raw, grad_q, grad_kv, small, queries, keys)
    grad_w_attn = attention_grads(attn_rows, grad_raw, grad_branch, mixed_low)
    sum_attn = lax.psum_scatter(grad_w_attn, "seq", scatter_dimension=0, tiled=True)
    grad_attn_part = nt(after(grad_raw, grad_w_attn), full_qkv)
    grad_attn_in, _ = sum_rows(grad_attn_part, grp, 10, "sum_attention_back")
    wide_shape = (depth, hidden_units)
    taken_down, taken_gate, taken_up = after((taken_down, taken_gate, taken_up), grad_attn_in)
    out_down = write(write_down_kernel, down, taken_down, wide_shape[::-1], "write_down")
    out_gate = write(write_kernel, gate, taken_gate, wide_shape, "write_gate")
    out_up = write(write_kernel, up, taken_up, wide_shape, "write_up")
    grad_gain_attn = jnp.sum(grad_attn_in * attn_unit, axis=(0, 1))
    grad_tokens = grad_hidden + norm_back(grad_attn_in * gain_attn, attn_unit, attn_inverse)

    head_gain_grads = jnp.stack(
        [
            jnp.sum(head_gain_parts[:queries, 0], axis=0),
            jnp.sum(head_gain_parts[queries : queries + keys, 0], axis=0),
        ]
    )
    vector = jnp.concatenate([grad_gain_attn, grad_gain_mlp, head_gain_grads.reshape(-1)])
    padded = -(-vector.shape[0] // 1024) * 1024
    vector = jnp.pad(vector, (0, padded - vector.shape[0])).reshape(-1, 128)
    sums, (taken_grads,) = total(
        vector, seq, grp, 12, [("opposite", to_give(grad_tokens).astype(BF16))]
    )
    sums = sums.reshape(-1)
    grad_tokens = both_rows(grad_tokens, taken_grads.astype(F32))
    place = (seq_index * grp + grp_index) * chunk
    out_attn_gain = lax.dynamic_slice(sums, (place,), (chunk,))
    out_mlp_gain = lax.dynamic_slice(sums, (width + place,), (chunk,))
    out_query_gain = sums[2 * width : 2 * width + dim]
    out_key_gain = sums[2 * width + dim : 2 * width + 2 * dim]

    out_query, out_key, out_value, out_out = write_attention(
        sum_attn, (queries * dim, keys * dim, keys * dim)
    )
    return (
        output,
        grad_tokens,
        out_attn_gain,
        out_query,
        out_key,
        out_value,
        out_query_gain,
        out_key_gain,
        out_out,
        out_mlp_gain,
        out_gate,
        out_up,
        out_down,
    )


def solution(mesh):
    rows = P(None, ("seq", "grp"), None)
    vector = P(("seq", "grp"))
    wide, tall = P("seq", "grp"), P("grp", "seq")
    return jax.shard_map(
        shards,
        mesh=mesh,
        in_specs=(
            rows,
            P(),
            vector,
            wide,
            wide,
            wide,
            P(),
            P(),
            tall,
            vector,
            wide,
            wide,
            tall,
            rows,
        ),
        out_specs=(
            rows,
            rows,
            vector,
            wide,
            wide,
            wide,
            P(),
            P(),
            tall,
            vector,
            wide,
            wide,
            tall,
        ),
        check_vma=False,
    )
```

```python
from functools import partial
import math

import jax
import jax.numpy as jnp
from jax import lax
from jax.experimental import pallas as pl
from jax.experimental.pallas import tpu as pltpu
from jax.sharding import PartitionSpec as P

EPSILON = 1e-06
ROPE_BASE = 1000000.0
MESH = pl.DeviceIdType.MESH
ANY = pl.BlockSpec(memory_space=pltpu.HBM)
VMEM = pl.BlockSpec(memory_space=pltpu.VMEM)
DMA = pltpu.SemaphoreType.DMA
F32 = jnp.float32
BF16 = jnp.bfloat16


def normalize(values):
    inverse = lax.rsqrt(jnp.mean(values * values, axis=-1, keepdims=True) + EPSILON)
    return (values * inverse, inverse)


def norm_back(gradient, unit_values, inverse):
    return inverse * (
        gradient - unit_values * jnp.mean(gradient * unit_values, axis=-1, keepdims=True)
    )


def after(value, earlier):
    return lax.optimization_barrier((value, earlier))[0]


def nt(a, b):
    return lax.dot_general(a, b, (((1,), (1,)), ((), ())), preferred_element_type=F32)


def tn(a, b):
    return lax.dot_general(a, b, (((0,), (0,)), ((), ())), preferred_element_type=F32)


def nn(a, b):
    return jnp.dot(a, b, preferred_element_type=F32)


NO_COST = pl.CostEstimate(flops=1, bytes_accessed=1, transcendentals=0)


def comm_params(collective_id, mib=32):
    return pltpu.CompilerParams(
        collective_id=collective_id, has_side_effects=True, vmem_limit_bytes=mib * 2**20
    )


def greet(peers):
    barrier = pltpu.get_barrier_semaphore()
    for peer in peers:
        pl.semaphore_signal(barrier, inc=1, device_id=peer, device_id_type=MESH)
    pl.semaphore_wait(barrier, len(peers))


def send(src, dst, send_sem, recv_sem, peer):
    copy = pltpu.make_async_remote_copy(
        src_ref=src,
        dst_ref=dst,
        send_sem=send_sem,
        recv_sem=recv_sem,
        device_id=peer,
        device_id_type=MESH,
    )
    copy.start()
    return copy


def peer_of(kind):
    s, g = lax.axis_index("seq"), lax.axis_index("grp")
    line = lax.axis_size("seq") // 2
    if kind == "opposite":
        return lax.rem(s + line, 2 * line), g
    if kind == "core":
        return s + 1 - 2 * lax.rem(s, 2), g
    place = lax.rem(s, line)
    return s - place + lax.rem(place + 2 * kind, line), g


def part_of(kind, part):
    s = lax.axis_index("seq")
    line = lax.axis_size("seq") // 2
    if part == "row":
        return 1 - s // line
    return lax.rem(lax.rem(s, line) + 2 * kind, line) // 2


class Riders:
    def __init__(self, kinds, parts, sources, targets, send_sems, recv_sems):
        self.kinds, self.parts, self.sources, self.targets = kinds, parts, sources, targets
        self.send_sems, self.recv_sems = send_sems, recv_sems
        self.copies = []

    def peers(self):
        return [peer_of(kind) for kind in dict.fromkeys(self.kinds)]

    def start(self):
        for i, (kind, part) in enumerate(zip(self.kinds, self.parts)):
            src = self.sources[i] if part is None else self.sources[i].at[part_of(kind, part)]
            self.copies.append(
                send(src, self.targets[i], self.send_sems.at[i], self.recv_sems.at[i], peer_of(kind))
            )

    def finish(self):
        for copy in self.copies:
            copy.wait()


def carried_call(kernel, operands, out_shape, in_specs, out_specs, scratch, params, name, riders=()):
    riders = [rider if len(rider) == 3 else rider + (None,) for rider in riders]
    kinds, parts = [rider[0] for rider in riders], [rider[2] for rider in riders]
    arrays = [rider[1] for rider in riders]
    carried = [x.shape if part is None else x.shape[1:] for x, part in zip(arrays, parts)]
    count, ins, outs = len(arrays), len(in_specs), len(out_specs)

    def body(*refs):
        sources, refs = refs[:count], refs[count:]
        own_in, refs = refs[:ins], refs[ins:]
        targets, refs = refs[:count], refs[count:]
        own_out, refs = refs[:outs], refs[outs:]
        sems, refs = (refs[:2], refs[2:]) if count else ((None, None), refs)
        kernel(Riders(kinds, parts, sources, targets, *sems), *own_in, *own_out, *refs)

    results = pl.pallas_call(
        body,
        name=name,
        cost_estimate=NO_COST,
        out_shape=[jax.ShapeDtypeStruct(shape, x.dtype) for shape, x in zip(carried, arrays)]
        + list(out_shape),
        in_specs=[ANY] * count + list(in_specs),
        out_specs=[ANY] * count + list(out_specs),
        scratch_shapes=([DMA((count,)), DMA((count,))] if count else []) + list(scratch),
        compiler_params=params,
    )(*arrays, *operands)
    return list(results[count:]), list(results[:count])


def spread_kernel(seq, grp, riders, x_ref, out_ref, send1, recv1, send2, recv2):
    s, g = lax.axis_index("seq"), lax.axis_index("grp")
    line = [(lax.rem(s + k, seq), g) for k in range(1, seq)]
    plane = [(s, lax.rem(g + k, grp)) for k in range(1, grp)]
    greet(line + plane + riders.peers())
    out_ref[pl.ds(g, 1), pl.ds(s, 1)] = x_ref[...][None, None]
    first = [
        send(x_ref, out_ref.at[g, s], send1.at[k], recv1.at[k], peer) for k, peer in enumerate(line)
    ]
    riders.start()
    for copy in first:
        copy.wait()
    second = [
        send(out_ref.at[g], out_ref.at[g], send2.at[k], recv2.at[k], peer)
        for k, peer in enumerate(plane)
    ]
    for copy in second:
        copy.wait()
    riders.finish()


def spread(block, seq, grp, collective_id, riders=()):
    (result,), arrived = carried_call(
        partial(spread_kernel, seq, grp),
        [block],
        [jax.ShapeDtypeStruct((grp, seq) + block.shape, block.dtype)],
        [VMEM],
        [VMEM],
        [DMA((seq - 1,)), DMA((seq - 1,)), DMA((grp - 1,)), DMA((grp - 1,))],
        comm_params(collective_id),
        "gather_gains",
        riders,
    )
    return result, arrived


def total_kernel(
    seq, grp, riders, x_ref, out_ref, line_buf, part, plane_buf, send1, recv1, send2, recv2
):
    s, g = lax.axis_index("seq"), lax.axis_index("grp")
    line = [(lax.rem(s + k, seq), g) for k in range(1, seq)]
    plane = [(s, lax.rem(g + k, grp)) for k in range(1, grp)]
    greet(line + plane + riders.peers())
    riders.start()
    line_buf[pl.ds(s, 1)] = x_ref[...][None]
    first = [
        send(x_ref, line_buf.at[s], send1.at[k], recv1.at[k], peer) for k, peer in enumerate(line)
    ]
    for copy in first:
        copy.wait()
    part[...] = jnp.sum(line_buf[...], axis=0)
    plane_buf[pl.ds(g, 1)] = part[...][None]
    second = [
        send(part, plane_buf.at[g], send2.at[k], recv2.at[k], peer) for k, peer in enumerate(plane)
    ]
    for copy in second:
        copy.wait()
    out_ref[...] = jnp.sum(plane_buf[...], axis=0)
    riders.finish()


def total(block, seq, grp, collective_id, riders=()):
    (result,), arrived = carried_call(
        partial(total_kernel, seq, grp),
        [block],
        [jax.ShapeDtypeStruct(block.shape, block.dtype)],
        [VMEM],
        [VMEM],
        [
            pltpu.VMEM((seq,) + block.shape, block.dtype),
            pltpu.VMEM(block.shape, block.dtype),
            pltpu.VMEM((grp,) + block.shape, block.dtype),
            DMA((seq - 1,)),
            DMA((seq - 1,)),
            DMA((grp - 1,)),
            DMA((grp - 1,)),
        ],
        comm_params(collective_id),
        "sum_gains",
        riders,
    )
    return result, arrived


def plane_peers(high):
    s, g = lax.axis_index("seq"), lax.axis_index("grp")
    a, b = g // 2, lax.rem(g, 2)
    across = (s, a * 2 + 1 - b)
    along = [(s, lax.rem(a + k, high) * 2 + b) for k in range(1, high)]
    return a, b, across, along


class PlaneGather:
    def __init__(self, high, first, second, target, send_sems, recv_sems):
        self.high, self.first, self.second, self.target = high, first, second, target
        self.send_sems, self.recv_sems = send_sems, recv_sems
        self.slots = iter(range(4 * high))
        self.place = plane_peers(high)

    def push(self, what, where, peer):
        k = next(self.slots)
        return send(what, where, self.send_sems.at[k], self.recv_sems.at[k], peer)

    def start(self):
        a, b, across, along = self.place
        here0, here1 = self.target.at[0, a, b], self.target.at[1, a, b]
        self.early = [self.push(self.first, here0, across)]
        self.early += [self.push(self.second, here1, peer) for peer in along]
        self.late = [self.push(self.second, here1, across)]
        self.late += [self.push(self.first, here0, peer) for peer in along]

    def forward(self):
        a, b, across, along = self.place
        self.early[0].wait_recv()
        passed = self.target.at[0, a, 1 - b]
        self.late += [self.push(passed, passed, peer) for peer in along]
        for k in range(1, self.high):
            self.early[k].wait_recv()
            passed = self.target.at[1, lax.rem(a + self.high - k, self.high), b]
            self.late.append(self.push(passed, passed, across))

    def finish(self):
        for copy in self.late:
            copy.wait_recv()
        for copy in self.early + self.late:
            copy.wait_send()


def gather_rows_kernel(high, riders, src, dst, send_sems, recv_sems, local_sem):
    a, b, across, along = plane_peers(high)
    greet([across] + along + riders.peers())
    riders.start()
    home = pltpu.make_async_copy(src, dst.at[:, a, b], local_sem)
    home.start()
    plane = PlaneGather(high, src.at[0], src.at[1], dst, send_sems, recv_sems)
    plane.start()
    plane.forward()
    plane.finish()
    home.wait()
    riders.finish()


def plane_shape(array, grp):
    rows, width = array.shape[1:]
    return jax.ShapeDtypeStruct((2, grp // 2, 2, rows, width), array.dtype)


def gather_rows(array, grp, collective_id, name, riders=()):
    high = grp // 2
    (result,), arrived = carried_call(
        partial(gather_rows_kernel, high),
        [array],
        [plane_shape(array, grp)],
        [ANY],
        [ANY],
        [DMA((4 * high,)), DMA((4 * high,)), DMA],
        comm_params(collective_id),
        name,
        riders,
    )
    return result.reshape(2 * grp * array.shape[1], array.shape[2]), arrived


def sum_rows_kernel(high, riders, src, out, recv0, mid0, last0, recv1, mid1, last1, own0, own1, send_sems, recv_sems, local_sems):
    a, b, across, along = plane_peers(high)
    greet([across] + along + riders.peers())
    riders.start()
    slots = iter(range(2 * high))

    def push(what, where, peer):
        k = next(slots)
        return send(what, where, send_sems.at[k], recv_sems.at[k], peer)

    over0 = push(src.at[0, :, 1 - b], recv0, across)
    up1 = [
        push(src.at[1, lax.rem(a + k, high)], recv1.at[k - 1], along[k - 1]) for k in range(1, high)
    ]
    load0 = pltpu.make_async_copy(src.at[0, :, b], own0, local_sems.at[0])
    load1 = pltpu.make_async_copy(src.at[1, a], own1, local_sems.at[1])
    load0.start()
    load1.start()
    load0.wait()
    load1.wait()
    over0.wait_recv()
    mid0[...] = (own0[...].astype(F32) + recv0[...].astype(F32)).astype(BF16)
    up0 = [
        push(mid0.at[lax.rem(a + k, high)], last0.at[k - 1], along[k - 1]) for k in range(1, high)
    ]
    for copy in up1:
        copy.wait_recv()
    joined = own1[...].astype(F32)
    for k in range(1, high):
        joined = joined + recv1[k - 1].astype(F32)
    mid1[...] = joined.astype(BF16)
    over1 = push(mid1.at[1 - b], last1, across)
    for copy in up0:
        copy.wait_recv()
    result = own0[pl.ds(a, 1)][0].astype(F32) + recv0[pl.ds(a, 1)][0].astype(F32)
    for k in range(1, high):
        result = result + last0[k - 1].astype(F32)
    out[0] = result
    over1.wait_recv()
    result = own1[pl.ds(b, 1)][0].astype(F32)
    for k in range(1, high):
        result = result + recv1[k - 1, pl.ds(b, 1)][0].astype(F32)
    out[1] = result + last1[...].astype(F32)
    for copy in [over0, over1] + up0 + up1:
        copy.wait_send()
    riders.finish()


def sum_rows(partial_sums, grp, collective_id, name, riders=()):
    high = grp // 2
    tokens, width = partial_sums.shape
    rows = tokens // (2 * grp)
    parts = partial_sums.astype(BF16).reshape(2, high, 2, rows, width)
    (result,), arrived = carried_call(
        partial(sum_rows_kernel, high),
        [parts],
        [jax.ShapeDtypeStruct((2, rows, width), F32)],
        [ANY],
        [VMEM],
        [
            pltpu.VMEM((high, rows, width), BF16),
            pltpu.VMEM((high, rows, width), BF16),
            pltpu.VMEM((high - 1, rows, width), BF16),
            pltpu.VMEM((high - 1, 2, rows, width), BF16),
            pltpu.VMEM((2, rows, width), BF16),
            pltpu.VMEM((rows, width), BF16),
            pltpu.VMEM((high, rows, width), BF16),
            pltpu.VMEM((2, rows, width), BF16),
            DMA((2 * high,)),
            DMA((2 * high,)),
            DMA((2,)),
        ],
        comm_params(collective_id),
        name,
        riders,
    )
    return result, arrived


def pair_peer():
    s, g = lax.axis_index("seq"), lax.axis_index("grp")
    line = lax.axis_size("seq") // 2
    return s // line, (lax.rem(s + line, 2 * line), g)


def gather_pair_kernel(
    high, riders, src, beside, dst, beside_dst, send_sems, recv_sems, pair_sems, local_sems
):
    a, b, across, along = plane_peers(high)
    _, pair = pair_peer()
    greet([across, pair] + along + riders.peers())
    over_pair = send(src, dst.at[1, :, a, b], pair_sems.at[0], pair_sems.at[1], pair)
    homes = [
        pltpu.make_async_copy(src, dst.at[0, :, a, b], local_sems.at[0]),
        pltpu.make_async_copy(beside, beside_dst.at[:, a, b], local_sems.at[1]),
    ]
    for copy in homes:
        copy.start()
    given = dst.at[1, :, a, b]
    planes = [
        PlaneGather(high, first, second, target, send_sems.at[i], recv_sems.at[i])
        for i, (first, second, target) in enumerate(
            (
                (src.at[0], src.at[1], dst.at[0]),
                (beside.at[0], beside.at[1], beside_dst),
                (given.at[0], given.at[1], dst.at[1]),
            )
        )
    ]
    planes[0].start()
    planes[1].start()
    planes[0].forward()
    over_pair.wait_recv()
    riders.start()
    planes[2].start()
    planes[1].forward()
    planes[2].forward()
    for plane in planes:
        plane.finish()
    over_pair.wait_send()
    for copy in homes:
        copy.wait()
    riders.finish()


def gather_pair(array, beside, grp, collective_id, name, riders=()):
    high = grp // 2
    rows, width = array.shape[1:]
    both = jax.ShapeDtypeStruct((2,) + plane_shape(array, grp).shape, array.dtype)
    (result, beside), arrived = carried_call(
        partial(gather_pair_kernel, high),
        [array, beside],
        [both, plane_shape(beside, grp)],
        [ANY, ANY],
        [ANY, ANY],
        [DMA((3, 4 * high)), DMA((3, 4 * high)), DMA((2,)), DMA((2,))],
        comm_params(collective_id, 60),
        name,
        riders,
    )
    result, beside = result.reshape(4 * grp * rows, width), beside.reshape(2, grp * rows, width)
    return result, beside, arrived


class PairSum:
    def __init__(self, high, src, out, scratch, base=None):
        self.high, self.src, self.out, self.base = high, src, out, base
        self.recv0, self.mid0, self.last0, self.recv1, self.mid1, self.last1 = scratch[:6]
        self.own0, self.own1, self.given, self.taken = scratch[6:10]
        self.send_sems, self.recv_sems, self.pair_sems, self.local_sems = scratch[10:]
        self.place = plane_peers(high)
        self.pair = pair_peer()[1]
        self.slots = [iter(range(2 * high)), iter(range(2 * high))]
        self.sent, self.first, self.second = [[], []], [None, None], [None, None]

    @staticmethod
    def scratch(high, rows, width):
        return [
            pltpu.VMEM((2, high, rows, width), BF16),
            pltpu.VMEM((2, high, rows, width), BF16),
            pltpu.VMEM((2, high - 1, rows, width), BF16),
            pltpu.VMEM((2, high - 1, 2, rows, width), BF16),
            pltpu.VMEM((2, 2, rows, width), BF16),
            pltpu.VMEM((2, rows, width), BF16),
            pltpu.VMEM((2, high, rows, width), BF16),
            pltpu.VMEM((2, 2, rows, width), BF16),
            pltpu.VMEM((2, rows, width), BF16),
            pltpu.VMEM((2, rows, width), BF16),
            DMA((2, 2 * high)),
            DMA((2, 2 * high)),
            DMA((2,)),
            DMA((2, 2)),
        ]

    def push(self, i, what, where, peer):
        k = next(self.slots[i])
        copy = send(what, where, self.send_sems.at[i, k], self.recv_sems.at[i, k], peer)
        self.sent[i].append(copy)
        return copy

    def block(self, i):
        row = pair_peer()[0]
        return row if i else 1 - row

    def start(self, i):
        a, b, across, along = self.place
        if self.base is None:
            first, second = self.src.at[1 - i, 0], self.src.at[1 - i, 1]
        else:
            first, second = self.src.at[0, self.block(i)], self.src.at[1, self.block(i)]
        over0 = self.push(i, first.at[:, 1 - b], self.recv0.at[i], across)
        up1 = [
            self.push(i, second.at[lax.rem(a + k, self.high)], self.recv1.at[i, k - 1], along[k - 1])
            for k in range(1, self.high)
        ]
        loads = [
            pltpu.make_async_copy(first.at[:, b], self.own0.at[i], self.local_sems.at[i, 0]),
            pltpu.make_async_copy(second.at[a], self.own1.at[i], self.local_sems.at[i, 1]),
        ]
        for load in loads:
            load.start()
        self.first[i] = (over0, up1, loads)

    def middle(self, i):
        a, b, across, along = self.place
        over0, up1, loads = self.first[i]
        for load in loads:
            load.wait()
        over0.wait_recv()
        self.mid0[i] = (self.own0[i].astype(F32) + self.recv0[i].astype(F32)).astype(BF16)
        up0 = [
            self.push(
                i, self.mid0.at[i, lax.rem(a + k, self.high)], self.last0.at[i, k - 1], along[k - 1]
            )
            for k in range(1, self.high)
        ]
        for copy in up1:
            copy.wait_recv()
        joined = self.own1[i].astype(F32)
        for k in range(1, self.high):
            joined = joined + self.recv1[i, k - 1].astype(F32)
        self.mid1[i] = joined.astype(BF16)
        over1 = self.push(i, self.mid1.at[i, 1 - b], self.last1.at[i], across)
        self.second[i] = (up0, over1)

    def last(self, i):
        a, b, across, along = self.place
        up0, over1 = self.second[i]
        for copy in up0:
            copy.wait_recv()
        result0 = self.own0[i, pl.ds(a, 1)][0].astype(F32) + self.recv0[i, pl.ds(a, 1)][0].astype(F32)
        for k in range(1, self.high):
            result0 = result0 + self.last0[i, k - 1].astype(F32)
        if self.base is not None:
            result0 = result0 + self.base[pl.ds(self.block(i), 1)][0]
        over1.wait_recv()
        result1 = self.own1[i, pl.ds(b, 1)][0].astype(F32) + self.last1[i].astype(F32)
        for k in range(1, self.high):
            result1 = result1 + self.recv1[i, k - 1, pl.ds(b, 1)][0].astype(F32)
        if i == 0:
            self.given[0] = result0.astype(BF16)
            self.given[1] = result1.astype(BF16)
            self.over_pair = send(
                self.given, self.taken, self.pair_sems.at[0], self.pair_sems.at[1], self.pair
            )
        else:
            self.out[0] = result0
            self.out[1] = result1

    def finish(self):
        self.over_pair.wait_recv()
        for k in range(2):
            self.out[k] += self.taken[k if self.base is None else 1 - k].astype(F32)
        self.over_pair.wait_send()
        for copy in self.sent[0] + self.sent[1]:
            copy.wait_send()


def sum_pair_kernel(high, riders, src, inner, weights, out, product, *scratch):
    a, b, across, along = plane_peers(high)
    greet([across, pair_peer()[1]] + along + riders.peers())
    riders.start()
    whole = PairSum(high, src, out, scratch)
    whole.start(0)
    whole.middle(0)
    whole.start(1)
    tile = 512

    def one(t, carry):
        here = pl.ds(pl.multiple_of(t * tile, tile), tile)
        product[here, :] = nt(inner[here, :], weights[...]).astype(BF16)
        return carry

    lax.fori_loop(0, inner.shape[0] // tile, one, 0)
    whole.last(0)
    whole.middle(1)
    whole.last(1)
    whole.finish()
    riders.finish()


def pair_parts(partial_sums, grp):
    tokens, width = partial_sums.shape
    return partial_sums.reshape(2, 2, grp // 2, 2, tokens // (4 * grp), width)


def sum_pair(partial_sums, inner, weights, grp, collective_id, name, riders=()):
    parts = pair_parts(partial_sums, grp)
    high, _, rows, width = parts.shape[2:]
    (result, product), arrived = carried_call(
        partial(sum_pair_kernel, high),
        [parts, inner, weights],
        [
            jax.ShapeDtypeStruct((2, rows, width), F32),
            jax.ShapeDtypeStruct(partial_sums.shape, BF16),
        ],
        [ANY, VMEM, VMEM],
        [VMEM, VMEM],
        PairSum.scratch(high, rows, width),
        comm_params(collective_id, 48),
        name,
        riders,
    )
    return result, product, arrived


def turn_half(values):
    half = values.shape[-1] // 2
    return jnp.concatenate([-values[:, half:], values[:, :half]], axis=-1)


def fill_tables(frequency, cosine, sine):
    line = lax.axis_size("seq") // 2
    rows, dim = cosine.shape[0] // 2, cosine.shape[1]
    for part in range(2):
        first = (lax.rem(lax.axis_index("seq"), line) + part * line) * rows
        position = first + lax.broadcasted_iota(jnp.int32, (rows, dim), 0)
        angles = position.astype(F32) * frequency[...]
        cosine[part * rows : (part + 1) * rows] = jnp.cos(angles)
        sine[part * rows : (part + 1) * rows] = jnp.sin(angles)


def heads_kernel(queries, keys, x, w, frequency, query_gain, key_gain, raw, q, kv, cosine, sine):
    step, dim = pl.program_id(0), cosine.shape[1]
    pl.when(step == 0)(lambda: fill_tables(frequency, cosine, sine))
    raw[...] = nn(x[...], w[...])
    for i in range(raw.shape[1] // dim):
        head, cut = step * (raw.shape[1] // dim) + i, slice(i * dim, (i + 1) * dim)

        def turned(gain):
            unit, _ = normalize(raw[:, cut])
            scaled = unit * gain[...]
            return (scaled * cosine[...] + turn_half(scaled) * sine[...]).astype(BF16)

        @pl.when(head < queries)
        def _():
            q[:, cut] = turned(query_gain)

        @pl.when((head >= queries) & (head < queries + keys))
        def _():
            kv[:, cut] = turned(key_gain)

        @pl.when(head >= queries + keys)
        def _():
            kv[:, cut] = raw[:, cut].astype(BF16)


def heads_forward(x, w, small, queries, keys):
    (tokens, depth), width, dim = x.shape, w.shape[1], small[0].shape[1]
    step = 2 * dim
    column = pl.BlockSpec((tokens, step), lambda h: (0, h))
    one = pl.BlockSpec((1, dim), lambda h: (0, 0))
    return pl.pallas_call(
        partial(heads_kernel, queries, keys),
        cost_estimate=NO_COST,
        name="heads_forward",
        grid=(width // step,),
        out_shape=[
            jax.ShapeDtypeStruct((tokens, width), F32),
            jax.ShapeDtypeStruct((tokens, queries * dim), BF16),
            jax.ShapeDtypeStruct((tokens, 2 * keys * dim), BF16),
        ],
        in_specs=[
            pl.BlockSpec((tokens, depth), lambda h: (0, 0)),
            pl.BlockSpec((depth, step), lambda h: (0, h)),
            one,
            one,
            one,
        ],
        out_specs=[
            column,
            pl.BlockSpec((tokens, step), lambda h: (0, jnp.minimum(h, queries // 2 - 1))),
            pl.BlockSpec((tokens, step), lambda h: (0, jnp.maximum(h - queries // 2, 0))),
        ],
        scratch_shapes=[pltpu.VMEM((tokens, dim), F32), pltpu.VMEM((tokens, dim), F32)],
        compiler_params=pltpu.CompilerParams(vmem_limit_bytes=60 * 2**20),
    )(x, w, *small)


def heads_back_kernel(
    queries, keys, raw, grad_q, grad_kv, frequency, query_gain, key_gain, out, gain_out, cosine, sine
):
    head = pl.program_id(0)
    pl.when(head == 0)(lambda: fill_tables(frequency, cosine, sine))

    def turned_back(given):
        unit, inverse = normalize(raw[...])
        turned = given * cosine[...] - turn_half(given * sine[...])
        gain_out[...] = jnp.broadcast_to(
            jnp.sum(turned * unit, axis=0, keepdims=True)[None], gain_out.shape
        )
        scaled = turned * jnp.where(head < queries, query_gain[...], key_gain[...])
        out[...] = norm_back(scaled, unit, inverse).astype(BF16)

    pl.when(head < queries)(lambda: turned_back(grad_q[...]))
    pl.when((head >= queries) & (head < queries + keys))(lambda: turned_back(grad_kv[...]))

    @pl.when(head >= queries + keys)
    def _():
        gain_out[...] = jnp.zeros_like(gain_out)
        out[...] = grad_kv[...].astype(BF16)


def heads_backward(raw, grad_q, grad_kv, small, queries, keys):
    (tokens, width), dim = raw.shape, small[0].shape[1]
    column = pl.BlockSpec((tokens, dim), lambda h: (0, h))
    one = pl.BlockSpec((1, dim), lambda h: (0, 0))
    return pl.pallas_call(
        partial(heads_back_kernel, queries, keys),
        cost_estimate=NO_COST,
        name="heads_backward",
        grid=(width // dim,),
        out_shape=[
            jax.ShapeDtypeStruct((tokens, width), BF16),
            jax.ShapeDtypeStruct((width // dim, 8, dim), F32),
        ],
        in_specs=[
            column,
            pl.BlockSpec((tokens, dim), lambda h: (0, jnp.minimum(h, queries - 1))),
            pl.BlockSpec((tokens, dim), lambda h: (0, jnp.maximum(h - queries, 0))),
            one,
            one,
            one,
        ],
        out_specs=[column, pl.BlockSpec((1, 8, dim), lambda h: (h, 0, 0))],
        scratch_shapes=[pltpu.VMEM((tokens, dim), F32), pltpu.VMEM((tokens, dim), F32)],
        compiler_params=pltpu.CompilerParams(vmem_limit_bytes=32 * 2**20),
    )(raw, grad_q, grad_kv, *small)


def half_line_peers(chips):
    s, g = lax.axis_index("seq"), lax.axis_index("grp")
    chip, core = s // 2, lax.rem(s, 2)
    place = lax.rem(chip, chips)
    others = [((chip - place + lax.rem(place + k, chips)) * 2 + core, g) for k in range(1, chips)]
    return place, core, (s + 1 - 2 * core, g), others


def remote(src, dst, send_sem, recv_sem, peer):
    return pltpu.make_async_remote_copy(
        src_ref=src,
        dst_ref=dst,
        send_sem=send_sem,
        recv_sem=recv_sem,
        device_id=peer,
        device_id_type=MESH,
    )


def allowed_pairs(query_block, key_block, length, rows, repeat, diagonal):
    key_pos = key_block * rows + lax.broadcasted_iota(jnp.int32, (rows, repeat * rows), 0)
    allowed = key_pos < length
    if diagonal:
        query_pos = lax.broadcasted_iota(jnp.int32, (rows, repeat * rows), 1)
        allowed = allowed & (key_pos <= query_block * rows + lax.rem(query_pos, rows))
    return allowed


def stacked(ref, part, rows, first, repeat, dim):
    return jnp.concatenate(
        [
            ref[part * rows : (part + 1) * rows, (first + r) * dim : (first + r + 1) * dim]
            for r in range(repeat)
        ],
        axis=0,
    )


def attend_kernel(
    shape,
    chips,
    high,
    riders,
    length,
    q,
    kv_home,
    beside,
    mixed,
    mixed_low,
    log_total,
    kv_all,
    beside_dst,
    plane_send,
    plane_recv,
    kv_buf,
    acc,
    sums,
    lane_send,
    lane_recv,
    cross_send,
    cross_recv,
    local_sems,
):
    rows, keys, repeat, dim = shape
    scale = 1.0 / math.sqrt(dim)
    place, core, cross, others = half_line_peers(chips)
    me = place * 2 + core
    a, b, across, along = plane_peers(high)
    greet([cross] + others + [across] + along + riders.peers())
    home = pltpu.make_async_copy(kv_home, kv_all.at[me], local_sems.at[0])
    home.start()
    beside_home = pltpu.make_async_copy(beside, beside_dst.at[:, a, b], local_sems.at[2])
    beside_home.start()
    plane = PlaneGather(high, beside.at[0], beside.at[1], beside_dst, plane_send, plane_recv)

    def over(i, src, owner):
        return remote(src, kv_all.at[owner], cross_send.at[i], cross_recv.at[i], cross)

    lanes = [
        remote(kv_home, kv_all.at[me], lane_send.at[k], lane_recv.at[k], peer)
        for k, peer in enumerate(others)
    ]
    crossed = [over(0, kv_home, me)]
    for copy in lanes + crossed:
        copy.start()
    plane.start()
    riders.start()
    acc[...] = jnp.zeros_like(acc)
    sums[...] = jnp.zeros_like(sums)

    def piece(owner, query_part, key_part, diagonal):
        query_block, key_block = me + query_part * 2 * chips, owner + key_part * 2 * chips
        allowed = allowed_pairs(query_block, key_block, length[0], rows, repeat, diagonal)
        here = slice(key_part * rows, (key_part + 1) * rows)
        for k in range(keys):
            unit = query_part * keys + k
            kk = kv_buf[here, k * dim : (k + 1) * dim]
            vv = kv_buf[here, (keys + k) * dim : (keys + k + 1) * dim]
            scores = nt(kk, stacked(q, query_part, rows, k * repeat, repeat, dim)) * scale
            weights = jnp.where(allowed, jnp.exp(scores), 0.0)
            sums[unit] += jnp.sum(weights, axis=0, keepdims=True)
            acc[unit] += tn(vv, weights.astype(BF16))

    def work(src, owner, own):
        load = pltpu.make_async_copy(src, kv_buf, local_sems.at[1])
        load.start()
        load.wait()
        piece(owner, 1, 0, False)
        if own:
            piece(owner, 0, 0, True)
            piece(owner, 1, 1, True)
        else:

            @pl.when(owner < me)
            def _():
                piece(owner, 0, 0, False)
                piece(owner, 1, 1, False)

    work(kv_home, me, True)
    for k in range(chips):
        near = lax.rem(place + chips - k, chips) * 2
        if k:
            owner = near + core
            lanes[k - 1].wait_recv()
            crossed.append(over(k, kv_all.at[owner], owner))
            crossed[k].start()
            work(kv_all.at[owner], owner, False)
        owner = near + 1 - core
        crossed[k].wait_recv()
        work(kv_all.at[owner], owner, False)
        if k == 0:
            plane.forward()
    for part in range(2):
        for k in range(keys):
            unit = part * keys + k
            log_total[unit] = jnp.log(sums[unit])
            result = (acc[unit] / sums[unit]).T
            for r in range(repeat):
                cut = result[r * rows : (r + 1) * rows]
                h = k * repeat + r
                mixed[part * rows : (part + 1) * rows, h * dim : (h + 1) * dim] = cut
                mixed_low[part * rows : (part + 1) * rows, h * dim : (h + 1) * dim] = cut.astype(BF16)
    home.wait()
    for copy in lanes + crossed:
        copy.wait_send()
    plane.finish()
    beside_home.wait()
    riders.finish()


def attend(length, q, kv_home, beside, seq, grp, keys, repeat, dim, collective_id, riders=()):
    tokens, kv_width = kv_home.shape
    rows, width = tokens // 2, keys * repeat * dim
    chips = seq // 4
    return carried_call(
        partial(attend_kernel, (rows, keys, repeat, dim), chips, grp // 2),
        [length, q, kv_home, beside],
        [
            jax.ShapeDtypeStruct((tokens, width), F32),
            jax.ShapeDtypeStruct((tokens, width), BF16),
            jax.ShapeDtypeStruct((2 * keys, 1, repeat * rows), F32),
            jax.ShapeDtypeStruct((2 * chips, tokens, kv_width), BF16),
            plane_shape(beside, grp),
        ],
        [pl.BlockSpec(memory_space=pltpu.SMEM), VMEM, ANY, ANY],
        [VMEM, VMEM, VMEM, ANY, ANY],
        [
            DMA((2 * grp,)),
            DMA((2 * grp,)),
            pltpu.VMEM((tokens, kv_width), BF16),
            pltpu.VMEM((2 * keys, dim, repeat * rows), F32),
            pltpu.VMEM((2 * keys, 1, repeat * rows), F32),
            DMA((chips,)),
            DMA((chips,)),
            DMA((chips,)),
            DMA((chips,)),
            DMA((3,)),
        ],
        comm_params(collective_id, 60),
        "attend",
        riders,
    )


def attend_back_kernel(
    shape,
    chips,
    high,
    riders,
    length,
    q,
    mixed,
    grad_mixed,
    log_total,
    kv_all,
    beside,
    base,
    grad_q,
    grad_kv,
    beside_out,
    kv_buf,
    acc,
    delta,
    mine,
    lane_out,
    lane_in,
    cross_out,
    cross_in,
    lane_send,
    lane_recv,
    cross_send,
    cross_recv,
    local_sem,
    *beside_scratch,
):
    rows, keys, repeat, dim = shape
    scale = 1.0 / math.sqrt(dim)
    place, core, cross, others = half_line_peers(chips)
    me = place * 2 + core
    _, _, across, along = plane_peers(high)
    greet([cross] + others + [across, pair_peer()[1]] + along + riders.peers())
    whole = PairSum(high, beside, beside_out, beside_scratch, base)
    whole.start(0)
    riders.start()
    acc[...] = jnp.zeros_like(acc)
    for part in range(2):
        for k in range(keys):
            product = stacked(mixed, part, rows, k * repeat, repeat, dim) * stacked(
                grad_mixed, part, rows, k * repeat, repeat, dim
            ).astype(F32)
            delta[part * keys + k] = jnp.sum(product.T, axis=0, keepdims=True)

    def piece(owner, query_part, key_part, diagonal, first):
        query_block, key_block = me + query_part * 2 * chips, owner + key_part * 2 * chips
        allowed = allowed_pairs(query_block, key_block, length[0], rows, repeat, diagonal)
        here = slice(key_part * rows, (key_part + 1) * rows)
        for k in range(keys):
            unit = query_part * keys + k
            key_cut, value_cut = slice(k * dim, (k + 1) * dim), slice((keys + k) * dim, (keys + k + 1) * dim)
            kk, vv = kv_buf[here, key_cut], kv_buf[here, value_cut]
            qq = stacked(q, query_part, rows, k * repeat, repeat, dim)
            gg = stacked(grad_mixed, query_part, rows, k * repeat, repeat, dim)
            weights = jnp.where(allowed, jnp.exp(nt(kk, qq) * scale - log_total[unit]), 0.0)
            grad_scores = (weights * (nt(vv, gg) - delta[unit])).astype(BF16)
            grad_k, grad_v = nn(grad_scores, qq) * scale, nn(weights.astype(BF16), gg)
            if first:
                mine[here, key_cut] = grad_k
                mine[here, value_cut] = grad_v
            else:
                mine[here, key_cut] += grad_k
                mine[here, value_cut] += grad_v
            acc[unit] += tn(grad_scores, kk)

    def work(owner, own):
        load = pltpu.make_async_copy(kv_all.at[owner], kv_buf, local_sem)
        load.start()
        load.wait()
        piece(owner, 1, 0, False, True)
        if own:
            piece(owner, 0, 0, True, False)
            piece(owner, 1, 1, True, True)
        else:

            @pl.when(owner < me)
            def _():
                piece(owner, 0, 0, False, False)
                piece(owner, 1, 1, False, True)

            @pl.when(owner > me)
            def _():
                mine[rows:, :] = jnp.zeros_like(mine[rows:, :])

    lanes, crossed = [], []
    for k in list(range(1, chips)) + [0]:
        near = lax.rem(place + k, chips) * 2
        work(near + 1 - core, False)
        if k == 1:
            whole.middle(0)
            whole.start(1)
        if k == 0:
            whole.middle(1)
        cross_out[k] = mine[...].astype(BF16)
        copy = remote(cross_out.at[k], cross_in.at[k], cross_send.at[k], cross_recv.at[k], cross)
        copy.start()
        crossed.append(copy)
        work(near + core, k == 0)
        if k == 1:
            whole.last(0)
        if k == 0:
            whole.last(1)
        copy.wait_recv()
        mine[...] += cross_in[k].astype(F32)
        if k:
            lane_out[k - 1] = mine[...].astype(BF16)
            copy = remote(
                lane_out.at[k - 1], lane_in.at[k - 1], lane_send.at[k - 1], lane_recv.at[k - 1], others[k - 1]
            )
            copy.start()
            lanes.append(copy)
    for k, copy in enumerate(lanes):
        copy.wait_recv()
        mine[...] += lane_in[k].astype(F32)
    grad_kv[...] = mine[...]
    for part in range(2):
        for k in range(keys):
            for r in range(repeat):
                h = k * repeat + r
                grad_q[part * rows : (part + 1) * rows, h * dim : (h + 1) * dim] = (
                    acc[part * keys + k, r * rows : (r + 1) * rows] * scale
                )
    for copy in lanes + crossed:
        copy.wait_send()
    whole.finish()
    riders.finish()


def attend_back(
    length, q, kv_all, mixed, grad_mixed, log_total, beside, base, grp, keys, repeat, dim, collective_id, riders=()
):
    owners, tokens, kv_width = kv_all.shape
    rows, width = tokens // 2, keys * repeat * dim
    chips = owners // 2
    parts = pair_parts(beside, grp)
    high, _, beside_rows, beside_width = parts.shape[2:]
    slots = pltpu.VMEM((chips, tokens, kv_width), BF16)
    return carried_call(
        partial(attend_back_kernel, (rows, keys, repeat, dim), chips, high),
        [length, q, mixed, grad_mixed, log_total, kv_all, parts, base],
        [
            jax.ShapeDtypeStruct((tokens, width), F32),
            jax.ShapeDtypeStruct((tokens, kv_width), F32),
            jax.ShapeDtypeStruct((2, beside_rows, beside_width), F32),
        ],
        [pl.BlockSpec(memory_space=pltpu.SMEM), VMEM, VMEM, VMEM, VMEM, ANY, ANY, VMEM],
        [VMEM, VMEM, VMEM],
        [
            pltpu.VMEM((tokens, kv_width), BF16),
            pltpu.VMEM((2 * keys, repeat * rows, dim), F32),
            pltpu.VMEM((2 * keys, 1, repeat * rows), F32),
            pltpu.VMEM((tokens, kv_width), F32),
            slots,
            slots,
            slots,
            slots,
            DMA((chips,)),
            DMA((chips,)),
            DMA((chips,)),
            DMA((chips,)),
            DMA,
        ]
        + PairSum.scratch(high, beside_rows, beside_width),
        comm_params(collective_id, 48),
        "attend_back",
        riders,
    )


def attention_grads_kernel(rows, grad_raw, branch, mixed_low, out):
    width = grad_raw.shape[1]
    out[:, :width] = tn(rows[...], grad_raw[...]).astype(BF16)
    out[:, width:] = tn(branch[...], mixed_low[...]).astype(BF16)


def attention_grads(rows, grad_raw, branch, mixed_low):
    (tokens, depth), width, inner = rows.shape, grad_raw.shape[1], mixed_low.shape[1]
    step = 512
    column = pl.BlockSpec((tokens, step), lambda d: (0, d))
    return pl.pallas_call(
        attention_grads_kernel,
        cost_estimate=NO_COST,
        name="attention_grads",
        grid=(depth // step,),
        out_shape=jax.ShapeDtypeStruct((depth, width + inner), BF16),
        in_specs=[
            column,
            pl.BlockSpec((tokens, width), lambda d: (0, 0)),
            column,
            pl.BlockSpec((tokens, inner), lambda d: (0, 0)),
        ],
        out_specs=pl.BlockSpec((step, width + inner), lambda d: (d, 0)),
        compiler_params=pltpu.CompilerParams(vmem_limit_bytes=32 * 2**20),
    )(rows, grad_raw, branch, mixed_low)


def write_attention_kernel(sums, *outs):
    first = 0
    for out in outs[:-1]:
        last = first + out.shape[1]
        out[...] = sums[:, first:last].astype(F32)
        first = last
    outs[-1][...] = sums[:, first:].astype(F32).T


def write_attention(sums, widths):
    depth, columns = sums.shape
    shapes = [(depth, width) for width in widths] + [(columns - sum(widths), depth)]
    return pl.pallas_call(
        write_attention_kernel,
        cost_estimate=NO_COST,
        name="write_attention",
        in_specs=[VMEM],
        out_specs=[VMEM] * len(shapes),
        out_shape=[jax.ShapeDtypeStruct(shape, F32) for shape in shapes],
        compiler_params=pltpu.CompilerParams(vmem_limit_bytes=32 * 2**20),
    )(sums)


def owner_of(kind, core):
    s = lax.axis_index("seq")
    line = lax.axis_size("seq") // 2
    other, back = kind
    half = 1 - s // line if other else s // line
    place = lax.rem(lax.rem(s, line) // 2 + line // 2 - back, line // 2)
    return half * line + place * 2 + core


def weight_grads(x, grads, keep, give, first=0, last=None):
    chips, halves, depth, _ = keep.shape
    core = lax.rem(lax.axis_index("seq"), 2)

    def one(t, carry):
        cut = pl.ds(pl.multiple_of(t * 2 * depth, 2 * depth), 2 * depth)
        both = tn(x[:, cut], grads[...]).astype(BF16)
        chip, which = lax.rem(t, chips), t // chips

        @pl.when(core == 0)
        def _():
            keep[chip, which] = both[:depth]
            give[chip, which] = both[depth:]

        @pl.when(core == 1)
        def _():
            keep[chip, which] = both[depth:]
            give[chip, which] = both[:depth]

        return carry

    lax.fori_loop(first, halves * chips if last is None else last, one, 0)


def mlp_kernel(shared, alone, rows, cot_home, cot_away, *refs):
    count = 2 * len(shared) + len(alone)
    blocks, refs = refs[:count], refs[count:]
    inner, out_weights, down, gate, up, grad_rows, refs = *refs[:6], refs[6:]
    pre, weights, cot, grad_pre, keep_down, give_down, got_down, keep, give, got, *refs = refs
    *far_down, weight_sems, over_sems, cot_sems, core_sems, chip_sems = refs
    core, mate = lax.rem(lax.axis_index("seq"), 2), peer_of("core")
    depth, chips = blocks[0].shape[0], keep.shape[0]
    greet([mate] + [peer_of(k) for k in range(1, chips)])

    def place(kind, which):
        return weights.at[pl.ds(pl.multiple_of(owner_of(kind, which) * depth, depth), depth)]

    over = [
        send(src, place(kind, core), over_sems.at[0, i], over_sems.at[1, i], mate)
        for i, (kind, src) in enumerate(zip(alone, blocks[2 * len(shared) :]))
    ]
    kinds = [(kind, core) for kind in shared] + [(kind, 1 - core) for kind in shared]
    kinds += [(kind, core) for kind in alone]
    loads = []
    for i, ((kind, which), src) in enumerate(zip(kinds, blocks)):
        loads.append(pltpu.make_async_copy(src, place(kind, which), weight_sems.at[i]))
        loads[i].start()

    block = cot_home.shape[1]
    row = lax.axis_index("seq") // (lax.axis_size("seq") // 2)

    def load(i, src):
        return pltpu.make_async_copy(src, cot.at[pl.ds(i * block, block)], cot_sems.at[i])

    for k, order in enumerate(
        (
            (cot_home.at[0], cot_away.at[0], cot_home.at[1], cot_away.at[1]),
            (cot_away.at[1], cot_home.at[1], cot_away.at[0], cot_home.at[0]),
        )
    ):

        @pl.when(row == k)
        def _():
            for i, src in enumerate(order):
                load(i, src).start()

    for copy in loads:
        copy.wait()
    for i in range(4):
        load(i, cot_home.at[0]).wait()
    for copy in over:
        copy.wait()

    units = inner.shape[1]
    step = 256 if units % 256 == 0 else 128
    tile = 512
    tiles = rows.shape[0] // tile

    def cuts(t):
        here = pl.ds(pl.multiple_of(lax.rem(t, tiles) * tile, tile), tile)
        return here, pl.multiple_of((t // tiles) * step, step)

    def forward(t, carry):
        here, first = cuts(t)
        cols, more = pl.ds(first, step), pl.ds(units + first, step)
        x = rows[here, :]
        gate_pre = nn(x, weights[:, cols])
        up_pre = nn(x, weights[:, more])
        pre[here, cols] = gate_pre
        pre[here, more] = up_pre
        inner[here, cols] = (gate_pre * jax.nn.sigmoid(gate_pre) * up_pre).astype(BF16)
        return carry

    def backward(t, carry):
        here, first = cuts(t)
        cols, more = pl.ds(first, step), pl.ds(units + first, step)
        gate_pre, up_pre = pre[here, cols], pre[here, more]
        grad = nn(cot[here, :], weights[:, pl.ds(2 * units + first, step)])
        sigmoid = jax.nn.sigmoid(gate_pre)
        grad_gate = grad * up_pre * sigmoid * (1.0 + gate_pre * (1.0 - sigmoid))
        grad_pre[here, cols] = grad_gate.astype(BF16)
        grad_pre[here, more] = (grad * gate_pre * sigmoid).astype(BF16)
        return carry

    lax.fori_loop(0, tiles * (units // step), forward, 0)
    weight_grads(cot, inner, keep_down, give_down)
    over_down = send(give_down, got_down, core_sems.at[0, 0], core_sems.at[0, 1], mate)
    lax.fori_loop(0, tiles * (units // step), backward, 0)
    over_down.wait()

    def add_down(t, carry):
        at = (lax.rem(t, chips), t // chips)
        keep_down[at] = (keep_down[at].astype(F32) + got_down[at].astype(F32)).astype(BF16)
        return carry

    lax.fori_loop(0, 2 * chips, add_down, 0)
    to_chips = [
        send(
            keep_down.at[part_of(k, "chip")],
            far_down[k - 1],
            chip_sems.at[0, k - 1],
            chip_sems.at[1, k - 1],
            peer_of(k),
        )
        for k in range(1, chips)
    ]
    weight_grads(rows, grad_pre, keep, give)
    over_pre = send(give, got, core_sems.at[1, 0], core_sems.at[1, 1], mate)

    def two(t, carry):
        here = pl.ds(pl.multiple_of(t * tile, tile), tile)
        grad_rows[here, :] = nt(grad_pre[here, :], weights[:, : 2 * units]).astype(BF16)
        return carry

    lax.fori_loop(0, tiles, two, 0)
    out_weights[...] = weights[:, 2 * units :]
    over_pre.wait()

    def add(t, carry):
        at = (lax.rem(t, chips), t // chips)
        both = (keep[at].astype(F32) + got[at].astype(F32)).astype(BF16)
        gate[at] = both[:, :units]
        up[at] = both[:, units:]
        return carry

    lax.fori_loop(0, 2 * chips, add, 0)
    total_down = keep_down[pl.ds(part_of(0, "chip"), 1)][0].astype(F32)
    for k, copy in enumerate(to_chips):
        copy.wait()
        total_down = total_down + far_down[k][...].astype(F32)
    down[...] = total_down.astype(BF16)


def grads_shape(width, columns):
    chips = lax.axis_size("seq") // 4
    return jax.ShapeDtypeStruct((chips, 2, width // chips // 4, columns), BF16)


def mlp(shared, alone, rows, cot_home, cot_away, collective_id):
    blocks = [x for x, _ in shared.values()] + [x for _, x in shared.values()] + list(alone.values())
    (tokens, width), columns = rows.shape, blocks[0].shape[1]
    units = columns // 3
    one, two = grads_shape(width, units), grads_shape(width, 2 * units)
    far, others = jax.ShapeDtypeStruct(one.shape[1:], BF16), one.shape[0] - 1
    results, _ = carried_call(
        lambda riders, *refs: mlp_kernel(list(shared), list(alone), *refs),
        [rows, cot_home, cot_away, *blocks],
        [
            jax.ShapeDtypeStruct((tokens, units), BF16),
            jax.ShapeDtypeStruct((width, units), BF16),
            far,
            one,
            one,
            jax.ShapeDtypeStruct((tokens, width), BF16),
        ],
        [VMEM, ANY, ANY] + [ANY] * len(blocks),
        [VMEM] * 6,
        [
            pltpu.VMEM((tokens, 2 * units), F32),
            pltpu.VMEM((width, columns), BF16),
            pltpu.VMEM((tokens, width), BF16),
            pltpu.VMEM((tokens, 2 * units), BF16),
        ]
        + [pltpu.VMEM(one.shape, BF16)] * 3
        + [pltpu.VMEM(two.shape, BF16)] * 3
        + [pltpu.VMEM(far.shape, BF16)] * others
        + [DMA((len(blocks),)), DMA((2, len(alone))), DMA((4,)), DMA((2, 2)), DMA((2, others))],
        comm_params(collective_id, 60),
        "mlp",
    )
    return results


def write_kernel(sums, taken, out):
    units = taken.shape[1]
    row = lax.axis_index("seq") // (lax.axis_size("seq") // 2)
    kept, other = sums[row].astype(F32), taken[...].astype(F32)
    out[:, :units] = jnp.where(row == 0, kept, other)
    out[:, units:] = jnp.where(row == 0, other, kept)


def write_down_kernel(sums, taken, out):
    units = taken.shape[1]
    row = lax.axis_index("seq") // (lax.axis_size("seq") // 2)
    kept, other = sums[row].astype(F32), taken[...].astype(F32)
    out[:units] = jnp.where(row == 0, kept, other).T
    out[units:] = jnp.where(row == 0, other, kept).T


def write(kernel, sums, taken, shape, name):
    return pl.pallas_call(
        kernel,
        cost_estimate=NO_COST,
        name=name,
        in_specs=[VMEM, VMEM],
        out_specs=VMEM,
        out_shape=jax.ShapeDtypeStruct(shape, F32),
        compiler_params=pltpu.CompilerParams(vmem_limit_bytes=32 * 2**20),
    )(sums, taken)


def shards(
    tokens,
    lengths,
    attn_gain,
    w_query,
    w_key,
    w_value,
    query_gain,
    key_gain,
    w_out,
    mlp_gain,
    w_gate,
    w_up,
    w_down,
    cotangent,
):
    seq, grp = lax.axis_size("seq"), lax.axis_size("grp")
    seq_index, grp_index = lax.axis_index("seq"), lax.axis_index("grp")
    local_rows, width = tokens.shape[1:]
    rows = local_rows * grp
    dim = query_gain.shape[0]
    queries, keys = w_query.shape[1] // dim, w_key.shape[1] // dim
    repeat = queries // keys
    hidden_units = w_gate.shape[1]
    chunk = attn_gain.shape[0]
    depth = width // seq

    line = seq // 2
    row = seq_index // line

    def to_give(values):
        return lax.dynamic_index_in_dim(values, 1 - row, 0, keepdims=False)

    def both_rows(values, taken):
        kept = lax.dynamic_index_in_dim(values, row, 0, keepdims=False)
        return jnp.stack([jnp.where(row == 0, kept, taken), jnp.where(row == 0, taken, kept)])

    length = lax.dynamic_slice(lengths, (row,), (1,))

    half_units = hidden_units // 2
    opposite = [(s, (s + line) % seq) for s in range(seq)]

    def half(which):
        cut = [
            lax.dynamic_slice_in_dim(w, which * half_units, half_units, 1)
            for w in (w_gate, w_up, w_down.T)
        ]
        return jnp.concatenate(cut, axis=1)

    chips = line // 2
    steps = range(1, chips)
    place = lax.rem(seq_index, line) // 2

    def next_chip(k):
        return [(s, s - s % line + (s % line + 2 * k) % line) for s in range(seq)]

    def chips_sum(parts, arrived):
        mine = lax.dynamic_index_in_dim(parts, place, 0, keepdims=False)
        return sum([x.astype(F32) for x in arrived], mine.astype(F32)).astype(BF16)

    def to_chips(parts):
        return [(k, parts, "chip") for k in steps]

    projections = jnp.concatenate([w_query, w_key, w_value], axis=1)
    full_qkv = lax.all_gather(projections, "seq", axis=0, tiled=True)
    lane = max(128, chunk)
    packed = jnp.pad(jnp.stack([attn_gain, mlp_gain]), ((0, 6), (0, lane - chunk)))
    spread_gains, (taken_tokens,) = spread(packed, seq, grp, 1, [("opposite", to_give(tokens))])
    spread_gains = spread_gains[:, :, :, :chunk].transpose(2, 1, 0, 3)
    gain_attn = spread_gains[0].reshape(-1)
    gain_mlp = spread_gains[1].reshape(-1)
    full_out = lax.all_gather(after(w_out.T, taken_tokens), "seq", axis=0, tiled=True)
    residual = both_rows(tokens, taken_tokens).astype(F32)
    attn_unit, attn_inverse = normalize(residual)
    attn_rows, _ = gather_rows((attn_unit * gain_attn).astype(BF16), grp, 2, "gather_inputs")
    kept_half, given_half = after((half(row), half(1 - row)), attn_rows)
    taken_half = lax.ppermute(given_half, "seq", opposite)
    token_pos = (seq_index * grp + grp_index) * local_rows + jnp.arange(local_rows, dtype=jnp.int32)
    valid_rows = (token_pos[None, :] < lengths[:, None]).astype(BF16)
    cot_home = cotangent * valid_rows[:, :, None]

    frequency = ROPE_BASE ** (-jnp.arange(dim // 2, dtype=F32) * 2.0 / dim)
    small = [jnp.tile(frequency, 2)[None], query_gain[None], key_gain[None]]
    raw, q, kv_home = heads_forward(attn_rows, full_qkv, small, queries, keys)

    (mixed, mixed_low, log_total, kv_all, cot_gathered), _ = attend(
        length, q, kv_home, cot_home, seq, grp, keys, repeat, dim, 3
    )
    cot_gathered = cot_gathered.reshape(2, rows, width)
    near = after(kept_half, mixed)
    kept_passed = [lax.ppermute(near, "seq", next_chip(k)) for k in steps]
    summed, (taken_cotangent,) = sum_rows(
        nt(mixed_low, full_out), grp, 4, "sum_attention", [("opposite", cot_home)]
    )
    early = jnp.where(row == 0, cot_home[0], taken_cotangent[1])
    late = jnp.where(row == 0, taken_cotangent[0], cot_home[1])
    cot_rows = jnp.stack([early, late]).astype(F32)
    hidden = residual + summed

    mlp_unit, mlp_inverse = normalize(hidden)
    mlp_rows, cot_away, (core_kept, core_taken, *taken_passed) = gather_pair(
        (mlp_unit * gain_mlp).astype(BF16),
        taken_cotangent,
        grp,
        5,
        "gather_mlp",
        [("core", kept_half), ("core", taken_half)] + [(k, taken_half) for k in steps],
    )
    shared = {(False, 0): (kept_half, core_kept), (True, 0): (taken_half, core_taken)}
    alone = {(False, k): x for k, x in zip(steps, kept_passed)}
    alone.update({(True, k): x for k, x in zip(steps, taken_passed)})
    inner_low, down_weights, down, gate, up, grad_mlp_part = mlp(
        shared, alone, mlp_rows, cot_gathered, cot_away, 13
    )
    grad_mlp_in, out_part, arrived = sum_pair(
        grad_mlp_part,
        inner_low,
        down_weights,
        grp,
        7,
        "sum_mlp_back",
        [("opposite", down, "row")] + to_chips(gate),
    )
    taken_down, *arrived = arrived
    gate = chips_sum(gate, arrived)
    grad_gain_mlp = jnp.sum(grad_mlp_in * mlp_unit, axis=(0, 1))
    grad_hidden = cot_rows + norm_back(grad_mlp_in * gain_mlp, mlp_unit, mlp_inverse)
    grad_branch, (taken_gate, *arrived) = gather_rows(
        grad_hidden.astype(BF16),
        grp,
        8,
        "gather_branch",
        [("opposite", gate, "row")] + to_chips(up),
    )
    up = chips_sum(up, arrived)

    grad_mixed = nn(grad_branch, full_out).astype(BF16)
    (grad_q, grad_kv, summed), (taken_up,) = attend_back(
        length,
        q,
        kv_all,
        mixed,
        grad_mixed,
        log_total,
        out_part,
        hidden,
        grp,
        keys,
        repeat,
        dim,
        9,
        [("opposite", up, "row")],
    )
    output = jnp.where(row == 0, summed, summed[::-1]).astype(BF16)
    grad_raw, head_gain_parts = heads_backward(raw, grad_q, grad_kv, small, queries, keys)
    grad_w_attn = attention_grads(attn_rows, grad_raw, grad_branch, mixed_low)
    sum_attn = lax.psum_scatter(grad_w_attn, "seq", scatter_dimension=0, tiled=True)
    grad_attn_part = nt(after(grad_raw, grad_w_attn), full_qkv)
    grad_attn_in, _ = sum_rows(grad_attn_part, grp, 10, "sum_attention_back")
    wide_shape = (depth, hidden_units)
    taken_down, taken_gate, taken_up = after((taken_down, taken_gate, taken_up), grad_attn_in)
    out_down = write(write_down_kernel, down, taken_down, wide_shape[::-1], "write_down")
    out_gate = write(write_kernel, gate, taken_gate, wide_shape, "write_gate")
    out_up = write(write_kernel, up, taken_up, wide_shape, "write_up")
    grad_gain_attn = jnp.sum(grad_attn_in * attn_unit, axis=(0, 1))
    grad_tokens = grad_hidden + norm_back(grad_attn_in * gain_attn, attn_unit, attn_inverse)

    head_gain_grads = jnp.stack(
        [
            jnp.sum(head_gain_parts[:queries, 0], axis=0),
            jnp.sum(head_gain_parts[queries : queries + keys, 0], axis=0),
        ]
    )
    vector = jnp.concatenate([grad_gain_attn, grad_gain_mlp, head_gain_grads.reshape(-1)])
    padded = -(-vector.shape[0] // 1024) * 1024
    vector = jnp.pad(vector, (0, padded - vector.shape[0])).reshape(-1, 128)
    sums, (taken_grads,) = total(
        vector, seq, grp, 12, [("opposite", to_give(grad_tokens).astype(BF16))]
    )
    sums = sums.reshape(-1)
    grad_tokens = both_rows(grad_tokens, taken_grads.astype(F32))
    place = (seq_index * grp + grp_index) * chunk
    out_attn_gain = lax.dynamic_slice(sums, (place,), (chunk,))
    out_mlp_gain = lax.dynamic_slice(sums, (width + place,), (chunk,))
    out_query_gain = sums[2 * width : 2 * width + dim]
    out_key_gain = sums[2 * width + dim : 2 * width + 2 * dim]

    out_query, out_key, out_value, out_out = write_attention(
        sum_attn, (queries * dim, keys * dim, keys * dim)
    )
    return (
        output,
        grad_tokens,
        out_attn_gain,
        out_query,
        out_key,
        out_value,
        out_query_gain,
        out_key_gain,
        out_out,
        out_mlp_gain,
        out_gate,
        out_up,
        out_down,
    )


def solution(mesh):
    rows = P(None, ("seq", "grp"), None)
    vector = P(("seq", "grp"))
    wide, tall = P("seq", "grp"), P("grp", "seq")
    return jax.shard_map(
        shards,
        mesh=mesh,
        in_specs=(
            rows,
            P(),
            vector,
            wide,
            wide,
            wide,
            P(),
            P(),
            tall,
            vector,
            wide,
            wide,
            tall,
            rows,
        ),
        out_specs=(
            rows,
            rows,
            vector,
            wide,
            wide,
            wide,
            P(),
            P(),
            tall,
            vector,
            wide,
            wide,
            tall,
        ),
        check_vma=False,
    )
```
